32 devices in a mesh: groups: 2 (over x), seq: 16 (over z, y, core).
Axes of the slice: x: 2, y: 2, z: 4, core: 2. Of those that a mesh axis runs over, the one named last changes fastest.
Arguments:
- hidden_states: bfloat16 [37, 512, 2560], P(None, ('groups', 'seq')), parts along dimension 1, may hold values from -80 to 80
- layer_mix: float32 [37], replicated, may hold values from 0.05 to 1
- norm_gain: float32 [2560], replicated, may hold values from 0.1 to 1.9
- norm_bias: float32 [2560], replicated, may hold values from -3 to 3
- proj_in: bfloat16 [2560, 1024], replicated, may hold values from -0.125 to 0.125
- proj_in_bias: float32 [1024], replicated, may hold values from -3 to 3
- proj_out: bfloat16 [1024, 1024], replicated, may hold values from -0.1875 to 0.1875
- proj_out_bias: float32 [1024], replicated, may hold values from -3 to 3
- residue_tokens: int32 [512], P(('groups', 'seq')), parts along dimension 0, may hold values from 0 to 22
- residue_table: float32 [23, 1024], replicated, may hold values from -5 to 5
- pair_norm_gain: float32 [1024], replicated, may hold values from 0.1 to 1.9
- pair_norm_bias: float32 [1024], replicated, may hold values from -3 to 3
- qk_weight: bfloat16 [1024, 128], replicated, may hold values from -0.1875 to 0.1875
- qk_bias: float32 [128], replicated, may hold values from -3 to 3
- pair_weight: bfloat16 [128, 128], replicated, may hold values from -0.75 to 0.75
- relpos_bins: int32 [512, 256], P(('groups', 'seq')), parts along dimension 0, may hold values from 0 to 65
- relpos_table: float32 [66, 128], replicated, may hold values from -5 to 5
- chain_ids: int32 [512], P(('groups', 'seq')), parts along dimension 0, may hold values from 0 to 7, never falling along the last dimension, each value on 1 to 64 neighbouring positions
- chain_table: float32 [2, 128], replicated, may hold values from -5 to 5
Outputs:
- single: bfloat16 [512, 1024], P(('groups', 'seq')), parts along dimension 0
- pair: bfloat16 [512, 256, 128], P(('groups', 'seq')), parts along dimension 0
The draws below stay inside these ranges and needn't reach their ends.
There are 2 independent parts, one for each index of `groups`. The reference program is written for one: setup_inputs(seed, part) draws one part's arguments, and reference() takes and returns one part's arrays. A program takes and returns all parts, laid end to end along the dimension named above; an argument that names none is the same for every part. Nothing has to cross between parts.
Inputs may be any that keep to these rules, and one draw needn't show every extreme that they name: `chain_ids`: chain numbers never fall along the residues; each chain has at most 64 residues.
All inputs are finite; a program needn't handle non-finite values.
Results may differ from the reference program's by a relative error of at most 0.0067.
Values may be sent and summed in bfloat16 or wider, within the bound.
No kernel may reach another device: no remote copies, remote signals or barrier semaphores. Data moves between devices by JAX's collectives and lax.ppermute only.
A program may use at most 64 MiB of HBM per device.

```python
import math
import jax
import jax.numpy as jnp
import numpy as np
from jax import lax

D = 2560
CS = 1024
CZ = 128
INNER = 64
NBINS = 66
NAA = 23
NST = 37
NCHAIN = 8
TOK_DEV = 16
L = 256
N_SEQ = 16


def draw_hidden_states(key, part):
    first, second, third = jax.random.split(jax.random.fold_in(key, 11), 3)
    base = jnp.clip(jax.random.normal(first, (NST, L, D), jnp.float32), -4.0, 4.0)
    highest = math.log(10.0)
    col_scale = jnp.exp(jax.random.uniform(second, (NST, 1, D), jnp.float32, 0.0, highest))
    row_scale = jnp.exp(jax.random.uniform(third, (NST, L, 1), jnp.float32, 0.0, highest))
    return (base * col_scale * row_scale * 0.1).astype(jnp.bfloat16)


def touch_ends(array, own_key, low, high):
    shape = array.shape
    spot = [jax.random.randint(jax.random.fold_in(own_key, axis), (), 0, shape[axis]) for axis in range(len(shape))]
    array = array.at[tuple(spot)].set(low)
    longest = shape.index(max(shape))
    spot[longest] = (spot[longest] + 1) % shape[longest]
    return array.at[tuple(spot)].set(high)


def split_up(number_of, total, limit, slope):
    portions = [(1 << 20) // math.isqrt(grade ** slope) + 1 for grade in range(2, number_of + 1)]
    rest, given = total - limit - (number_of - 1), [1] * (number_of - 1)
    while rest > 0:
        movable = [i for i in range(number_of - 1) if given[i] < limit]
        pool, remaining = sum([portions[i] for i in movable]), rest
        for i in movable:
            addition = min(limit - given[i], max(1, remaining * portions[i] // pool), rest)
            given[i] = given[i] + addition
            rest = rest - addition
    return np.array([limit] + given)


def ragged_sizes(stream_key, count, total, limit, lean):
    if count == 2:
        one = jax.random.randint(stream_key, (), max(1, total - limit), min(limit, total - 1) + 1)
        return jnp.stack([one, total - one])
    tallies = jnp.asarray(split_up(count, total, limit, lean), jnp.int32)
    twos = (count - 1) // 2
    source_of, receiver = tallies[1:1 + 2 * twos:2], tallies[2:2 + 2 * twos:2]
    slack = jnp.minimum(source_of - 1, limit - receiver)
    passed = jax.random.randint(jax.random.fold_in(stream_key, 1), (twos,), 0, 1 << 20) % (slack + 1)
    tallies = tallies.at[1:1 + 2 * twos:2].set(source_of - passed).at[2:2 + 2 * twos:2].set(receiver + passed)
    return tallies[jax.random.permutation(jax.random.fold_in(stream_key, 2), count)]


def noise(own_key, shape, scale, bound, held_as=jnp.bfloat16):
    return jnp.clip(scale * jax.random.normal(own_key, shape, jnp.float32), -bound, bound).astype(held_as)


def setup_inputs(seed: int = 0, part: int = 0) -> dict:
    splits = jax.random.split(jax.random.key(seed), 20)
    part_keys = jax.random.split(jax.random.fold_in(splits[19], part), 20)
    hidden_states = draw_hidden_states(jax.random.fold_in(jax.random.fold_in(splits[19], part), 71), part)
    layer_mix = jnp.clip(jnp.exp(jax.random.uniform(splits[1], (NST,), jnp.float32, math.log(0.05), math.log(1.0))), 0.05, 1.0)
    norm_gain = jnp.clip(1.0 + 0.18 * jax.random.normal(splits[2], (D,), jnp.float32), 0.1, 1.9)
    norm_bias = noise(splits[3], (D,), 0.5, 3.0, jnp.float32)
    proj_in = noise(splits[4], (D, CS), D ** -0.5, 0.125)
    proj_in_bias = noise(splits[5], (CS,), 0.5, 3.0, jnp.float32)
    proj_out = noise(splits[6], (CS, CS), CS ** -0.5, 0.1875)
    proj_out_bias = noise(splits[7], (CS,), 0.5, 3.0, jnp.float32)
    residue_tokens = touch_ends(jax.random.randint(part_keys[8], (L,), 0, NAA), jax.random.fold_in(part_keys[8], 1), 0, NAA - 1).astype(jnp.int32)
    residue_table = noise(splits[9], (NAA, CS), 1.0, 5.0, jnp.float32)
    pair_norm_gain = jnp.clip(1.0 + 0.18 * jax.random.normal(splits[10], (CS,), jnp.float32), 0.1, 1.9)
    pair_norm_bias = noise(splits[11], (CS,), 0.5, 3.0, jnp.float32)
    qk_weight = noise(splits[12], (CS, 2 * INNER), CS ** -0.5, 0.1875)
    qk_bias = noise(splits[13], (2 * INNER,), 0.5, 3.0, jnp.float32)
    pair_weight = noise(splits[14], (2 * INNER, CZ), INNER ** -0.5, 0.75)
    relpos_bins = touch_ends(jax.random.randint(part_keys[15], (L, L), 0, NBINS), jax.random.fold_in(part_keys[15], 1), 0, NBINS - 1).astype(jnp.int32)
    relpos_table = noise(splits[16], (NBINS, CZ), 1.0, 5.0, jnp.float32)
    chain_ids = jnp.searchsorted(jnp.cumsum(ragged_sizes(part_keys[17], NCHAIN, L, L // 4, 1)), jnp.arange(L), side="right").astype(jnp.int32)
    chain_table = noise(splits[18], (2, CZ), 1.0, 5.0, jnp.float32)
    return dict(hidden_states=hidden_states, layer_mix=layer_mix, norm_gain=norm_gain, norm_bias=norm_bias, proj_in=proj_in, proj_in_bias=proj_in_bias, proj_out=proj_out, proj_out_bias=proj_out_bias, residue_tokens=residue_tokens, residue_table=residue_table, pair_norm_gain=pair_norm_gain, pair_norm_bias=pair_norm_bias, qk_weight=qk_weight, qk_bias=qk_bias, pair_weight=pair_weight, relpos_bins=relpos_bins, relpos_table=relpos_table, chain_ids=chain_ids, chain_table=chain_table)


epsilon = 1e-05

def layer_norm(values, weight_gain, weight_bias):
    center = values - lax.optimization_barrier(jnp.mean(values, axis=-1, keepdims=True))
    spread = lax.optimization_barrier(jnp.mean(center * center, axis=-1, keepdims=True))
    return center * lax.rsqrt(spread + epsilon) * weight_gain + weight_bias

def single_path(mixture, norm_gain, norm_bias, proj_in, proj_in_bias, proj_out, proj_out_bias, residue_tokens, residue_table, pair_norm_gain, pair_norm_bias, qk_weight, qk_bias, pair_weight):
    normed = layer_norm(mixture, norm_gain, norm_bias).astype(jnp.bfloat16)
    hidden = jax.nn.relu(jnp.dot(normed, proj_in, preferred_element_type=jnp.float32) + proj_in_bias).astype(jnp.bfloat16)
    onehot = (residue_tokens[:, None] == jnp.arange(residue_table.shape[0], dtype=jnp.int32)[None, :]).astype(jnp.float32)
    residue_term = jnp.dot(onehot, residue_table, precision=lax.Precision.HIGHEST)
    single_f = jnp.dot(hidden, proj_out, preferred_element_type=jnp.float32) + proj_out_bias + residue_term
    pair_in = layer_norm(single_f, pair_norm_gain, pair_norm_bias).astype(jnp.bfloat16)
    query_key = jnp.dot(pair_in, qk_weight, preferred_element_type=jnp.float32) + qk_bias
    inner_dim = pair_weight.shape[0] // 2
    queries = query_key[:, :inner_dim].astype(jnp.bfloat16)
    key_rows = query_key[:, inner_dim:].astype(jnp.bfloat16)
    row_diff = jnp.dot(queries, pair_weight[inner_dim:], preferred_element_type=jnp.float32)
    return (single_f, queries, key_rows, row_diff)

def pair_tile(queries, row_diff, row_chain, key_rows, col_diff, col_chain, bin_block, pair_weight, relpos_table, chain_table):
    inner_dim = queries.shape[1]
    row_count = queries.shape[0]
    col_count = key_rows.shape[0]
    products = (queries[:, None, :].astype(jnp.float32) * key_rows[None, :, :].astype(jnp.float32)).astype(jnp.bfloat16)
    product_term = jnp.dot(products.reshape(row_count * col_count, inner_dim), pair_weight[:inner_dim], preferred_element_type=jnp.float32)
    product_term = product_term.reshape(row_count, col_count, -1)
    onehot = (bin_block[:, :, None] == jnp.arange(relpos_table.shape[0], dtype=jnp.int32)[None, None, :]).astype(jnp.float32)
    relpos = jnp.einsum('ijb,bc->ijc', onehot, relpos_table, precision=lax.Precision.HIGHEST)
    same_chain = (row_chain[:, None] == col_chain[None, :])[:, :, None]
    chain_term = jnp.where(same_chain, chain_table[1][None, None, :], chain_table[0][None, None, :])
    summed = product_term + row_diff[:, None, :] - col_diff[None, :, :] + relpos + chain_term
    return summed.astype(jnp.bfloat16)

def reference(hidden_states, layer_mix, norm_gain, norm_bias, proj_in, proj_in_bias, proj_out, proj_out_bias, residue_tokens, residue_table, pair_norm_gain, pair_norm_bias, qk_weight, qk_bias, pair_weight, relpos_bins, relpos_table, chain_ids, chain_table):
    mixture = lax.optimization_barrier(jnp.sum(layer_mix[:, None, None] * hidden_states.astype(jnp.float32), axis=0))
    single_f, queries, key_rows, row_diff = single_path(mixture, norm_gain, norm_bias, proj_in, proj_in_bias, proj_out, proj_out_bias, residue_tokens, residue_table, pair_norm_gain, pair_norm_bias, qk_weight, qk_bias, pair_weight)
    inner_dim = pair_weight.shape[0] // 2
    col_diff = jnp.dot(key_rows, pair_weight[inner_dim:], preferred_element_type=jnp.float32)
    length = relpos_bins.shape[0]
    blocked = (queries.reshape(N_SEQ, TOK_DEV, -1), row_diff.reshape(N_SEQ, TOK_DEV, -1), chain_ids.reshape(N_SEQ, TOK_DEV), relpos_bins.reshape(N_SEQ, TOK_DEV, length))

    def one_block(blocks):
        return pair_tile(blocks[0], blocks[1], blocks[2], key_rows, col_diff, chain_ids, blocks[3], pair_weight, relpos_table, chain_table)
    pair = lax.map(one_block, blocked)
    return (single_f.astype(jnp.bfloat16), pair.reshape(length, length, -1))
```

```python
import jax
import jax.numpy as jnp
from jax import lax
from jax.sharding import PartitionSpec as P

epsilon = 1e-05


def layer_norm(values, weight_gain, weight_bias):
    center = values - jnp.mean(values, axis=-1, keepdims=True)
    spread = jnp.mean(center * center, axis=-1, keepdims=True)
    return center * lax.rsqrt(spread + epsilon) * weight_gain + weight_bias


def single_path(
    mixture,
    norm_gain,
    norm_bias,
    proj_in,
    proj_in_bias,
    proj_out,
    proj_out_bias,
    residue_tokens,
    residue_table,
    pair_norm_gain,
    pair_norm_bias,
    qk_weight,
    qk_bias,
    pair_weight,
):
    normed = layer_norm(mixture, norm_gain, norm_bias).astype(jnp.bfloat16)
    hidden = jax.nn.relu(
        jnp.dot(normed, proj_in, preferred_element_type=jnp.float32) + proj_in_bias
    ).astype(jnp.bfloat16)
    onehot = (
        residue_tokens[:, None] == jnp.arange(residue_table.shape[0], dtype=jnp.int32)[None, :]
    ).astype(jnp.float32)
    residue_term = jnp.dot(onehot, residue_table, precision=lax.Precision.HIGHEST)
    single_f = (
        jnp.dot(hidden, proj_out, preferred_element_type=jnp.float32) + proj_out_bias + residue_term
    )
    pair_in = layer_norm(single_f, pair_norm_gain, pair_norm_bias).astype(jnp.bfloat16)
    query_key = jnp.dot(pair_in, qk_weight, preferred_element_type=jnp.float32) + qk_bias
    inner_dim = pair_weight.shape[0] // 2
    queries = query_key[:, :inner_dim].astype(jnp.bfloat16)
    key_rows = query_key[:, inner_dim:].astype(jnp.bfloat16)
    row_diff = jnp.dot(queries, pair_weight[inner_dim:], preferred_element_type=jnp.float32)
    return (single_f, queries, key_rows, row_diff)


def pair_tile(
    queries,
    row_diff,
    row_chain,
    key_rows,
    col_diff,
    col_chain,
    bin_block,
    pair_weight,
    relpos_table,
    chain_table,
):
    inner_dim = queries.shape[1]
    row_count = queries.shape[0]
    col_count = key_rows.shape[0]
    products = (
        queries[:, None, :].astype(jnp.float32) * key_rows[None, :, :].astype(jnp.float32)
    ).astype(jnp.bfloat16)
    product_term = jnp.dot(
        products.reshape(row_count * col_count, inner_dim),
        pair_weight[:inner_dim],
        preferred_element_type=jnp.float32,
    )
    product_term = product_term.reshape(row_count, col_count, -1)
    onehot = (
        bin_block[:, :, None] == jnp.arange(relpos_table.shape[0], dtype=jnp.int32)[None, None, :]
    ).astype(jnp.float32)
    relpos = jnp.einsum("ijb,bc->ijc", onehot, relpos_table, precision=lax.Precision.HIGHEST)
    same_chain = (row_chain[:, None] == col_chain[None, :])[:, :, None]
    chain_term = jnp.where(same_chain, chain_table[1][None, None, :], chain_table[0][None, None, :])
    summed = product_term + row_diff[:, None, :] - col_diff[None, :, :] + relpos + chain_term
    return summed.astype(jnp.bfloat16)


def shards(
    hidden_states,
    layer_mix,
    norm_gain,
    norm_bias,
    proj_in,
    proj_in_bias,
    proj_out,
    proj_out_bias,
    residue_tokens,
    residue_table,
    pair_norm_gain,
    pair_norm_bias,
    qk_weight,
    qk_bias,
    pair_weight,
    relpos_bins,
    relpos_table,
    chain_ids,
    chain_table,
):
    mixture = jnp.sum(layer_mix[:, None, None] * hidden_states.astype(jnp.float32), axis=0)
    single_f, queries, key_rows, row_diff = single_path(
        mixture,
        norm_gain,
        norm_bias,
        proj_in,
        proj_in_bias,
        proj_out,
        proj_out_bias,
        residue_tokens,
        residue_table,
        pair_norm_gain,
        pair_norm_bias,
        qk_weight,
        qk_bias,
        pair_weight,
    )
    tok_count = key_rows.shape[0]
    inner_dim = key_rows.shape[1]
    device_count = lax.axis_size("seq")
    lane_pad = pair_weight.shape[1] - inner_dim - 1
    block = jnp.concatenate(
        [
            key_rows,
            chain_ids.astype(jnp.bfloat16)[:, None],
            jnp.zeros((tok_count, lane_pad), jnp.bfloat16),
        ],
        axis=1,
    )
    copies = jnp.broadcast_to(block[None], (device_count,) + block.shape)
    blocks = lax.all_to_all(copies, "seq", split_axis=0, concat_axis=0).reshape(
        device_count * tok_count, -1
    )
    key_cols = blocks[:, :inner_dim]
    col_chain = blocks[:, inner_dim].astype(jnp.int32)
    diff_cols = jnp.dot(key_cols, pair_weight[inner_dim:], preferred_element_type=jnp.float32)
    tile_value = pair_tile(
        queries,
        row_diff,
        chain_ids,
        key_cols,
        diff_cols,
        col_chain,
        relpos_bins,
        pair_weight,
        relpos_table,
        chain_table,
    )
    return (single_f.astype(jnp.bfloat16), tile_value)


def solution(mesh):
    in_specs = (
        P(None, ("groups", "seq"), None),
        P(),
        P(),
        P(),
        P(),
        P(),
        P(),
        P(),
        P(("groups", "seq")),
        P(),
        P(),
        P(),
        P(),
        P(),
        P(),
        P(("groups", "seq"), None),
        P(),
        P(("groups", "seq")),
        P(),
    )
    out_specs = (P(("groups", "seq"), None), P(("groups", "seq"), None, None))
    return jax.shard_map(shards, mesh=mesh, in_specs=in_specs, out_specs=out_specs, check_vma=False)
```

```python
import jax
import jax.numpy as jnp
from jax import lax
from jax.sharding import PartitionSpec as P

epsilon = 1e-05


def layer_norm(values, weight_gain, weight_bias):
    center = values - jnp.mean(values, axis=-1, keepdims=True)
    spread = jnp.mean(center * center, axis=-1, keepdims=True)
    return center * lax.rsqrt(spread + epsilon) * weight_gain + weight_bias


def single_path(
    mixture,
    norm_gain,
    norm_bias,
    proj_in,
    proj_in_bias,
    proj_out,
    proj_out_bias,
    residue_tokens,
    residue_table,
    pair_norm_gain,
    pair_norm_bias,
    qk_weight,
    qk_bias,
    pair_weight,
):
    normed = layer_norm(mixture, norm_gain, norm_bias).astype(jnp.bfloat16)
    hidden = jax.nn.relu(
        jnp.dot(normed, proj_in, preferred_element_type=jnp.float32) + proj_in_bias
    ).astype(jnp.bfloat16)
    onehot = (
        residue_tokens[:, None] == jnp.arange(residue_table.shape[0], dtype=jnp.int32)[None, :]
    ).astype(jnp.float32)
    residue_term = jnp.dot(onehot, residue_table, precision=lax.Precision.HIGHEST)
    single_f = (
        jnp.dot(hidden, proj_out, preferred_element_type=jnp.float32) + proj_out_bias + residue_term
    )
    pair_in = layer_norm(single_f, pair_norm_gain, pair_norm_bias).astype(jnp.bfloat16)
    query_key = jnp.dot(pair_in, qk_weight, preferred_element_type=jnp.float32) + qk_bias
    inner_dim = pair_weight.shape[0] // 2
    queries = query_key[:, :inner_dim].astype(jnp.bfloat16)
    key_rows = query_key[:, inner_dim:].astype(jnp.bfloat16)
    row_diff = jnp.dot(queries, pair_weight[inner_dim:], preferred_element_type=jnp.float32)
    return (single_f, queries, key_rows, row_diff)


def pair_tile(
    queries,
    row_diff,
    row_chain,
    key_rows,
    col_diff,
    col_chain,
    bin_block,
    pair_weight,
    relpos_table,
    chain_table,
):
    inner_dim = queries.shape[1]
    row_count = queries.shape[0]
    col_count = key_rows.shape[0]
    products = (
        queries[:, None, :].astype(jnp.float32) * key_rows[None, :, :].astype(jnp.float32)
    ).astype(jnp.bfloat16)
    product_term = jnp.dot(
        products.reshape(row_count * col_count, inner_dim),
        pair_weight[:inner_dim],
        preferred_element_type=jnp.float32,
    )
    product_term = product_term.reshape(row_count, col_count, -1)
    onehot = (
        bin_block[:, :, None] == jnp.arange(relpos_table.shape[0], dtype=jnp.int32)[None, None, :]
    ).astype(jnp.float32)
    relpos = jnp.einsum("ijb,bc->ijc", onehot, relpos_table, precision=lax.Precision.HIGHEST)
    same_chain = (row_chain[:, None] == col_chain[None, :])[:, :, None]
    chain_term = jnp.where(same_chain, chain_table[1][None, None, :], chain_table[0][None, None, :])
    summed = product_term + row_diff[:, None, :] - col_diff[None, :, :] + relpos + chain_term
    return summed.astype(jnp.bfloat16)


def gather_blocks(block, device_count):
    if device_count & (device_count - 1):
        return lax.all_gather(block, "seq", axis=0, tiled=True)
    index = lax.axis_index("seq")
    span = 1
    while span < device_count:
        pairs = [(source, source ^ span) for source in range(device_count)]
        other = lax.ppermute(block, "seq", pairs)
        block = jnp.where(
            index & span,
            jnp.concatenate([other, block], axis=0),
            jnp.concatenate([block, other], axis=0),
        )
        span *= 2
    return block


def shards(
    hidden_states,
    layer_mix,
    norm_gain,
    norm_bias,
    proj_in,
    proj_in_bias,
    proj_out,
    proj_out_bias,
    residue_tokens,
    residue_table,
    pair_norm_gain,
    pair_norm_bias,
    qk_weight,
    qk_bias,
    pair_weight,
    relpos_bins,
    relpos_table,
    chain_ids,
    chain_table,
):
    mixture = jnp.sum(layer_mix[:, None, None] * hidden_states.astype(jnp.float32), axis=0)
    single_f, queries, key_rows, row_diff = single_path(
        mixture,
        norm_gain,
        norm_bias,
        proj_in,
        proj_in_bias,
        proj_out,
        proj_out_bias,
        residue_tokens,
        residue_table,
        pair_norm_gain,
        pair_norm_bias,
        qk_weight,
        qk_bias,
        pair_weight,
    )
    tok_count = key_rows.shape[0]
    inner_dim = key_rows.shape[1]
    device_count = lax.axis_size("seq")
    lane_pad = pair_weight.shape[1] - inner_dim - 1
    block = jnp.concatenate(
        [
            key_rows,
            chain_ids.astype(jnp.bfloat16)[:, None],
            jnp.zeros((tok_count, lane_pad), jnp.bfloat16),
        ],
        axis=1,
    )
    blocks = gather_blocks(block, device_count)
    key_cols = blocks[:, :inner_dim]
    col_chain = blocks[:, inner_dim].astype(jnp.int32)
    diff_cols = jnp.dot(key_cols, pair_weight[inner_dim:], preferred_element_type=jnp.float32)
    tile_value = pair_tile(
        queries,
        row_diff,
        chain_ids,
        key_cols,
        diff_cols,
        col_chain,
        relpos_bins,
        pair_weight,
        relpos_table,
        chain_table,
    )
    return (single_f.astype(jnp.bfloat16), tile_value)


def solution(mesh):
    in_specs = (
        P(None, ("groups", "seq"), None),
        P(),
        P(),
        P(),
        P(),
        P(),
        P(),
        P(),
        P(("groups", "seq")),
        P(),
        P(),
        P(),
        P(),
        P(),
        P(),
        P(("groups", "seq"), None),
        P(),
        P(("groups", "seq")),
        P(),
    )
    out_specs = (P(("groups", "seq"), None), P(("groups", "seq"), None, None))
    return jax.shard_map(shards, mesh=mesh, in_specs=in_specs, out_specs=out_specs, check_vma=False)
```

```python
import jax
import jax.numpy as jnp
from jax import lax
from jax.sharding import PartitionSpec as P

epsilon = 1e-05


def layer_norm(values, weight_gain, weight_bias):
    center = values - jnp.mean(values, axis=-1, keepdims=True)
    spread = jnp.mean(center * center, axis=-1, keepdims=True)
    return center * lax.rsqrt(spread + epsilon) * weight_gain + weight_bias


def single_path(
    mixture,
    norm_gain,
    norm_bias,
    proj_in,
    proj_in_bias,
    proj_out,
    proj_out_bias,
    residue_tokens,
    residue_table,
    pair_norm_gain,
    pair_norm_bias,
    qk_weight,
    qk_bias,
    pair_weight,
):
    normed = layer_norm(mixture, norm_gain, norm_bias).astype(jnp.bfloat16)
    hidden = jax.nn.relu(
        jnp.dot(normed, proj_in, preferred_element_type=jnp.float32) + proj_in_bias
    ).astype(jnp.bfloat16)
    onehot = (
        residue_tokens[:, None] == jnp.arange(residue_table.shape[0], dtype=jnp.int32)[None, :]
    ).astype(jnp.float32)
    residue_term = jnp.dot(onehot, residue_table, precision=lax.Precision.HIGHEST)
    single_f = (
        jnp.dot(hidden, proj_out, preferred_element_type=jnp.float32) + proj_out_bias + residue_term
    )
    pair_in = layer_norm(single_f, pair_norm_gain, pair_norm_bias).astype(jnp.bfloat16)
    query_key = jnp.dot(pair_in, qk_weight, preferred_element_type=jnp.float32) + qk_bias
    inner_dim = pair_weight.shape[0] // 2
    queries = query_key[:, :inner_dim].astype(jnp.bfloat16)
    key_rows = query_key[:, inner_dim:].astype(jnp.bfloat16)
    row_diff = jnp.dot(queries, pair_weight[inner_dim:], preferred_element_type=jnp.float32)
    return (single_f, queries, key_rows, row_diff)


def pair_tile(
    queries,
    row_diff,
    row_chain,
    key_rows,
    col_diff,
    col_chain,
    bin_block,
    pair_weight,
    relpos_table,
    chain_table,
):
    inner_dim = queries.shape[1]
    row_count = queries.shape[0]
    col_count = key_rows.shape[0]
    products = (
        queries[:, None, :].astype(jnp.float32) * key_rows[None, :, :].astype(jnp.float32)
    ).astype(jnp.bfloat16)
    product_term = jnp.dot(
        products.reshape(row_count * col_count, inner_dim),
        pair_weight[:inner_dim],
        preferred_element_type=jnp.float32,
    )
    product_term = product_term.reshape(row_count, col_count, -1)
    onehot = (
        bin_block[:, :, None] == jnp.arange(relpos_table.shape[0], dtype=jnp.int32)[None, None, :]
    ).astype(jnp.float32)
    relpos = jnp.einsum("ijb,bc->ijc", onehot, relpos_table, precision=lax.Precision.HIGHEST)
    same_chain = (row_chain[:, None] == col_chain[None, :])[:, :, None]
    chain_term = jnp.where(same_chain, chain_table[1][None, None, :], chain_table[0][None, None, :])
    summed = product_term + row_diff[:, None, :] - col_diff[None, :, :] + relpos + chain_term
    return summed.astype(jnp.bfloat16)


def shards(
    hidden_states,
    layer_mix,
    norm_gain,
    norm_bias,
    proj_in,
    proj_in_bias,
    proj_out,
    proj_out_bias,
    residue_tokens,
    residue_table,
    pair_norm_gain,
    pair_norm_bias,
    qk_weight,
    qk_bias,
    pair_weight,
    relpos_bins,
    relpos_table,
    chain_ids,
    chain_table,
):
    mixture = jnp.sum(layer_mix[:, None, None] * hidden_states.astype(jnp.float32), axis=0)
    single_f, queries, key_rows, row_diff = single_path(
        mixture,
        norm_gain,
        norm_bias,
        proj_in,
        proj_in_bias,
        proj_out,
        proj_out_bias,
        residue_tokens,
        residue_table,
        pair_norm_gain,
        pair_norm_bias,
        qk_weight,
        qk_bias,
        pair_weight,
    )
    tok_count = key_rows.shape[0]
    inner_dim = key_rows.shape[1]
    device_count = lax.axis_size("seq")
    lane_pad = pair_weight.shape[1] - inner_dim - 1
    block = jnp.concatenate(
        [
            key_rows,
            chain_ids.astype(jnp.bfloat16)[:, None],
            jnp.zeros((tok_count, lane_pad), jnp.bfloat16),
        ],
        axis=1,
    )
    placed = lax.dynamic_update_slice(
        jnp.zeros((device_count * tok_count, block.shape[1]), block.dtype),
        block,
        (lax.axis_index("seq") * tok_count, 0),
    )
    blocks = lax.psum(placed, "seq")
    key_cols = blocks[:, :inner_dim]
    col_chain = blocks[:, inner_dim].astype(jnp.int32)
    diff_cols = jnp.dot(key_cols, pair_weight[inner_dim:], preferred_element_type=jnp.float32)
    tile_value = pair_tile(
        queries,
        row_diff,
        chain_ids,
        key_cols,
        diff_cols,
        col_chain,
        relpos_bins,
        pair_weight,
        relpos_table,
        chain_table,
    )
    return (single_f.astype(jnp.bfloat16), tile_value)


def solution(mesh):
    in_specs = (
        P(None, ("groups", "seq"), None),
        P(),
        P(),
        P(),
        P(),
        P(),
        P(),
        P(),
        P(("groups", "seq")),
        P(),
        P(),
        P(),
        P(),
        P(),
        P(),
        P(("groups", "seq"), None),
        P(),
        P(("groups", "seq")),
        P(),
    )
    out_specs = (P(("groups", "seq"), None), P(("groups", "seq"), None, None))
    return jax.shard_map(shards, mesh=mesh, in_specs=in_specs, out_specs=out_specs, check_vma=False)
```

```python
import functools

import jax
import jax.numpy as jnp
from jax import lax
from jax.experimental import pallas as pl
from jax.experimental.pallas import tpu as pltpu
from jax.sharding import PartitionSpec as P

epsilon = 1e-05
BF16 = jnp.bfloat16
F32 = jnp.float32


def pieces(total, count):
    count = max(1, min(count, total))
    ends = [total * step // count for step in range(count + 1)]
    return [(low, high - low) for low, high in zip(ends[:-1], ends[1:])]


def row_norm(values, gain, bias):
    center = values - jnp.mean(values, axis=-1, keepdims=True)
    spread = jnp.mean(center * center, axis=-1, keepdims=True)
    return center * lax.rsqrt(spread + epsilon) * gain + bias


def single_kernel(
    plan,
    hidden_hbm, mix_hbm, norm_gain_hbm, norm_bias_hbm, proj_in_hbm, proj_in_bias_hbm,
    proj_out_hbm, proj_out_bias_hbm, tokens_hbm, residue_hbm, pair_gain_hbm, pair_bias_hbm,
    qk_hbm, qk_bias_hbm, chain_hbm,
    single_hbm, query_key_ref, copies_ref,
    hidden, mix, norm_gain, norm_bias, proj_in, proj_in_bias, proj_out, proj_out_bias, tokens,
    residue, pair_gain, pair_bias, qk, qk_bias, chain, mixture, residue_rows, single,
    sem_hidden, sem_in, sem_out, sem_small, sem_single,
):
    state_pieces, in_pieces, out_pieces, lane_step = plan
    tok_count = mixture.shape[0]
    inner_dim = qk.shape[1] // 2

    small = [
        (mix_hbm, mix), (tokens_hbm, tokens), (residue_hbm, residue),
        (norm_gain_hbm, norm_gain), (norm_bias_hbm, norm_bias),
        (proj_in_bias_hbm, proj_in_bias), (proj_out_bias_hbm, proj_out_bias),
        (pair_gain_hbm, pair_gain), (pair_bias_hbm, pair_bias),
        (qk_hbm, qk), (qk_bias_hbm, qk_bias), (chain_hbm, chain),
    ]
    small = [
        pltpu.make_async_copy(source, target, sem_small.at[at])
        for at, (source, target) in enumerate(small)
    ]
    states = [
        pltpu.make_async_copy(
            hidden_hbm.at[pl.ds(low, size)], hidden.at[pl.ds(low, size)], sem_hidden.at[at]
        )
        for at, (low, size) in enumerate(state_pieces)
    ]
    firsts = [
        pltpu.make_async_copy(
            proj_in_hbm.at[pl.ds(low, size)], proj_in.at[pl.ds(low, size)], sem_in.at[at]
        )
        for at, (low, size) in enumerate(in_pieces)
    ]
    seconds = [
        pltpu.make_async_copy(
            proj_out_hbm.at[pl.ds(low, size)], proj_out.at[pl.ds(low, size)], sem_out.at[at]
        )
        for at, (low, size) in enumerate(out_pieces)
    ]
    small[0].start()
    for copy in states:
        copy.start()
    for copy in small[1:]:
        copy.start()
    for copy in firsts + seconds:
        copy.start()

    small[0].wait()
    width = mixture.shape[1]
    for at, (low, size) in enumerate(state_pieces):
        states[at].wait()
        for lane in range(0, width, lane_step):
            span = slice(lane, min(lane + lane_step, width))
            total = mixture[:, span] if at else None
            for state in range(low, low + size):
                term = mix[state] * hidden[state, :, span].astype(F32)
                total = term if total is None else total + term
            mixture[:, span] = total

    for copy in small[1:]:
        copy.wait()
    for row in range(tok_count):
        residue_rows[pl.ds(row, 1), :] = residue[pl.ds(tokens[row], 1), :]

    normed = row_norm(mixture[...], norm_gain[...], norm_bias[...]).astype(BF16)
    total = None
    for at, (low, size) in enumerate(in_pieces):
        firsts[at].wait()
        term = jnp.dot(
            normed[:, low:low + size], proj_in[pl.ds(low, size), :], preferred_element_type=F32
        )
        total = term if total is None else total + term
    middle = jnp.maximum(total + proj_in_bias[...], 0.0).astype(BF16)

    total = None
    for at, (low, size) in enumerate(out_pieces):
        seconds[at].wait()
        term = jnp.dot(
            middle[:, low:low + size], proj_out[pl.ds(low, size), :], preferred_element_type=F32
        )
        total = term if total is None else total + term
    single_f = total + proj_out_bias[...] + residue_rows[...]
    single[...] = single_f.astype(BF16)
    out_copy = pltpu.make_async_copy(single, single_hbm, sem_single)
    out_copy.start()

    pair_in = row_norm(single_f, pair_gain[...], pair_bias[...]).astype(BF16)
    query_key = jnp.dot(pair_in, qk[...], preferred_element_type=F32) + qk_bias[...]
    query_key_ref[...] = query_key.astype(BF16)

    shape = (tok_count, 2 * inner_dim)
    lanes = lax.broadcasted_iota(jnp.int32, shape, 1)
    square = (tok_count, tok_count)
    own = lax.broadcasted_iota(jnp.int32, square, 0) == lax.broadcasted_iota(jnp.int32, square, 1)
    chain_col = jnp.sum(
        jnp.where(own, chain[...].astype(F32), 0.0), axis=1, keepdims=True
    )
    keys = pltpu.roll(query_key, inner_dim, 1)
    block = jnp.where(lanes < inner_dim, keys, jnp.where(lanes == inner_dim, chain_col, 0.0))
    block = block.astype(BF16)
    for peer in range(copies_ref.shape[0]):
        copies_ref[peer] = block
    out_copy.wait()


def single_part(device_count, operands):
    (hidden, mix, norm_gain, norm_bias, proj_in, proj_in_bias, proj_out, proj_out_bias, tokens,
     residue, pair_gain, pair_bias, qk, qk_bias, chain) = operands
    state_count, tok_count, width = hidden.shape
    channels = proj_out.shape[1]
    lanes = qk.shape[1]
    plan = (pieces(state_count, 4), pieces(width, 5), pieces(channels, 2), 512)
    args = (
        hidden, mix, norm_gain[None], norm_bias[None], proj_in, proj_in_bias[None],
        proj_out, proj_out_bias[None], tokens, residue, pair_gain[None], pair_bias[None],
        qk, qk_bias[None], chain[None],
    )
    in_smem = (1, 8)
    scratch = [
        (pltpu.SMEM if at in in_smem else pltpu.VMEM)(arg.shape, arg.dtype)
        for at, arg in enumerate(args)
    ]
    scratch += [
        pltpu.VMEM((tok_count, width), F32),
        pltpu.VMEM((tok_count, channels), F32),
        pltpu.VMEM((tok_count, channels), BF16),
        pltpu.SemaphoreType.DMA((len(plan[0]),)),
        pltpu.SemaphoreType.DMA((len(plan[1]),)),
        pltpu.SemaphoreType.DMA((len(plan[2]),)),
        pltpu.SemaphoreType.DMA((12,)),
        pltpu.SemaphoreType.DMA,
    ]
    moved = sum(arg.size * arg.dtype.itemsize for arg in args)
    return pl.pallas_call(
        functools.partial(single_kernel, plan),
        out_shape=(
            jax.ShapeDtypeStruct((tok_count, channels), BF16),
            jax.ShapeDtypeStruct((tok_count, lanes), BF16),
            jax.ShapeDtypeStruct((device_count, tok_count, lanes), BF16),
        ),
        in_specs=[pl.BlockSpec(memory_space=pltpu.HBM)] * len(args),
        out_specs=(
            pl.BlockSpec(memory_space=pltpu.HBM),
            pl.BlockSpec(memory_space=pltpu.VMEM),
            pl.BlockSpec(memory_space=pltpu.VMEM),
        ),
        scratch_shapes=scratch,
        compiler_params=pltpu.CompilerParams(vmem_limit_bytes=32 * 2**20),
        cost_estimate=pl.CostEstimate(
            flops=2 * tok_count * channels * (width + channels + lanes),
            bytes_accessed=moved,
            transcendentals=0,
        ),
        name="single_path",
    )(*args)


def pair_kernel(
    blocks, query_key, chain, bins, pair_weight, relpos, chain_table,
    pair_hbm, right, table, pair, sem,
):
    tok_count, col_count = bins.shape
    bin_count, lanes_count = relpos.shape
    inner_dim = pair_weight.shape[0] // 2
    half = 2 * inner_dim

    step = chain_table[1:2, :] - chain_table[0:1, :]
    step_high = step.astype(BF16).astype(F32)
    table[...] = jnp.zeros(table.shape, F32)
    table[0:bin_count, :] = relpos[...]
    table[bin_count:bin_count + 1, :] = step_high
    table[bin_count + 1:bin_count + 2, :] = step - step_high
    right[0:inner_dim, :] = pair_weight[0:inner_dim, :]
    right[inner_dim:half, :] = -pair_weight[inner_dim:half, :]
    right[half:, :] = table[...].astype(BF16)

    lanes = lax.broadcasted_iota(jnp.int32, (tok_count, half), 1)
    queries = query_key[...]
    row_base = jnp.dot(
        queries[:, 0:inner_dim], pair_weight[inner_dim:half, :], preferred_element_type=F32
    ) + chain_table[0:1, :]
    queries = jnp.where(lanes < inner_dim, queries.astype(F32), 1.0).astype(BF16)

    lanes = lax.broadcasted_iota(jnp.int32, (col_count, half), 1)
    keys = blocks[...].astype(F32)
    col_chain = keys[:, inner_dim:inner_dim + 1].astype(jnp.int32)
    keys = jnp.where(lanes < inner_dim, keys, pltpu.roll(keys, inner_dim, 1)).astype(BF16)

    lanes = lax.broadcasted_iota(jnp.int32, (col_count, table.shape[0]), 1)
    chain_lanes = (lanes >= bin_count) & (lanes < bin_count + 2)
    col_chain = jnp.where(chain_lanes, col_chain, -1)

    padded = jnp.concatenate(
        [bins[...], jnp.zeros((128 - tok_count, col_count), jnp.int32)], axis=0
    )
    bins_col = padded.T
    copies = []
    for row in range(tok_count):
        products = keys * queries[row:row + 1, :]
        hit = (bins_col[:, row:row + 1] == lanes) | (col_chain == chain[row])
        onehot = jnp.where(hit, 1.0, 0.0).astype(BF16)
        value = jnp.dot(
            jnp.concatenate([products, onehot], axis=1), right[...], preferred_element_type=F32
        )
        pair[row] = (value + row_base[row:row + 1, :]).astype(BF16)
        copy = pltpu.make_async_copy(pair.at[row], pair_hbm.at[row], sem.at[row])
        copy.start()
        copies.append(copy)
    for copy in copies:
        copy.wait()


def pair_part(blocks, query_key, chain, bins, pair_weight, relpos, chain_table):
    tok_count, col_count = bins.shape
    channels = pair_weight.shape[1]
    half = pair_weight.shape[0]
    table_rows = -(-(relpos.shape[0] + 2) // 128) * 128
    vmem = pl.BlockSpec(memory_space=pltpu.VMEM)
    return pl.pallas_call(
        pair_kernel,
        out_shape=jax.ShapeDtypeStruct((tok_count, col_count, channels), BF16),
        in_specs=[vmem, vmem, pl.BlockSpec(memory_space=pltpu.SMEM), vmem, vmem, vmem, vmem],
        out_specs=pl.BlockSpec(memory_space=pltpu.HBM),
        scratch_shapes=[
            pltpu.VMEM((half + table_rows, channels), BF16),
            pltpu.VMEM((table_rows, channels), F32),
            pltpu.VMEM((tok_count, col_count, channels), BF16),
            pltpu.SemaphoreType.DMA((tok_count,)),
        ],
        compiler_params=pltpu.CompilerParams(vmem_limit_bytes=32 * 2**20),
        cost_estimate=pl.CostEstimate(
            flops=2 * tok_count * col_count * channels * (half + table_rows),
            bytes_accessed=2 * tok_count * col_count * channels,
            transcendentals=0,
        ),
        name="pair_rows",
    )(blocks, query_key, chain, bins, pair_weight, relpos, chain_table)


def shards(
    hidden_states,
    layer_mix,
    norm_gain,
    norm_bias,
    proj_in,
    proj_in_bias,
    proj_out,
    proj_out_bias,
    residue_tokens,
    residue_table,
    pair_norm_gain,
    pair_norm_bias,
    qk_weight,
    qk_bias,
    pair_weight,
    relpos_bins,
    relpos_table,
    chain_ids,
    chain_table,
):
    device_count = lax.axis_size("seq")
    single, query_key, copies = single_part(
        device_count,
        (
            hidden_states, layer_mix, norm_gain, norm_bias, proj_in, proj_in_bias, proj_out,
            proj_out_bias, residue_tokens, residue_table, pair_norm_gain, pair_norm_bias,
            qk_weight, qk_bias, chain_ids,
        ),
    )
    blocks = lax.all_to_all(copies, "seq", split_axis=0, concat_axis=0)
    blocks = blocks.reshape(-1, blocks.shape[-1])
    pair = pair_part(
        blocks, query_key, chain_ids, relpos_bins, pair_weight, relpos_table, chain_table
    )
    return (single, pair)


def solution(mesh):
    in_specs = (
        P(None, ("groups", "seq"), None),
        P(),
        P(),
        P(),
        P(),
        P(),
        P(),
        P(),
        P(("groups", "seq")),
        P(),
        P(),
        P(),
        P(),
        P(),
        P(),
        P(("groups", "seq"), None),
        P(),
        P(("groups", "seq")),
        P(),
    )
    out_specs = (P(("groups", "seq"), None), P(("groups", "seq"), None, None))
    return jax.shard_map(shards, mesh=mesh, in_specs=in_specs, out_specs=out_specs, check_vma=False)
```

```python
import functools

import jax
import jax.numpy as jnp
from jax import lax
from jax.experimental import pallas as pl
from jax.experimental.pallas import tpu as pltpu
from jax.sharding import PartitionSpec as P

epsilon = 1e-05
BF16 = jnp.bfloat16
F32 = jnp.float32


def pieces(total, count):
    count = max(1, min(count, total))
    ends = [total * step // count for step in range(count + 1)]
    return [(low, high - low) for low, high in zip(ends[:-1], ends[1:])]


def row_norm(values, gain, bias):
    center = values - jnp.mean(values, axis=-1, keepdims=True)
    spread = jnp.mean(center * center, axis=-1, keepdims=True)
    return center * lax.rsqrt(spread + epsilon) * gain + bias


def single_kernel(
    plan,
    hidden_hbm, mix_hbm, norm_gain_hbm, norm_bias_hbm, proj_in_hbm, proj_in_bias_hbm,
    proj_out_hbm, proj_out_bias_hbm, tokens_hbm, residue_hbm, pair_gain_hbm, pair_bias_hbm,
    qk_hbm, qk_bias_hbm, chain_hbm,
    single_hbm, query_key_ref, copies_ref,
    hidden, mix, norm_gain, norm_bias, proj_in, proj_in_bias, proj_out, proj_out_bias, tokens,
    residue, pair_gain, pair_bias, qk, qk_bias, chain, mixture, residue_rows, single,
    sem_hidden, sem_in, sem_out, sem_small, sem_single,
):
    state_pieces, in_pieces, out_pieces, lane_step = plan
    tok_count = mixture.shape[0]
    inner_dim = qk.shape[1] // 2

    small = [
        (mix_hbm, mix), (tokens_hbm, tokens), (residue_hbm, residue),
        (norm_gain_hbm, norm_gain), (norm_bias_hbm, norm_bias),
        (proj_in_bias_hbm, proj_in_bias), (proj_out_bias_hbm, proj_out_bias),
        (pair_gain_hbm, pair_gain), (pair_bias_hbm, pair_bias),
        (qk_hbm, qk), (qk_bias_hbm, qk_bias), (chain_hbm, chain),
    ]
    small = [
        pltpu.make_async_copy(source, target, sem_small.at[at])
        for at, (source, target) in enumerate(small)
    ]
    states = [
        pltpu.make_async_copy(
            hidden_hbm.at[pl.ds(low, size)], hidden.at[pl.ds(low, size)], sem_hidden.at[at]
        )
        for at, (low, size) in enumerate(state_pieces)
    ]
    firsts = [
        pltpu.make_async_copy(
            proj_in_hbm.at[pl.ds(low, size)], proj_in.at[pl.ds(low, size)], sem_in.at[at]
        )
        for at, (low, size) in enumerate(in_pieces)
    ]
    seconds = [
        pltpu.make_async_copy(
            proj_out_hbm.at[pl.ds(low, size)], proj_out.at[pl.ds(low, size)], sem_out.at[at]
        )
        for at, (low, size) in enumerate(out_pieces)
    ]
    small[0].start()
    for copy in states:
        copy.start()
    for copy in small[1:]:
        copy.start()
    for copy in firsts + seconds:
        copy.start()

    small[0].wait()
    width = mixture.shape[1]
    for at, (low, size) in enumerate(state_pieces):
        states[at].wait()
        for lane in range(0, width, lane_step):
            span = slice(lane, min(lane + lane_step, width))
            total = mixture[:, span] if at else None
            for state in range(low, low + size):
                term = mix[state] * hidden[state, :, span].astype(F32)
                total = term if total is None else total + term
            mixture[:, span] = total

    for copy in small[1:]:
        copy.wait()
    for row in range(tok_count):
        residue_rows[pl.ds(row, 1), :] = residue[pl.ds(tokens[row], 1), :]

    normed = row_norm(
        mixture[...], norm_gain[...].reshape(1, width), norm_bias[...].reshape(1, width)
    ).astype(BF16)
    total = None
    for at, (low, size) in enumerate(in_pieces):
        firsts[at].wait()
        term = jnp.dot(
            normed[:, low:low + size], proj_in[pl.ds(low, size), :], preferred_element_type=F32
        )
        total = term if total is None else total + term
    middle = jnp.maximum(total + proj_in_bias[...], 0.0).astype(BF16)

    total = None
    for at, (low, size) in enumerate(out_pieces):
        seconds[at].wait()
        term = jnp.dot(
            middle[:, low:low + size], proj_out[pl.ds(low, size), :], preferred_element_type=F32
        )
        total = term if total is None else total + term
    single_f = total + proj_out_bias[...] + residue_rows[...]
    single[...] = single_f.astype(BF16)
    out_copy = pltpu.make_async_copy(single, single_hbm, sem_single)
    out_copy.start()

    pair_in = row_norm(single_f, pair_gain[...], pair_bias[...]).astype(BF16)
    query_key = jnp.dot(pair_in, qk[...], preferred_element_type=F32) + qk_bias[...]
    query_key_ref[...] = query_key.astype(BF16)

    shape = (tok_count, 2 * inner_dim)
    lanes = lax.broadcasted_iota(jnp.int32, shape, 1)
    square = (tok_count, tok_count)
    own = lax.broadcasted_iota(jnp.int32, square, 0) == lax.broadcasted_iota(jnp.int32, square, 1)
    chain_col = jnp.sum(
        jnp.where(own, chain[...].astype(F32), 0.0), axis=1, keepdims=True
    )
    keys = pltpu.roll(query_key, inner_dim, 1)
    block = jnp.where(lanes < inner_dim, keys, jnp.where(lanes == inner_dim, chain_col, 0.0))
    block = block.astype(BF16)
    for peer in range(copies_ref.shape[0]):
        copies_ref[peer] = block
    out_copy.wait()


def single_part(device_count, operands):
    (hidden, mix, norm_gain, norm_bias, proj_in, proj_in_bias, proj_out, proj_out_bias, tokens,
     residue, pair_gain, pair_bias, qk, qk_bias, chain) = operands
    state_count, tok_count, width = hidden.shape
    channels = proj_out.shape[1]
    lanes = qk.shape[1]
    plan = (pieces(state_count, 4), pieces(width, 5), pieces(channels, 2), 512)
    args = (
        hidden, mix, norm_gain, norm_bias, proj_in, proj_in_bias[None],
        proj_out, proj_out_bias[None], tokens, residue, pair_gain[None], pair_bias[None],
        qk, qk_bias[None], chain[None],
    )
    in_smem = (1, 8)
    scratch = [
        (pltpu.SMEM if at in in_smem else pltpu.VMEM)(arg.shape, arg.dtype)
        for at, arg in enumerate(args)
    ]
    scratch += [
        pltpu.VMEM((tok_count, width), F32),
        pltpu.VMEM((tok_count, channels), F32),
        pltpu.VMEM((tok_count, channels), BF16),
        pltpu.SemaphoreType.DMA((len(plan[0]),)),
        pltpu.SemaphoreType.DMA((len(plan[1]),)),
        pltpu.SemaphoreType.DMA((len(plan[2]),)),
        pltpu.SemaphoreType.DMA((12,)),
        pltpu.SemaphoreType.DMA,
    ]
    moved = sum(arg.size * arg.dtype.itemsize for arg in args)
    return pl.pallas_call(
        functools.partial(single_kernel, plan),
        out_shape=(
            jax.ShapeDtypeStruct((tok_count, channels), BF16),
            jax.ShapeDtypeStruct((tok_count, lanes), BF16),
            jax.ShapeDtypeStruct((device_count, tok_count, lanes), BF16),
        ),
        in_specs=[pl.BlockSpec(memory_space=pltpu.HBM)] * len(args),
        out_specs=(
            pl.BlockSpec(memory_space=pltpu.HBM),
            pl.BlockSpec(memory_space=pltpu.VMEM),
            pl.BlockSpec(memory_space=pltpu.VMEM),
        ),
        scratch_shapes=scratch,
        compiler_params=pltpu.CompilerParams(vmem_limit_bytes=60 * 2**20),
        cost_estimate=pl.CostEstimate(
            flops=2 * tok_count * channels * (width + channels + lanes),
            bytes_accessed=moved,
            transcendentals=0,
        ),
        name="single_path",
    )(*args)


def pair_kernel(
    blocks, query_key, chain, bins, pair_weight, relpos, chain_table,
    pair_hbm, right, table, pair, sem,
):
    tok_count, col_count = bins.shape
    bin_count, lanes_count = relpos.shape
    inner_dim = pair_weight.shape[0] // 2
    half = 2 * inner_dim

    step = chain_table[1:2, :] - chain_table[0:1, :]
    step_high = step.astype(BF16).astype(F32)
    table[...] = jnp.zeros(table.shape, F32)
    table[0:bin_count, :] = relpos[...]
    table[bin_count:bin_count + 1, :] = step_high
    table[bin_count + 1:bin_count + 2, :] = step - step_high
    right[0:inner_dim, :] = pair_weight[0:inner_dim, :]
    right[inner_dim:half, :] = -pair_weight[inner_dim:half, :]
    right[half:, :] = table[...].astype(BF16)

    lanes = lax.broadcasted_iota(jnp.int32, (tok_count, half), 1)
    queries = query_key[...]
    row_base = jnp.dot(
        queries[:, 0:inner_dim], pair_weight[inner_dim:half, :], preferred_element_type=F32
    ) + chain_table[0:1, :]
    queries = jnp.where(lanes < inner_dim, queries.astype(F32), 1.0).astype(BF16)

    lanes = lax.broadcasted_iota(jnp.int32, (col_count, half), 1)
    keys = blocks[...].astype(F32)
    col_chain = keys[:, inner_dim:inner_dim + 1].astype(jnp.int32)
    keys = jnp.where(lanes < inner_dim, keys, pltpu.roll(keys, inner_dim, 1)).astype(BF16)

    lanes = lax.broadcasted_iota(jnp.int32, (col_count, table.shape[0]), 1)
    chain_lanes = (lanes >= bin_count) & (lanes < bin_count + 2)
    col_chain = jnp.where(chain_lanes, col_chain, -1)

    padded = jnp.concatenate(
        [bins[...], jnp.zeros((128 - tok_count, col_count), jnp.int32)], axis=0
    )
    bins_col = padded.T
    copies = []
    for row in range(tok_count):
        products = keys * queries[row:row + 1, :]
        hit = (bins_col[:, row:row + 1] == lanes) | (col_chain == chain[row])
        onehot = jnp.where(hit, 1.0, 0.0).astype(BF16)
        value = jnp.dot(
            jnp.concatenate([products, onehot], axis=1), right[...], preferred_element_type=F32
        )
        pair[row] = (value + row_base[row:row + 1, :]).astype(BF16)
        copy = pltpu.make_async_copy(pair.at[row], pair_hbm.at[row], sem.at[row])
        copy.start()
        copies.append(copy)
    for copy in copies:
        copy.wait()


def pair_part(blocks, query_key, chain, bins, pair_weight, relpos, chain_table):
    tok_count, col_count = bins.shape
    channels = pair_weight.shape[1]
    half = pair_weight.shape[0]
    table_rows = -(-(relpos.shape[0] + 2) // 128) * 128
    vmem = pl.BlockSpec(memory_space=pltpu.VMEM)
    return pl.pallas_call(
        pair_kernel,
        out_shape=jax.ShapeDtypeStruct((tok_count, col_count, channels), BF16),
        in_specs=[vmem, vmem, pl.BlockSpec(memory_space=pltpu.SMEM), vmem, vmem, vmem, vmem],
        out_specs=pl.BlockSpec(memory_space=pltpu.HBM),
        scratch_shapes=[
            pltpu.VMEM((half + table_rows, channels), BF16),
            pltpu.VMEM((table_rows, channels), F32),
            pltpu.VMEM((tok_count, col_count, channels), BF16),
            pltpu.SemaphoreType.DMA((tok_count,)),
        ],
        compiler_params=pltpu.CompilerParams(vmem_limit_bytes=60 * 2**20),
        cost_estimate=pl.CostEstimate(
            flops=2 * tok_count * col_count * channels * (half + table_rows),
            bytes_accessed=2 * tok_count * col_count * channels,
            transcendentals=0,
        ),
        name="pair_rows",
    )(blocks, query_key, chain, bins, pair_weight, relpos, chain_table)


def shards(
    hidden_states,
    layer_mix,
    norm_gain,
    norm_bias,
    proj_in,
    proj_in_bias,
    proj_out,
    proj_out_bias,
    residue_tokens,
    residue_table,
    pair_norm_gain,
    pair_norm_bias,
    qk_weight,
    qk_bias,
    pair_weight,
    relpos_bins,
    relpos_table,
    chain_ids,
    chain_table,
):
    device_count = lax.axis_size("seq")
    single, query_key, copies = single_part(
        device_count,
        (
            hidden_states, layer_mix, norm_gain, norm_bias, proj_in, proj_in_bias, proj_out,
            proj_out_bias, residue_tokens, residue_table, pair_norm_gain, pair_norm_bias,
            qk_weight, qk_bias, chain_ids,
        ),
    )
    blocks = lax.all_to_all(copies, "seq", split_axis=0, concat_axis=0)
    blocks = blocks.reshape(-1, blocks.shape[-1])
    pair = pair_part(
        blocks, query_key, chain_ids, relpos_bins, pair_weight, relpos_table, chain_table
    )
    return (single, pair)


def solution(mesh):
    in_specs = (
        P(None, ("groups", "seq"), None),
        P(),
        P(),
        P(),
        P(),
        P(),
        P(),
        P(),
        P(("groups", "seq")),
        P(),
        P(),
        P(),
        P(),
        P(),
        P(),
        P(("groups", "seq"), None),
        P(),
        P(("groups", "seq")),
        P(),
    )
    out_specs = (P(("groups", "seq"), None), P(("groups", "seq"), None, None))
    return jax.shard_map(shards, mesh=mesh, in_specs=in_specs, out_specs=out_specs, check_vma=False)
```

```python
import functools

import jax
import jax.numpy as jnp
from jax import lax
from jax.experimental import pallas as pl
from jax.experimental.pallas import tpu as pltpu
from jax.sharding import PartitionSpec as P

epsilon = 1e-05
BF16 = jnp.bfloat16
F32 = jnp.float32


def pieces(total, count):
    count = max(1, min(count, total))
    ends = [total * step // count for step in range(count + 1)]
    return [(low, high - low) for low, high in zip(ends[:-1], ends[1:])]


def row_norm(values, gain, bias):
    center = values - jnp.mean(values, axis=-1, keepdims=True)
    spread = jnp.mean(center * center, axis=-1, keepdims=True)
    return center * lax.rsqrt(spread + epsilon) * gain + bias


def single_kernel(
    plan,
    hidden_hbm, mix_hbm, norm_gain_hbm, norm_bias_hbm, proj_in_hbm, proj_in_bias_hbm,
    proj_out_hbm, proj_out_bias_hbm, tokens_hbm, residue_hbm, pair_gain_hbm, pair_bias_hbm,
    qk_hbm, qk_bias_hbm, chain_hbm,
    single_hbm, query_key_ref, copies_ref,
    hidden, mix, norm_gain, norm_bias, proj_in, proj_in_bias, proj_out, proj_out_bias, tokens,
    residue, pair_gain, pair_bias, qk, qk_bias, chain, mixture, residue_rows, single,
    sem_hidden, sem_in, sem_out, sem_small, sem_single,
):
    state_pieces, in_pieces, out_pieces, lane_step = plan
    tok_count = mixture.shape[0]
    inner_dim = qk.shape[1] // 2

    small = [
        (mix_hbm, mix), (tokens_hbm, tokens), (residue_hbm, residue),
        (norm_gain_hbm, norm_gain), (norm_bias_hbm, norm_bias),
        (proj_in_bias_hbm, proj_in_bias), (proj_out_bias_hbm, proj_out_bias),
        (pair_gain_hbm, pair_gain), (pair_bias_hbm, pair_bias),
        (qk_hbm, qk), (qk_bias_hbm, qk_bias), (chain_hbm, chain),
    ]
    small = [
        pltpu.make_async_copy(source, target, sem_small.at[at])
        for at, (source, target) in enumerate(small)
    ]
    states = [
        pltpu.make_async_copy(
            hidden_hbm.at[pl.ds(low, size)], hidden.at[pl.ds(low, size)], sem_hidden.at[at]
        )
        for at, (low, size) in enumerate(state_pieces)
    ]
    firsts = [
        pltpu.make_async_copy(
            proj_in_hbm.at[pl.ds(low, size)], proj_in.at[pl.ds(low, size)], sem_in.at[at]
        )
        for at, (low, size) in enumerate(in_pieces)
    ]
    seconds = [
        pltpu.make_async_copy(
            proj_out_hbm.at[pl.ds(low, size)], proj_out.at[pl.ds(low, size)], sem_out.at[at]
        )
        for at, (low, size) in enumerate(out_pieces)
    ]
    small[0].start()
    for copy in states:
        copy.start()
    firsts[0].start()
    for copy in small[1:]:
        copy.start()
    later = firsts[1:] + seconds

    small[0].wait()
    width = mixture.shape[1]
    for at, (low, size) in enumerate(state_pieces):
        states[at].wait()
        last = at == len(state_pieces) - 1
        for copy in later if last else later[:1]:
            copy.start()
        later = later[1:]
        for lane in range(0, width, lane_step):
            span = slice(lane, min(lane + lane_step, width))
            total = mixture[:, span] if at else None
            for state in range(low, low + size):
                term = mix[state] * hidden[state, :, span].astype(F32)
                total = term if total is None else total + term
            mixture[:, span] = total

    for copy in small[1:]:
        copy.wait()
    normed = row_norm(
        mixture[...], norm_gain[...].reshape(1, width), norm_bias[...].reshape(1, width)
    ).astype(BF16)
    total = None
    for at, (low, size) in enumerate(in_pieces):
        firsts[at].wait()
        term = jnp.dot(
            normed[:, low:low + size], proj_in[pl.ds(low, size), :], preferred_element_type=F32
        )
        total = term if total is None else total + term
    for row in range(tok_count):
        residue_rows[pl.ds(row, 1), :] = residue[pl.ds(tokens[row], 1), :]
    middle = jnp.maximum(total + proj_in_bias[...], 0.0).astype(BF16)

    total = None
    for at, (low, size) in enumerate(out_pieces):
        seconds[at].wait()
        term = jnp.dot(
            middle[:, low:low + size], proj_out[pl.ds(low, size), :], preferred_element_type=F32
        )
        total = term if total is None else total + term
    single_f = total + proj_out_bias[...] + residue_rows[...]
    single[...] = single_f.astype(BF16)
    out_copy = pltpu.make_async_copy(single, single_hbm, sem_single)
    out_copy.start()

    pair_in = row_norm(single_f, pair_gain[...], pair_bias[...]).astype(BF16)
    query_key = jnp.dot(pair_in, qk[...], preferred_element_type=F32) + qk_bias[...]
    query_key_ref[...] = query_key.astype(BF16)

    shape = (tok_count, 2 * inner_dim)
    lanes = lax.broadcasted_iota(jnp.int32, shape, 1)
    square = (tok_count, tok_count)
    own = lax.broadcasted_iota(jnp.int32, square, 0) == lax.broadcasted_iota(jnp.int32, square, 1)
    chain_col = jnp.sum(
        jnp.where(own, chain[...].astype(F32), 0.0), axis=1, keepdims=True
    )
    keys = pltpu.roll(query_key, inner_dim, 1)
    block = jnp.where(lanes < inner_dim, keys, jnp.where(lanes == inner_dim, chain_col, 0.0))
    block = block.astype(BF16)
    for peer in range(copies_ref.shape[0]):
        copies_ref[peer] = block
    out_copy.wait()


def single_part(device_count, operands):
    (hidden, mix, norm_gain, norm_bias, proj_in, proj_in_bias, proj_out, proj_out_bias, tokens,
     residue, pair_gain, pair_bias, qk, qk_bias, chain) = operands
    state_count, tok_count, width = hidden.shape
    channels = proj_out.shape[1]
    lanes = qk.shape[1]
    plan = (pieces(state_count, 6), pieces(width, 5), pieces(channels, 2), 512)
    args = (
        hidden, mix, norm_gain, norm_bias, proj_in, proj_in_bias[None],
        proj_out, proj_out_bias[None], tokens, residue, pair_gain[None], pair_bias[None],
        qk, qk_bias[None], chain[None],
    )
    args = [pltpu.with_memory_space_constraint(arg, pltpu.HBM) for arg in args]
    in_smem = (1, 8)
    scratch = [
        (pltpu.SMEM if at in in_smem else pltpu.VMEM)(arg.shape, arg.dtype)
        for at, arg in enumerate(args)
    ]
    scratch += [
        pltpu.VMEM((tok_count, width), F32),
        pltpu.VMEM((tok_count, channels), F32),
        pltpu.VMEM((tok_count, channels), BF16),
        pltpu.SemaphoreType.DMA((len(plan[0]),)),
        pltpu.SemaphoreType.DMA((len(plan[1]),)),
        pltpu.SemaphoreType.DMA((len(plan[2]),)),
        pltpu.SemaphoreType.DMA((12,)),
        pltpu.SemaphoreType.DMA,
    ]
    moved = sum(arg.size * arg.dtype.itemsize for arg in args)
    return pl.pallas_call(
        functools.partial(single_kernel, plan),
        out_shape=(
            jax.ShapeDtypeStruct((tok_count, channels), BF16),
            jax.ShapeDtypeStruct((tok_count, lanes), BF16),
            jax.ShapeDtypeStruct((device_count, tok_count, lanes), BF16),
        ),
        in_specs=[pl.BlockSpec(memory_space=pltpu.HBM)] * len(args),
        out_specs=(
            pl.BlockSpec(memory_space=pltpu.HBM),
            pl.BlockSpec(memory_space=pltpu.VMEM),
            pl.BlockSpec(memory_space=pltpu.VMEM),
        ),
        scratch_shapes=scratch,
        compiler_params=pltpu.CompilerParams(vmem_limit_bytes=32 * 2**20),
        cost_estimate=pl.CostEstimate(
            flops=2 * tok_count * channels * (width + channels + lanes),
            bytes_accessed=moved,
            transcendentals=0,
        ),
        name="single_path",
    )(*args)


def pair_kernel(
    blocks, query_key, chain, bins, pair_weight, relpos, chain_table,
    pair_hbm, right, table, pair, sem,
):
    tok_count, col_count = bins.shape
    bin_count, lanes_count = relpos.shape
    inner_dim = pair_weight.shape[0] // 2
    half = 2 * inner_dim

    step = chain_table[1:2, :] - chain_table[0:1, :]
    step_high = step.astype(BF16).astype(F32)
    table[...] = jnp.zeros(table.shape, F32)
    table[0:bin_count, :] = relpos[...]
    table[bin_count:bin_count + 1, :] = step_high
    table[bin_count + 1:bin_count + 2, :] = step - step_high
    right[0:inner_dim, :] = pair_weight[0:inner_dim, :]
    right[inner_dim:half, :] = -pair_weight[inner_dim:half, :]
    right[half:, :] = table[...].astype(BF16)

    lanes = lax.broadcasted_iota(jnp.int32, (tok_count, half), 1)
    queries = query_key[...]
    row_base = jnp.dot(
        queries[:, 0:inner_dim], pair_weight[inner_dim:half, :], preferred_element_type=F32
    ) + chain_table[0:1, :]
    queries = jnp.where(lanes < inner_dim, queries.astype(F32), 1.0).astype(BF16)

    lanes = lax.broadcasted_iota(jnp.int32, (col_count, half), 1)
    keys = blocks[...].astype(F32)
    col_chain = keys[:, inner_dim:inner_dim + 1].astype(jnp.int32)
    keys = jnp.where(lanes < inner_dim, keys, pltpu.roll(keys, inner_dim, 1)).astype(BF16)

    lanes = lax.broadcasted_iota(jnp.int32, (col_count, table.shape[0]), 1)
    chain_lanes = (lanes >= bin_count) & (lanes < bin_count + 2)
    col_chain = jnp.where(chain_lanes, col_chain, -1)

    padded = jnp.concatenate(
        [bins[...], jnp.zeros((128 - tok_count, col_count), jnp.int32)], axis=0
    )
    bins_col = padded.T
    copies = []
    for row in range(tok_count):
        products = keys * queries[row:row + 1, :]
        hit = (bins_col[:, row:row + 1] == lanes) | (col_chain == chain[row])
        onehot = jnp.where(hit, 1.0, 0.0).astype(BF16)
        value = jnp.dot(
            jnp.concatenate([products, onehot], axis=1), right[...], preferred_element_type=F32
        )
        pair[row] = (value + row_base[row:row + 1, :]).astype(BF16)
        copy = pltpu.make_async_copy(pair.at[row], pair_hbm.at[row], sem.at[row])
        copy.start()
        copies.append(copy)
    for copy in copies:
        copy.wait()


def pair_part(blocks, query_key, chain, bins, pair_weight, relpos, chain_table):
    tok_count, col_count = bins.shape
    channels = pair_weight.shape[1]
    half = pair_weight.shape[0]
    table_rows = -(-(relpos.shape[0] + 2) // 128) * 128
    vmem = pl.BlockSpec(memory_space=pltpu.VMEM)
    return pl.pallas_call(
        pair_kernel,
        out_shape=jax.ShapeDtypeStruct((tok_count, col_count, channels), BF16),
        in_specs=[vmem, vmem, pl.BlockSpec(memory_space=pltpu.SMEM), vmem, vmem, vmem, vmem],
        out_specs=pl.BlockSpec(memory_space=pltpu.HBM),
        scratch_shapes=[
            pltpu.VMEM((half + table_rows, channels), BF16),
            pltpu.VMEM((table_rows, channels), F32),
            pltpu.VMEM((tok_count, col_count, channels), BF16),
            pltpu.SemaphoreType.DMA((tok_count,)),
        ],
        compiler_params=pltpu.CompilerParams(vmem_limit_bytes=32 * 2**20),
        cost_estimate=pl.CostEstimate(
            flops=2 * tok_count * col_count * channels * (half + table_rows),
            bytes_accessed=2 * tok_count * col_count * channels,
            transcendentals=0,
        ),
        name="pair_rows",
    )(blocks, query_key, chain, bins, pair_weight, relpos, chain_table)


def shards(
    hidden_states,
    layer_mix,
    norm_gain,
    norm_bias,
    proj_in,
    proj_in_bias,
    proj_out,
    proj_out_bias,
    residue_tokens,
    residue_table,
    pair_norm_gain,
    pair_norm_bias,
    qk_weight,
    qk_bias,
    pair_weight,
    relpos_bins,
    relpos_table,
    chain_ids,
    chain_table,
):
    device_count = lax.axis_size("seq")
    single, query_key, copies = single_part(
        device_count,
        (
            hidden_states, layer_mix, norm_gain, norm_bias, proj_in, proj_in_bias, proj_out,
            proj_out_bias, residue_tokens, residue_table, pair_norm_gain, pair_norm_bias,
            qk_weight, qk_bias, chain_ids,
        ),
    )
    blocks = lax.all_to_all(copies, "seq", split_axis=0, concat_axis=0)
    blocks = blocks.reshape(-1, blocks.shape[-1])
    pair = pair_part(
        blocks, query_key, chain_ids, relpos_bins, pair_weight, relpos_table, chain_table
    )
    return (single, pair)


def solution(mesh):
    in_specs = (
        P(None, ("groups", "seq"), None),
        P(),
        P(),
        P(),
        P(),
        P(),
        P(),
        P(),
        P(("groups", "seq")),
        P(),
        P(),
        P(),
        P(),
        P(),
        P(),
        P(("groups", "seq"), None),
        P(),
        P(("groups", "seq")),
        P(),
    )
    out_specs = (P(("groups", "seq"), None), P(("groups", "seq"), None, None))
    return jax.shard_map(shards, mesh=mesh, in_specs=in_specs, out_specs=out_specs, check_vma=False)
```

```python
import functools

import jax
import jax.numpy as jnp
from jax import lax
from jax.experimental import pallas as pl
from jax.experimental.pallas import tpu as pltpu
from jax.sharding import PartitionSpec as P

epsilon = 1e-05
BF16 = jnp.bfloat16
F32 = jnp.float32


def pieces(total, count):
    count = max(1, min(count, total))
    ends = [total * step // count for step in range(count + 1)]
    return [(low, high - low) for low, high in zip(ends[:-1], ends[1:])]


def row_norm(values, gain, bias):
    center = values - jnp.mean(values, axis=-1, keepdims=True)
    spread = jnp.mean(center * center, axis=-1, keepdims=True)
    return center * lax.rsqrt(spread + epsilon) * gain + bias


def single_kernel(
    plan,
    hidden_hbm, mix_hbm, norm_gain_hbm, norm_bias_hbm, proj_in_hbm, proj_in_bias_hbm,
    proj_out_hbm, proj_out_bias_hbm, tokens_hbm, residue_hbm, pair_gain_hbm, pair_bias_hbm,
    qk_hbm, qk_bias_hbm, chain_hbm,
    single_hbm, query_key_ref, copies_ref,
    hidden, mix, norm_gain, norm_bias, proj_in, proj_in_bias, proj_out, proj_out_bias, tokens,
    residue, pair_gain, pair_bias, qk, qk_bias, chain, mixture, residue_rows, single,
    sem_hidden, sem_in, sem_out, sem_small, sem_single,
):
    state_pieces, in_pieces, out_pieces, lane_step = plan
    tok_count = mixture.shape[0]
    inner_dim = qk.shape[1] // 2

    small = [
        (mix_hbm, mix), (tokens_hbm, tokens), (residue_hbm, residue),
        (norm_gain_hbm, norm_gain), (norm_bias_hbm, norm_bias),
        (proj_in_bias_hbm, proj_in_bias), (proj_out_bias_hbm, proj_out_bias),
        (pair_gain_hbm, pair_gain), (pair_bias_hbm, pair_bias),
        (qk_hbm, qk), (qk_bias_hbm, qk_bias), (chain_hbm, chain),
    ]
    small = [
        pltpu.make_async_copy(source, target, sem_small.at[at])
        for at, (source, target) in enumerate(small)
    ]
    states = [
        pltpu.make_async_copy(
            hidden_hbm.at[pl.ds(low, size)], hidden.at[pl.ds(low, size)], sem_hidden.at[at]
        )
        for at, (low, size) in enumerate(state_pieces)
    ]
    firsts = [
        pltpu.make_async_copy(
            proj_in_hbm.at[pl.ds(low, size)], proj_in.at[pl.ds(low, size)], sem_in.at[at]
        )
        for at, (low, size) in enumerate(in_pieces)
    ]
    seconds = [
        pltpu.make_async_copy(
            proj_out_hbm.at[pl.ds(low, size)], proj_out.at[pl.ds(low, size)], sem_out.at[at]
        )
        for at, (low, size) in enumerate(out_pieces)
    ]
    small[0].start()
    for copy in states:
        copy.start()
    firsts[0].start()
    for copy in small[1:]:
        copy.start()
    later = firsts[1:] + seconds

    small[0].wait()
    width = mixture.shape[1]
    for at, (low, size) in enumerate(state_pieces):
        states[at].wait()
        last = at == len(state_pieces) - 1
        for copy in later if last else later[:1]:
            copy.start()
        later = later[1:]
        for lane in range(0, width, lane_step):
            span = slice(lane, min(lane + lane_step, width))
            total = mixture[:, span] if at else None
            for state in range(low, low + size):
                term = mix[state] * hidden[state, :, span].astype(F32)
                total = term if total is None else total + term
            mixture[:, span] = total

    for copy in small[1:]:
        copy.wait()
    normed = row_norm(
        mixture[...], norm_gain[...].reshape(1, width), norm_bias[...].reshape(1, width)
    ).astype(BF16)
    total = None
    for at, (low, size) in enumerate(in_pieces):
        firsts[at].wait()
        term = jnp.dot(
            normed[:, low:low + size], proj_in[pl.ds(low, size), :], preferred_element_type=F32
        )
        total = term if total is None else total + term
    for row in range(tok_count):
        residue_rows[pl.ds(row, 1), :] = residue[pl.ds(tokens[row], 1), :]
    middle = jnp.maximum(total + proj_in_bias[...], 0.0).astype(BF16)

    total = None
    for at, (low, size) in enumerate(out_pieces):
        seconds[at].wait()
        term = jnp.dot(
            middle[:, low:low + size], proj_out[pl.ds(low, size), :], preferred_element_type=F32
        )
        total = term if total is None else total + term
    single_f = total + proj_out_bias[...] + residue_rows[...]
    single[...] = single_f.astype(BF16)
    out_copy = pltpu.make_async_copy(single, single_hbm, sem_single)
    out_copy.start()

    pair_in = row_norm(single_f, pair_gain[...], pair_bias[...]).astype(BF16)
    query_key = jnp.dot(pair_in, qk[...], preferred_element_type=F32) + qk_bias[...]
    query_key_ref[...] = query_key.astype(BF16)

    shape = (tok_count, 2 * inner_dim)
    lanes = lax.broadcasted_iota(jnp.int32, shape, 1)
    square = (tok_count, tok_count)
    own = lax.broadcasted_iota(jnp.int32, square, 0) == lax.broadcasted_iota(jnp.int32, square, 1)
    chain_col = jnp.sum(
        jnp.where(own, chain[...].astype(F32), 0.0), axis=1, keepdims=True
    )
    keys = pltpu.roll(query_key, inner_dim, 1)
    block = jnp.where(lanes < inner_dim, keys, jnp.where(lanes == inner_dim, chain_col, 0.0))
    block = block.astype(BF16)
    for peer in range(copies_ref.shape[0]):
        copies_ref[peer] = block
    out_copy.wait()


def single_part(copy_count, operands):
    (hidden, mix, norm_gain, norm_bias, proj_in, proj_in_bias, proj_out, proj_out_bias, tokens,
     residue, pair_gain, pair_bias, qk, qk_bias, chain) = operands
    state_count, tok_count, width = hidden.shape
    channels = proj_out.shape[1]
    lanes = qk.shape[1]
    plan = (pieces(state_count, 6), pieces(width, 5), pieces(channels, 2), 512)
    args = (
        hidden, mix, norm_gain, norm_bias, proj_in, proj_in_bias[None],
        proj_out, proj_out_bias[None], tokens, residue, pair_gain[None], pair_bias[None],
        qk, qk_bias[None], chain[None],
    )
    args = [pltpu.with_memory_space_constraint(arg, pltpu.HBM) for arg in args]
    in_smem = (1, 8)
    scratch = [
        (pltpu.SMEM if at in in_smem else pltpu.VMEM)(arg.shape, arg.dtype)
        for at, arg in enumerate(args)
    ]
    scratch += [
        pltpu.VMEM((tok_count, width), F32),
        pltpu.VMEM((tok_count, channels), F32),
        pltpu.VMEM((tok_count, channels), BF16),
        pltpu.SemaphoreType.DMA((len(plan[0]),)),
        pltpu.SemaphoreType.DMA((len(plan[1]),)),
        pltpu.SemaphoreType.DMA((len(plan[2]),)),
        pltpu.SemaphoreType.DMA((12,)),
        pltpu.SemaphoreType.DMA,
    ]
    moved = sum(arg.size * arg.dtype.itemsize for arg in args)
    return pl.pallas_call(
        functools.partial(single_kernel, plan),
        out_shape=(
            jax.ShapeDtypeStruct((tok_count, channels), BF16),
            jax.ShapeDtypeStruct((tok_count, lanes), BF16),
            jax.ShapeDtypeStruct((copy_count, tok_count, lanes), BF16),
        ),
        in_specs=[pl.BlockSpec(memory_space=pltpu.HBM)] * len(args),
        out_specs=(
            pl.BlockSpec(memory_space=pltpu.HBM),
            pl.BlockSpec(memory_space=pltpu.VMEM),
            pl.BlockSpec(memory_space=pltpu.VMEM),
        ),
        scratch_shapes=scratch,
        compiler_params=pltpu.CompilerParams(vmem_limit_bytes=32 * 2**20),
        cost_estimate=pl.CostEstimate(
            flops=2 * tok_count * channels * (width + channels + lanes),
            bytes_accessed=moved,
            transcendentals=0,
        ),
        name="single_path",
    )(*args)


def pair_kernel(
    blocks, other, query_key, chain, bins, pair_weight, relpos, chain_table,
    pair_hbm, right, table, pair, sem,
):
    tok_count, col_count = bins.shape
    bin_count, lanes_count = relpos.shape
    inner_dim = pair_weight.shape[0] // 2
    half = 2 * inner_dim

    step = chain_table[1:2, :] - chain_table[0:1, :]
    step_high = step.astype(BF16).astype(F32)
    table[...] = jnp.zeros(table.shape, F32)
    table[0:bin_count, :] = relpos[...]
    table[bin_count:bin_count + 1, :] = step_high
    table[bin_count + 1:bin_count + 2, :] = step - step_high
    right[0:inner_dim, :] = pair_weight[0:inner_dim, :]
    right[inner_dim:half, :] = -pair_weight[inner_dim:half, :]
    right[half:, :] = table[...].astype(BF16)

    lanes = lax.broadcasted_iota(jnp.int32, (tok_count, half), 1)
    queries = query_key[...]
    row_base = jnp.dot(
        queries[:, 0:inner_dim], pair_weight[inner_dim:half, :], preferred_element_type=F32
    ) + chain_table[0:1, :]
    queries = jnp.where(lanes < inner_dim, queries.astype(F32), 1.0).astype(BF16)

    lanes = lax.broadcasted_iota(jnp.int32, (col_count, half), 1)
    odd = lax.axis_index("seq") % 2 == 1
    own_blocks, other_blocks = blocks[...].astype(F32), other[...].astype(F32)
    keys = jnp.stack(
        [jnp.where(odd, other_blocks, own_blocks), jnp.where(odd, own_blocks, other_blocks)],
        axis=1,
    ).reshape(col_count, half)
    col_chain = keys[:, inner_dim:inner_dim + 1].astype(jnp.int32)
    keys = jnp.where(lanes < inner_dim, keys, pltpu.roll(keys, inner_dim, 1)).astype(BF16)

    lanes = lax.broadcasted_iota(jnp.int32, (col_count, table.shape[0]), 1)
    chain_lanes = (lanes >= bin_count) & (lanes < bin_count + 2)
    col_chain = jnp.where(chain_lanes, col_chain, -1)

    padded = jnp.concatenate(
        [bins[...], jnp.zeros((128 - tok_count, col_count), jnp.int32)], axis=0
    )
    bins_col = padded.T
    copies = []
    for row in range(tok_count):
        products = keys * queries[row:row + 1, :]
        hit = (bins_col[:, row:row + 1] == lanes) | (col_chain == chain[row])
        onehot = jnp.where(hit, 1.0, 0.0).astype(BF16)
        value = jnp.dot(
            jnp.concatenate([products, onehot], axis=1), right[...], preferred_element_type=F32
        )
        pair[row] = (value + row_base[row:row + 1, :]).astype(BF16)
        copy = pltpu.make_async_copy(pair.at[row], pair_hbm.at[row], sem.at[row])
        copy.start()
        copies.append(copy)
    for copy in copies:
        copy.wait()


def pair_part(blocks, other, query_key, chain, bins, pair_weight, relpos, chain_table):
    tok_count, col_count = bins.shape
    channels = pair_weight.shape[1]
    half = pair_weight.shape[0]
    table_rows = -(-(relpos.shape[0] + 2) // 128) * 128
    vmem = pl.BlockSpec(memory_space=pltpu.VMEM)
    return pl.pallas_call(
        pair_kernel,
        out_shape=jax.ShapeDtypeStruct((tok_count, col_count, channels), BF16),
        in_specs=[vmem, vmem, vmem, pl.BlockSpec(memory_space=pltpu.SMEM)] + [vmem] * 4,
        out_specs=pl.BlockSpec(memory_space=pltpu.HBM),
        scratch_shapes=[
            pltpu.VMEM((half + table_rows, channels), BF16),
            pltpu.VMEM((table_rows, channels), F32),
            pltpu.VMEM((tok_count, col_count, channels), BF16),
            pltpu.SemaphoreType.DMA((tok_count,)),
        ],
        compiler_params=pltpu.CompilerParams(vmem_limit_bytes=32 * 2**20),
        cost_estimate=pl.CostEstimate(
            flops=2 * tok_count * col_count * channels * (half + table_rows),
            bytes_accessed=2 * tok_count * col_count * channels,
            transcendentals=0,
        ),
        name="pair_rows",
    )(blocks, other, query_key, chain, bins, pair_weight, relpos, chain_table)


def shards(
    hidden_states,
    layer_mix,
    norm_gain,
    norm_bias,
    proj_in,
    proj_in_bias,
    proj_out,
    proj_out_bias,
    residue_tokens,
    residue_table,
    pair_norm_gain,
    pair_norm_bias,
    qk_weight,
    qk_bias,
    pair_weight,
    relpos_bins,
    relpos_table,
    chain_ids,
    chain_table,
):
    device_count = lax.axis_size("seq")
    single, query_key, copies = single_part(
        device_count // 2,
        (
            hidden_states, layer_mix, norm_gain, norm_bias, proj_in, proj_in_bias, proj_out,
            proj_out_bias, residue_tokens, residue_table, pair_norm_gain, pair_norm_bias,
            qk_weight, qk_bias, chain_ids,
        ),
    )
    chips = [list(range(core, device_count, 2)) for core in range(2)]
    blocks = lax.all_to_all(
        copies, "seq", split_axis=0, concat_axis=0, axis_index_groups=chips
    )
    other = lax.ppermute(blocks, "seq", [(at, at ^ 1) for at in range(device_count)])
    pair = pair_part(
        blocks, other, query_key, chain_ids, relpos_bins, pair_weight, relpos_table, chain_table
    )
    return (single, pair)


def solution(mesh):
    in_specs = (
        P(None, ("groups", "seq"), None),
        P(),
        P(),
        P(),
        P(),
        P(),
        P(),
        P(),
        P(("groups", "seq")),
        P(),
        P(),
        P(),
        P(),
        P(),
        P(),
        P(("groups", "seq"), None),
        P(),
        P(("groups", "seq")),
        P(),
    )
    out_specs = (P(("groups", "seq"), None), P(("groups", "seq"), None, None))
    return jax.shard_map(shards, mesh=mesh, in_specs=in_specs, out_specs=out_specs, check_vma=False)
```

```python
import functools

import jax
import jax.numpy as jnp
from jax import lax
from jax.experimental import pallas as pl
from jax.experimental.pallas import tpu as pltpu
from jax.sharding import PartitionSpec as P

epsilon = 1e-05
BF16 = jnp.bfloat16
F32 = jnp.float32


def pieces(total, count):
    count = max(1, min(count, total))
    ends = [total * step // count for step in range(count + 1)]
    return [(low, high - low) for low, high in zip(ends[:-1], ends[1:])]


def row_norm(values, gain, bias):
    center = values - jnp.mean(values, axis=-1, keepdims=True)
    spread = jnp.mean(center * center, axis=-1, keepdims=True)
    return center * lax.rsqrt(spread + epsilon) * gain + bias


def single_kernel(
    plan,
    hidden_hbm, mix_hbm, norm_gain_hbm, norm_bias_hbm, proj_in_hbm, proj_in_bias_hbm,
    proj_out_hbm, proj_out_bias_hbm, tokens_hbm, residue_hbm, pair_gain_hbm, pair_bias_hbm,
    qk_hbm, qk_bias_hbm, chain_hbm,
    single_hbm, query_ref, copies_ref,
    hidden, mix, norm_gain, norm_bias, proj_in, proj_in_bias, proj_out, proj_out_bias, tokens,
    residue, pair_gain, pair_bias, qk, qk_bias, chain, mixture, residue_rows, single,
    sem_hidden, sem_in, sem_out, sem_small, sem_single,
):
    state_pieces, in_pieces, out_pieces, lane_step = plan
    tok_count = mixture.shape[0]
    inner_dim = qk.shape[1] // 2

    small = [
        (mix_hbm, mix), (tokens_hbm, tokens), (residue_hbm, residue),
        (norm_gain_hbm, norm_gain), (norm_bias_hbm, norm_bias),
        (proj_in_bias_hbm, proj_in_bias), (proj_out_bias_hbm, proj_out_bias),
        (pair_gain_hbm, pair_gain), (pair_bias_hbm, pair_bias),
        (qk_hbm, qk), (qk_bias_hbm, qk_bias), (chain_hbm, chain),
    ]
    small = [
        pltpu.make_async_copy(source, target, sem_small.at[at])
        for at, (source, target) in enumerate(small)
    ]
    states = [
        pltpu.make_async_copy(
            hidden_hbm.at[pl.ds(low, size)], hidden.at[pl.ds(low, size)], sem_hidden.at[at]
        )
        for at, (low, size) in enumerate(state_pieces)
    ]
    firsts = [
        pltpu.make_async_copy(
            proj_in_hbm.at[pl.ds(low, size)], proj_in.at[pl.ds(low, size)], sem_in.at[at]
        )
        for at, (low, size) in enumerate(in_pieces)
    ]
    seconds = [
        pltpu.make_async_copy(
            proj_out_hbm.at[pl.ds(low, size)], proj_out.at[pl.ds(low, size)], sem_out.at[at]
        )
        for at, (low, size) in enumerate(out_pieces)
    ]
    small[0].start()
    for copy in states:
        copy.start()
    firsts[0].start()
    for copy in small[1:]:
        copy.start()
    later = firsts[1:] + seconds

    small[0].wait()
    width = mixture.shape[1]
    for at, (low, size) in enumerate(state_pieces):
        states[at].wait()
        last = at == len(state_pieces) - 1
        for copy in later if last else later[:1]:
            copy.start()
        later = later[1:]
        for lane in range(0, width, lane_step):
            span = slice(lane, min(lane + lane_step, width))
            total = mixture[:, span] if at else None
            for state in range(low, low + size):
                term = mix[state] * hidden[state, :, span].astype(F32)
                total = term if total is None else total + term
            mixture[:, span] = total

    for copy in small[1:]:
        copy.wait()
    normed = row_norm(
        mixture[...], norm_gain[...].reshape(1, width), norm_bias[...].reshape(1, width)
    ).astype(BF16)
    total = None
    for at, (low, size) in enumerate(in_pieces):
        firsts[at].wait()
        term = jnp.dot(
            normed[:, low:low + size], proj_in[pl.ds(low, size), :], preferred_element_type=F32
        )
        total = term if total is None else total + term
    for row in range(tok_count):
        residue_rows[pl.ds(row, 1), :] = residue[pl.ds(tokens[row], 1), :]
    middle = jnp.maximum(total + proj_in_bias[...], 0.0).astype(BF16)

    total = None
    for at, (low, size) in enumerate(out_pieces):
        seconds[at].wait()
        term = jnp.dot(
            middle[:, low:low + size], proj_out[pl.ds(low, size), :], preferred_element_type=F32
        )
        total = term if total is None else total + term
    single_f = total + proj_out_bias[...] + residue_rows[...]
    single[...] = single_f.astype(BF16)
    out_copy = pltpu.make_async_copy(single, single_hbm, sem_single)
    out_copy.start()

    pair_in = row_norm(single_f, pair_gain[...], pair_bias[...]).astype(BF16)
    query_key = jnp.dot(pair_in, qk[...], preferred_element_type=F32) + qk_bias[...]

    shape = (tok_count, 2 * inner_dim)
    lanes = lax.broadcasted_iota(jnp.int32, shape, 1)
    flag = lax.rem(lanes, inner_dim // 2).astype(F32)
    square = (tok_count, tok_count)
    own = lax.broadcasted_iota(jnp.int32, square, 0) == lax.broadcasted_iota(jnp.int32, square, 1)
    chain_col = jnp.sum(jnp.where(own, chain[...].astype(F32), 0.0), axis=1, keepdims=True)
    flags = jnp.where(flag == chain_col, 1.0, 0.0)
    front = lanes < inner_dim
    query_ref[...] = jnp.where(front, query_key, flags).astype(BF16)
    block = jnp.where(front, pltpu.roll(query_key, inner_dim, 1), flags).astype(BF16)
    for peer in range(copies_ref.shape[0]):
        copies_ref[peer] = block
    out_copy.wait()


def single_part(device_count, operands):
    (hidden, mix, norm_gain, norm_bias, proj_in, proj_in_bias, proj_out, proj_out_bias, tokens,
     residue, pair_gain, pair_bias, qk, qk_bias, chain) = operands
    state_count, tok_count, width = hidden.shape
    channels = proj_out.shape[1]
    lanes = qk.shape[1]
    plan = (pieces(state_count, 6), pieces(width, 5), pieces(channels, 2), 512)
    args = (
        hidden, mix, norm_gain, norm_bias, proj_in, proj_in_bias[None],
        proj_out, proj_out_bias[None], tokens, residue, pair_gain[None], pair_bias[None],
        qk, qk_bias[None], chain[None],
    )
    args = [pltpu.with_memory_space_constraint(arg, pltpu.HBM) for arg in args]
    in_smem = (1, 8)
    scratch = [
        (pltpu.SMEM if at in in_smem else pltpu.VMEM)(arg.shape, arg.dtype)
        for at, arg in enumerate(args)
    ]
    scratch += [
        pltpu.VMEM((tok_count, width), F32),
        pltpu.VMEM((tok_count, channels), F32),
        pltpu.VMEM((tok_count, channels), BF16),
        pltpu.SemaphoreType.DMA((len(plan[0]),)),
        pltpu.SemaphoreType.DMA((len(plan[1]),)),
        pltpu.SemaphoreType.DMA((len(plan[2]),)),
        pltpu.SemaphoreType.DMA((12,)),
        pltpu.SemaphoreType.DMA,
    ]
    moved = sum(arg.size * arg.dtype.itemsize for arg in args)
    return pl.pallas_call(
        functools.partial(single_kernel, plan),
        out_shape=(
            jax.ShapeDtypeStruct((tok_count, channels), BF16),
            jax.ShapeDtypeStruct((tok_count, lanes), BF16),
            jax.ShapeDtypeStruct((device_count, tok_count, lanes), BF16),
        ),
        in_specs=[pl.BlockSpec(memory_space=pltpu.HBM)] * len(args),
        out_specs=(
            pl.BlockSpec(memory_space=pltpu.HBM),
            pl.BlockSpec(memory_space=pltpu.VMEM),
            pl.BlockSpec(memory_space=pltpu.VMEM),
        ),
        scratch_shapes=scratch,
        compiler_params=pltpu.CompilerParams(vmem_limit_bytes=32 * 2**20),
        cost_estimate=pl.CostEstimate(
            flops=2 * tok_count * channels * (width + channels + lanes),
            bytes_accessed=moved,
            transcendentals=0,
        ),
        name="single_path",
    )(*args)


def first_kernel(queries, bins, pair_weight, relpos, chain_table, first, right, minus, table):
    tok_count, col_count = bins.shape
    bin_count = relpos.shape[0]
    inner_dim = pair_weight.shape[0] // 2
    flag_count = inner_dim // 2

    step = chain_table[1:2, :] - chain_table[0:1, :]
    step_high = step.astype(BF16).astype(F32)
    shape = (flag_count, step.shape[1])
    right[0:inner_dim, :] = pair_weight[0:inner_dim, :]
    right[inner_dim:inner_dim + flag_count, :] = jnp.broadcast_to(step_high, shape).astype(BF16)
    right[inner_dim + flag_count:, :] = jnp.broadcast_to(step - step_high, shape).astype(BF16)
    minus[0:inner_dim, :] = pair_weight[inner_dim:, :]
    minus[inner_dim:, :] = jnp.zeros((inner_dim, step.shape[1]), BF16)

    row_base = jnp.dot(queries[...], minus[...], preferred_element_type=F32) + chain_table[0:1, :]
    table[...] = jnp.zeros(table.shape, F32)
    table[0:bin_count, :] = relpos[...]
    bin_rows = table[...].astype(BF16)
    padded = jnp.concatenate(
        [bins[...], jnp.zeros((128 - tok_count, col_count), jnp.int32)], axis=0
    )
    bins_col = padded.T
    lanes = lax.broadcasted_iota(jnp.int32, (col_count, table.shape[0]), 1)
    for row in range(tok_count):
        onehot = jnp.where(bins_col[:, row:row + 1] == lanes, 1.0, 0.0).astype(BF16)
        value = jnp.dot(onehot, bin_rows, preferred_element_type=F32)
        first[row] = value + row_base[row:row + 1, :]


def first_part(queries, bins, pair_weight, relpos, chain_table):
    tok_count, col_count = bins.shape
    channels = pair_weight.shape[1]
    table_rows = -(-relpos.shape[0] // 128) * 128
    vmem = pl.BlockSpec(memory_space=pltpu.VMEM)
    return pl.pallas_call(
        first_kernel,
        out_shape=(
            jax.ShapeDtypeStruct((tok_count, col_count, channels), F32),
            jax.ShapeDtypeStruct(pair_weight.shape, BF16),
            jax.ShapeDtypeStruct(pair_weight.shape, BF16),
        ),
        in_specs=[vmem] * 5,
        out_specs=(vmem, vmem, vmem),
        scratch_shapes=[pltpu.VMEM((table_rows, channels), F32)],
        compiler_params=pltpu.CompilerParams(vmem_limit_bytes=32 * 2**20),
        cost_estimate=pl.CostEstimate(
            flops=2 * tok_count * col_count * channels * table_rows,
            bytes_accessed=4 * tok_count * col_count * channels,
            transcendentals=0,
        ),
        name="rows_first",
    )(queries, bins, pair_weight, relpos, chain_table)


def pair_kernel(blocks, queries, first, right, minus, pair_hbm, pair, sem):
    keys = blocks[...]
    col_diff = jnp.dot(keys, minus[...], preferred_element_type=F32)
    copies = []
    for row in range(first.shape[0]):
        products = keys * queries[row:row + 1, :]
        value = jnp.dot(products, right[...], preferred_element_type=F32)
        pair[row] = (value + first[row] - col_diff).astype(BF16)
        copy = pltpu.make_async_copy(pair.at[row], pair_hbm.at[row], sem.at[row])
        copy.start()
        copies.append(copy)
    for copy in copies:
        copy.wait()


def pair_part(blocks, queries, first, right, minus):
    tok_count = first.shape[0]
    vmem = pl.BlockSpec(memory_space=pltpu.VMEM)
    return pl.pallas_call(
        pair_kernel,
        out_shape=jax.ShapeDtypeStruct(first.shape, BF16),
        in_specs=[vmem] * 5,
        out_specs=pl.BlockSpec(memory_space=pltpu.HBM),
        scratch_shapes=[
            pltpu.VMEM(first.shape, BF16),
            pltpu.SemaphoreType.DMA((tok_count,)),
        ],
        compiler_params=pltpu.CompilerParams(vmem_limit_bytes=32 * 2**20),
        cost_estimate=pl.CostEstimate(
            flops=2 * first.size * right.shape[0],
            bytes_accessed=6 * first.size,
            transcendentals=0,
        ),
        name="pair_rows",
    )(blocks, queries, first, right, minus)


def shards(
    hidden_states,
    layer_mix,
    norm_gain,
    norm_bias,
    proj_in,
    proj_in_bias,
    proj_out,
    proj_out_bias,
    residue_tokens,
    residue_table,
    pair_norm_gain,
    pair_norm_bias,
    qk_weight,
    qk_bias,
    pair_weight,
    relpos_bins,
    relpos_table,
    chain_ids,
    chain_table,
):
    device_count = lax.axis_size("seq")
    single, queries, copies = single_part(
        device_count,
        (
            hidden_states, layer_mix, norm_gain, norm_bias, proj_in, proj_in_bias, proj_out,
            proj_out_bias, residue_tokens, residue_table, pair_norm_gain, pair_norm_bias,
            qk_weight, qk_bias, chain_ids,
        ),
    )
    blocks = lax.all_to_all(copies, "seq", split_axis=0, concat_axis=0)
    blocks = blocks.reshape(-1, blocks.shape[-1])
    first, right, minus = first_part(
        queries, relpos_bins, pair_weight, relpos_table, chain_table
    )
    pair = pair_part(blocks, queries, first, right, minus)
    return (single, pair)


def solution(mesh):
    in_specs = (
        P(None, ("groups", "seq"), None),
        P(),
        P(),
        P(),
        P(),
        P(),
        P(),
        P(),
        P(("groups", "seq")),
        P(),
        P(),
        P(),
        P(),
        P(),
        P(),
        P(("groups", "seq"), None),
        P(),
        P(("groups", "seq")),
        P(),
    )
    out_specs = (P(("groups", "seq"), None), P(("groups", "seq"), None, None))
    return jax.shard_map(shards, mesh=mesh, in_specs=in_specs, out_specs=out_specs, check_vma=False)
```

```python
import functools

import jax
import jax.numpy as jnp
from jax import lax
from jax.experimental import pallas as pl
from jax.experimental.pallas import tpu as pltpu
from jax.sharding import PartitionSpec as P

epsilon = 1e-05
BF16 = jnp.bfloat16
F32 = jnp.float32


def pieces(total, count):
    count = max(1, min(count, total))
    ends = [total * step // count for step in range(count + 1)]
    return [(low, high - low) for low, high in zip(ends[:-1], ends[1:])]


def row_norm(values, gain, bias):
    center = values - jnp.mean(values, axis=-1, keepdims=True)
    spread = jnp.mean(center * center, axis=-1, keepdims=True)
    return center * lax.rsqrt(spread + epsilon) * gain + bias


def chain_flags(chain, tok_count, inner_dim):
    lanes = lax.broadcasted_iota(jnp.int32, (tok_count, 2 * inner_dim), 1)
    flag = lax.rem(lanes, inner_dim // 2).astype(F32)
    square = (tok_count, tok_count)
    own = lax.broadcasted_iota(jnp.int32, square, 0) == lax.broadcasted_iota(jnp.int32, square, 1)
    chain_col = jnp.sum(jnp.where(own, chain[...].astype(F32), 0.0), axis=1, keepdims=True)
    return jnp.where(flag == chain_col, 1.0, 0.0)


def operand_rows(bins, pair_weight, relpos, chain_table, bin_rows, right, minus, tok_count):
    bin_count = relpos.shape[0]
    inner_dim = pair_weight.shape[0] // 2
    flag_count = inner_dim // 2
    step = chain_table[1:2, :] - chain_table[0:1, :]
    step_high = step.astype(BF16).astype(F32)
    shape = (flag_count, step.shape[1])
    right[0:inner_dim, :] = pair_weight[0:inner_dim, :]
    right[inner_dim:inner_dim + flag_count, :] = jnp.broadcast_to(step_high, shape).astype(BF16)
    right[inner_dim + flag_count:, :] = jnp.broadcast_to(step - step_high, shape).astype(BF16)
    minus[0:inner_dim, :] = pair_weight[inner_dim:, :]
    minus[inner_dim:, :] = jnp.zeros((inner_dim, step.shape[1]), BF16)
    bin_rows[...] = jnp.zeros(bin_rows.shape, F32)
    bin_rows[0:bin_count, :] = relpos[...] + chain_table[0:1, :]
    padded = jnp.concatenate(
        [bins[...], jnp.zeros((128 - tok_count, bins.shape[1]), jnp.int32)], axis=0
    )
    return padded.T


def single_kernel(
    plan,
    hidden_hbm, mix_hbm, norm_gain_hbm, norm_bias_hbm, proj_in_hbm, proj_in_bias_hbm,
    proj_out_hbm, proj_out_bias_hbm, tokens_hbm, residue_hbm, pair_gain_hbm, pair_bias_hbm,
    qk_hbm, qk_bias_hbm, chain_hbm, bins_hbm, pair_weight_hbm, relpos_hbm, chain_table_hbm,
    single, query_ref, copies_ref, first, right, minus,
    hidden, mix, norm_gain, norm_bias, proj_in, proj_in_bias, proj_out, proj_out_bias, tokens,
    residue, pair_gain, pair_bias, qk, qk_bias, chain, bins, pair_weight, relpos, chain_table,
    mixture, residue_rows, bin_rows, sem_hidden, sem_in, sem_out, sem_small,
):
    state_pieces, in_pieces, out_pieces, lane_step = plan
    tok_count = mixture.shape[0]
    inner_dim = qk.shape[1] // 2

    small = [
        (mix_hbm, mix), (tokens_hbm, tokens), (residue_hbm, residue),
        (norm_gain_hbm, norm_gain), (norm_bias_hbm, norm_bias),
        (proj_in_bias_hbm, proj_in_bias), (proj_out_bias_hbm, proj_out_bias),
        (pair_gain_hbm, pair_gain), (pair_bias_hbm, pair_bias),
        (qk_hbm, qk), (qk_bias_hbm, qk_bias), (chain_hbm, chain), (bins_hbm, bins),
        (pair_weight_hbm, pair_weight), (relpos_hbm, relpos), (chain_table_hbm, chain_table),
    ]
    small = [
        pltpu.make_async_copy(source, target, sem_small.at[at])
        for at, (source, target) in enumerate(small)
    ]
    states = [
        pltpu.make_async_copy(
            hidden_hbm.at[pl.ds(low, size)], hidden.at[pl.ds(low, size)], sem_hidden.at[at]
        )
        for at, (low, size) in enumerate(state_pieces)
    ]
    firsts = [
        pltpu.make_async_copy(
            proj_in_hbm.at[pl.ds(low, size)], proj_in.at[pl.ds(low, size)], sem_in.at[at]
        )
        for at, (low, size) in enumerate(in_pieces)
    ]
    seconds = [
        pltpu.make_async_copy(
            proj_out_hbm.at[pl.ds(low, size)], proj_out.at[pl.ds(low, size)], sem_out.at[at]
        )
        for at, (low, size) in enumerate(out_pieces)
    ]
    small[0].start()
    for copy in states:
        copy.start()
    firsts[0].start()
    for copy in small[1:]:
        copy.start()
    later = firsts[1:] + seconds

    small[0].wait()
    width = mixture.shape[1]
    for at, (low, size) in enumerate(state_pieces):
        states[at].wait()
        last = at == len(state_pieces) - 1
        for copy in later if last else later[:1]:
            copy.start()
        later = later[1:]
        for lane in range(0, width, lane_step):
            span = slice(lane, min(lane + lane_step, width))
            total = mixture[:, span] if at else None
            for state in range(low, low + size):
                term = mix[state] * hidden[state, :, span].astype(F32)
                total = term if total is None else total + term
            mixture[:, span] = total

    for copy in small[1:]:
        copy.wait()
    normed = row_norm(
        mixture[...], norm_gain[...].reshape(1, width), norm_bias[...].reshape(1, width)
    ).astype(BF16)
    bins_col = operand_rows(
        bins, pair_weight, relpos, chain_table, bin_rows, right, minus, tok_count
    )
    flags = chain_flags(chain, tok_count, inner_dim)
    bin_table = bin_rows[...].astype(BF16)
    lanes = lax.broadcasted_iota(jnp.int32, (bins_col.shape[0], bin_table.shape[0]), 1)
    row_pieces = pieces(tok_count, max(1, len(in_pieces) - 1))
    total = None
    for at, (low, size) in enumerate(in_pieces):
        firsts[at].wait()
        term = jnp.dot(
            normed[:, low:low + size], proj_in[pl.ds(low, size), :], preferred_element_type=F32
        )
        total = term if total is None else total + term
        if at < len(row_pieces):
            for row in range(row_pieces[at][0], sum(row_pieces[at])):
                onehot = jnp.where(bins_col[:, row:row + 1] == lanes, 1.0, 0.0).astype(BF16)
                first[row] = jnp.dot(onehot, bin_table, preferred_element_type=F32)
    for row in range(tok_count):
        residue_rows[pl.ds(row, 1), :] = residue[pl.ds(tokens[row], 1), :]
    middle = jnp.maximum(total + proj_in_bias[...], 0.0).astype(BF16)

    total = None
    for at, (low, size) in enumerate(out_pieces):
        seconds[at].wait()
        term = jnp.dot(
            middle[:, low:low + size], proj_out[pl.ds(low, size), :], preferred_element_type=F32
        )
        total = term if total is None else total + term
    single_f = total + proj_out_bias[...] + residue_rows[...]
    single[...] = single_f.astype(BF16)

    pair_in = row_norm(single_f, pair_gain[...], pair_bias[...]).astype(BF16)
    query_key = jnp.dot(pair_in, qk[...], preferred_element_type=F32) + qk_bias[...]

    front = lax.broadcasted_iota(jnp.int32, flags.shape, 1) < inner_dim
    query_ref[...] = jnp.where(front, query_key, flags).astype(BF16)
    block = jnp.where(front, pltpu.roll(query_key, inner_dim, 1), flags).astype(BF16)
    for peer in range(copies_ref.shape[0]):
        copies_ref[peer] = block


def single_part(device_count, operands):
    (hidden, mix, norm_gain, norm_bias, proj_in, proj_in_bias, proj_out, proj_out_bias, tokens,
     residue, pair_gain, pair_bias, qk, qk_bias, chain, bins, pair_weight, relpos,
     chain_table) = operands
    state_count, tok_count, width = hidden.shape
    channels = proj_out.shape[1]
    lanes = qk.shape[1]
    table_rows = -(-relpos.shape[0] // 128) * 128
    vmem = pl.BlockSpec(memory_space=pltpu.VMEM)
    plan = (pieces(state_count, 6), pieces(width, 5), pieces(channels, 2), 512)
    args = (
        hidden, mix, norm_gain, norm_bias, proj_in, proj_in_bias[None],
        proj_out, proj_out_bias[None], tokens, residue, pair_gain[None], pair_bias[None],
        qk, qk_bias[None], chain[None], bins, pair_weight, relpos, chain_table,
    )
    args = [pltpu.with_memory_space_constraint(arg, pltpu.HBM) for arg in args]
    in_smem = (1, 8)
    scratch = [
        (pltpu.SMEM if at in in_smem else pltpu.VMEM)(arg.shape, arg.dtype)
        for at, arg in enumerate(args)
    ]
    scratch += [
        pltpu.VMEM((tok_count, width), F32),
        pltpu.VMEM((tok_count, channels), F32),
        pltpu.VMEM((table_rows, pair_weight.shape[1]), F32),
        pltpu.SemaphoreType.DMA((len(plan[0]),)),
        pltpu.SemaphoreType.DMA((len(plan[1]),)),
        pltpu.SemaphoreType.DMA((len(plan[2]),)),
        pltpu.SemaphoreType.DMA((16,)),
    ]
    moved = sum(arg.size * arg.dtype.itemsize for arg in args)
    return pl.pallas_call(
        functools.partial(single_kernel, plan),
        out_shape=(
            jax.ShapeDtypeStruct((tok_count, channels), BF16),
            jax.ShapeDtypeStruct((tok_count, lanes), BF16),
            jax.ShapeDtypeStruct((device_count, tok_count, lanes), BF16),
            jax.ShapeDtypeStruct(bins.shape + pair_weight.shape[1:], F32),
            jax.ShapeDtypeStruct(pair_weight.shape, BF16),
            jax.ShapeDtypeStruct(pair_weight.shape, BF16),
        ),
        in_specs=[pl.BlockSpec(memory_space=pltpu.HBM)] * len(args),
        out_specs=(vmem,) * 6,
        scratch_shapes=scratch,
        compiler_params=pltpu.CompilerParams(vmem_limit_bytes=32 * 2**20),
        cost_estimate=pl.CostEstimate(
            flops=2 * tok_count * channels * (width + channels + lanes),
            bytes_accessed=moved,
            transcendentals=0,
        ),
        name="single_path",
    )(*args)


def pair_kernel(
    blocks, queries, first, right, minus, single, single_hbm, pair_hbm, pair, sem, sem_single
):
    single_copy = pltpu.make_async_copy(single, single_hbm, sem_single)
    single_copy.start()
    keys = blocks[...]
    row_diff = jnp.dot(queries[...], minus[...], preferred_element_type=F32)
    col_diff = jnp.dot(keys, minus[...], preferred_element_type=F32)
    copies = []
    for row in range(first.shape[0]):
        products = keys * queries[row:row + 1, :]
        value = jnp.dot(products, right[...], preferred_element_type=F32)
        value = value + first[row] + (row_diff[row:row + 1, :] - col_diff)
        pair[row] = value.astype(BF16)
        copy = pltpu.make_async_copy(pair.at[row], pair_hbm.at[row], sem.at[row])
        copy.start()
        copies.append(copy)
    for copy in copies:
        copy.wait()
    single_copy.wait()


def pair_part(blocks, queries, first, right, minus, single):
    tok_count = first.shape[0]
    vmem = pl.BlockSpec(memory_space=pltpu.VMEM)
    return pl.pallas_call(
        pair_kernel,
        out_shape=(
            jax.ShapeDtypeStruct(single.shape, BF16),
            jax.ShapeDtypeStruct(first.shape, BF16),
        ),
        in_specs=[vmem] * 6,
        out_specs=(pl.BlockSpec(memory_space=pltpu.HBM),) * 2,
        scratch_shapes=[
            pltpu.VMEM(first.shape, BF16),
            pltpu.SemaphoreType.DMA((tok_count,)),
            pltpu.SemaphoreType.DMA,
        ],
        compiler_params=pltpu.CompilerParams(vmem_limit_bytes=32 * 2**20),
        cost_estimate=pl.CostEstimate(
            flops=2 * first.size * right.shape[0],
            bytes_accessed=6 * first.size,
            transcendentals=0,
        ),
        name="pair_rows",
    )(blocks, queries, first, right, minus, single)


def shards(
    hidden_states,
    layer_mix,
    norm_gain,
    norm_bias,
    proj_in,
    proj_in_bias,
    proj_out,
    proj_out_bias,
    residue_tokens,
    residue_table,
    pair_norm_gain,
    pair_norm_bias,
    qk_weight,
    qk_bias,
    pair_weight,
    relpos_bins,
    relpos_table,
    chain_ids,
    chain_table,
):
    device_count = lax.axis_size("seq")
    single, queries, copies, first, right, minus = single_part(
        device_count,
        (
            hidden_states, layer_mix, norm_gain, norm_bias, proj_in, proj_in_bias, proj_out,
            proj_out_bias, residue_tokens, residue_table, pair_norm_gain, pair_norm_bias,
            qk_weight, qk_bias, chain_ids, relpos_bins, pair_weight, relpos_table, chain_table,
        ),
    )
    blocks = lax.all_to_all(copies, "seq", split_axis=0, concat_axis=0)
    blocks = blocks.reshape(-1, blocks.shape[-1])
    return pair_part(blocks, queries, first, right, minus, single)


def solution(mesh):
    in_specs = (
        P(None, ("groups", "seq"), None),
        P(),
        P(),
        P(),
        P(),
        P(),
        P(),
        P(),
        P(("groups", "seq")),
        P(),
        P(),
        P(),
        P(),
        P(),
        P(),
        P(("groups", "seq"), None),
        P(),
        P(("groups", "seq")),
        P(),
    )
    out_specs = (P(("groups", "seq"), None), P(("groups", "seq"), None, None))
    return jax.shard_map(shards, mesh=mesh, in_specs=in_specs, out_specs=out_specs, check_vma=False)
```

```python
import functools

import jax
import jax.numpy as jnp
from jax import lax
from jax.experimental import pallas as pl
from jax.experimental.pallas import tpu as pltpu
from jax.sharding import PartitionSpec as P

epsilon = 1e-05
BF16 = jnp.bfloat16
F32 = jnp.float32


def pieces(total, count):
    count = max(1, min(count, total))
    ends = [total * step // count for step in range(count + 1)]
    return [(low, high - low) for low, high in zip(ends[:-1], ends[1:])]


def row_norm(values, gain, bias):
    center = values - jnp.mean(values, axis=-1, keepdims=True)
    spread = jnp.mean(center * center, axis=-1, keepdims=True)
    return center * lax.rsqrt(spread + epsilon) * gain + bias


def chain_flags(chain, tok_count, inner_dim):
    lanes = lax.broadcasted_iota(jnp.int32, (tok_count, 2 * inner_dim), 1)
    flag = lax.rem(lanes, inner_dim // 2).astype(F32)
    square = (tok_count, tok_count)
    own = lax.broadcasted_iota(jnp.int32, square, 0) == lax.broadcasted_iota(jnp.int32, square, 1)
    chain_col = jnp.sum(jnp.where(own, chain[...].astype(F32), 0.0), axis=1, keepdims=True)
    return jnp.where(flag == chain_col, 1.0, 0.0)


def operand_rows(bins, pair_weight, relpos, chain_table, bin_rows, right, minus, tok_count):
    bin_count = relpos.shape[0]
    inner_dim = pair_weight.shape[0] // 2
    flag_count = inner_dim // 2
    step = chain_table[1:2, :] - chain_table[0:1, :]
    step_high = step.astype(BF16).astype(F32)
    shape = (flag_count, step.shape[1])
    right[0:inner_dim, :] = pair_weight[0:inner_dim, :]
    right[inner_dim:inner_dim + flag_count, :] = jnp.broadcast_to(step_high, shape).astype(BF16)
    right[inner_dim + flag_count:, :] = jnp.broadcast_to(step - step_high, shape).astype(BF16)
    minus[0:inner_dim, :] = pair_weight[inner_dim:, :]
    minus[inner_dim:, :] = jnp.zeros((inner_dim, step.shape[1]), BF16)
    bin_rows[...] = jnp.zeros(bin_rows.shape, F32)
    bin_rows[0:bin_count, :] = relpos[...] + chain_table[0:1, :]
    padded = jnp.concatenate(
        [bins[...], jnp.zeros((128 - tok_count, bins.shape[1]), jnp.int32)], axis=0
    )
    return padded.T


def single_kernel(
    plan,
    hidden_hbm, mix_hbm, norm_gain_hbm, norm_bias_hbm, proj_in_hbm, proj_in_bias_hbm,
    proj_out_hbm, proj_out_bias_hbm, tokens_hbm, residue_hbm, pair_gain_hbm, pair_bias_hbm,
    qk_hbm, qk_bias_hbm, chain_hbm, bins_hbm, pair_weight_hbm, relpos_hbm, chain_table_hbm,
    single, query_ref, copies_ref, first, right, minus,
    hidden, mix, norm_gain, norm_bias, proj_in, proj_in_bias, proj_out, proj_out_bias, tokens,
    residue, pair_gain, pair_bias, qk, qk_bias, chain, bins, pair_weight, relpos, chain_table,
    mixture, residue_rows, bin_rows, sem_hidden, sem_in, sem_out, sem_small,
):
    state_pieces, in_pieces, out_pieces, lane_step = plan
    tok_count = mixture.shape[0]
    inner_dim = qk.shape[1] // 2

    small = [
        (mix_hbm, mix), (tokens_hbm, tokens), (residue_hbm, residue),
        (norm_gain_hbm, norm_gain), (norm_bias_hbm, norm_bias),
        (proj_in_bias_hbm, proj_in_bias), (proj_out_bias_hbm, proj_out_bias),
        (pair_gain_hbm, pair_gain), (pair_bias_hbm, pair_bias),
        (qk_hbm, qk), (qk_bias_hbm, qk_bias), (chain_hbm, chain), (bins_hbm, bins),
        (pair_weight_hbm, pair_weight), (relpos_hbm, relpos), (chain_table_hbm, chain_table),
    ]
    small = [
        pltpu.make_async_copy(source, target, sem_small.at[at])
        for at, (source, target) in enumerate(small)
    ]
    states = [
        pltpu.make_async_copy(
            hidden_hbm.at[pl.ds(low, size)], hidden.at[pl.ds(low, size)], sem_hidden.at[at]
        )
        for at, (low, size) in enumerate(state_pieces)
    ]
    firsts = [
        pltpu.make_async_copy(
            proj_in_hbm.at[pl.ds(low, size)], proj_in.at[pl.ds(low, size)], sem_in.at[at]
        )
        for at, (low, size) in enumerate(in_pieces)
    ]
    seconds = [
        pltpu.make_async_copy(
            proj_out_hbm.at[pl.ds(low, size)], proj_out.at[pl.ds(low, size)], sem_out.at[at]
        )
        for at, (low, size) in enumerate(out_pieces)
    ]
    small[0].start()
    for copy in states:
        copy.start()
    firsts[0].start()
    for copy in small[1:]:
        copy.start()
    later = firsts[1:] + seconds

    small[0].wait()
    width = mixture.shape[1]
    for at, (low, size) in enumerate(state_pieces):
        states[at].wait()
        last = at == len(state_pieces) - 1
        for copy in later if last else later[:1]:
            copy.start()
        later = later[1:]
        for lane in range(0, width, lane_step):
            span = slice(lane, min(lane + lane_step, width))
            total = mixture[:, span] if at else None
            for state in range(low, low + size):
                term = mix[state] * hidden[state, :, span].astype(F32)
                total = term if total is None else total + term
            mixture[:, span] = total

    for copy in small[1:]:
        copy.wait()
    normed = row_norm(
        mixture[...], norm_gain[...].reshape(1, width), norm_bias[...].reshape(1, width)
    ).astype(BF16)
    bins_col = operand_rows(
        bins, pair_weight, relpos, chain_table, bin_rows, right, minus, tok_count
    )
    flags = chain_flags(chain, tok_count, inner_dim)
    bin_table = bin_rows[...].astype(BF16)
    lanes = lax.broadcasted_iota(jnp.int32, (bins_col.shape[0], bin_table.shape[0]), 1)
    row_pieces = pieces(tok_count, max(1, len(in_pieces) - 1))
    total = None
    for at, (low, size) in enumerate(in_pieces):
        firsts[at].wait()
        term = jnp.dot(
            normed[:, low:low + size], proj_in[pl.ds(low, size), :], preferred_element_type=F32
        )
        total = term if total is None else total + term
        if at < len(row_pieces):
            for row in range(row_pieces[at][0], sum(row_pieces[at])):
                onehot = jnp.where(bins_col[:, row:row + 1] == lanes, 1.0, 0.0).astype(BF16)
                first[row] = jnp.dot(onehot, bin_table, preferred_element_type=F32)
    for row in range(tok_count):
        residue_rows[pl.ds(row, 1), :] = residue[pl.ds(tokens[row], 1), :]
    middle = jnp.maximum(total + proj_in_bias[...], 0.0).astype(BF16)

    total = None
    for at, (low, size) in enumerate(out_pieces):
        seconds[at].wait()
        term = jnp.dot(
            middle[:, low:low + size], proj_out[pl.ds(low, size), :], preferred_element_type=F32
        )
        total = term if total is None else total + term
    single_f = total + proj_out_bias[...] + residue_rows[...]
    single[...] = single_f.astype(BF16)

    pair_in = row_norm(single_f, pair_gain[...], pair_bias[...]).astype(BF16)
    query_key = jnp.dot(pair_in, qk[...], preferred_element_type=F32) + qk_bias[...]

    front = lax.broadcasted_iota(jnp.int32, flags.shape, 1) < inner_dim
    query_ref[...] = jnp.where(front, query_key, flags).astype(BF16)
    block = jnp.where(front, pltpu.roll(query_key, inner_dim, 1), flags).astype(BF16)
    for peer in range(copies_ref.shape[0]):
        copies_ref[peer] = block


def single_part(device_count, operands):
    (hidden, mix, norm_gain, norm_bias, proj_in, proj_in_bias, proj_out, proj_out_bias, tokens,
     residue, pair_gain, pair_bias, qk, qk_bias, chain, bins, pair_weight, relpos,
     chain_table) = operands
    state_count, tok_count, width = hidden.shape
    channels = proj_out.shape[1]
    lanes = qk.shape[1]
    table_rows = -(-relpos.shape[0] // 128) * 128
    vmem = pl.BlockSpec(memory_space=pltpu.VMEM)
    plan = (pieces(state_count, 6), pieces(width, 5), pieces(channels, 2), 512)
    args = (
        hidden, mix, norm_gain, norm_bias, proj_in, proj_in_bias[None],
        proj_out, proj_out_bias[None], tokens, residue, pair_gain[None], pair_bias[None],
        qk, qk_bias[None], chain[None], bins, pair_weight, relpos, chain_table,
    )
    args = [pltpu.with_memory_space_constraint(arg, pltpu.HBM) for arg in args]
    in_smem = (1, 8)
    scratch = [
        (pltpu.SMEM if at in in_smem else pltpu.VMEM)(arg.shape, arg.dtype)
        for at, arg in enumerate(args)
    ]
    scratch += [
        pltpu.VMEM((tok_count, width), F32),
        pltpu.VMEM((tok_count, channels), F32),
        pltpu.VMEM((table_rows, pair_weight.shape[1]), F32),
        pltpu.SemaphoreType.DMA((len(plan[0]),)),
        pltpu.SemaphoreType.DMA((len(plan[1]),)),
        pltpu.SemaphoreType.DMA((len(plan[2]),)),
        pltpu.SemaphoreType.DMA((16,)),
    ]
    moved = sum(arg.size * arg.dtype.itemsize for arg in args)
    return pl.pallas_call(
        functools.partial(single_kernel, plan),
        out_shape=(
            jax.ShapeDtypeStruct((tok_count, channels), BF16),
            jax.ShapeDtypeStruct((tok_count, lanes), BF16),
            jax.ShapeDtypeStruct((device_count, tok_count, lanes), BF16),
            jax.ShapeDtypeStruct(bins.shape + pair_weight.shape[1:], F32),
            jax.ShapeDtypeStruct(pair_weight.shape, BF16),
            jax.ShapeDtypeStruct(pair_weight.shape, BF16),
        ),
        in_specs=[pl.BlockSpec(memory_space=pltpu.HBM)] * len(args),
        out_specs=(vmem,) * 6,
        scratch_shapes=scratch,
        compiler_params=pltpu.CompilerParams(vmem_limit_bytes=32 * 2**20),
        cost_estimate=pl.CostEstimate(
            flops=2 * tok_count * channels * (width + channels + lanes),
            bytes_accessed=moved,
            transcendentals=0,
        ),
        name="single_path",
    )(*args)


def pair_kernel(
    blocks, queries, first, right, minus, single, single_hbm, pair_hbm, pair, sem, sem_single
):
    single_copy = pltpu.make_async_copy(single, single_hbm, sem_single)
    single_copy.start()
    device_count = blocks.shape[0]
    keys = jnp.concatenate([blocks[device_count - 1 - at] for at in range(device_count)], axis=0)
    row_diff = jnp.dot(queries[...], minus[...], preferred_element_type=F32)
    col_diff = jnp.dot(keys, minus[...], preferred_element_type=F32)
    copies = []
    for row in range(first.shape[0]):
        products = keys * queries[row:row + 1, :]
        value = jnp.dot(products, right[...], preferred_element_type=F32)
        value = value + first[row] + (row_diff[row:row + 1, :] - col_diff)
        pair[row] = value.astype(BF16)
        copy = pltpu.make_async_copy(pair.at[row], pair_hbm.at[row], sem.at[row])
        copy.start()
        copies.append(copy)
    for copy in copies:
        copy.wait()
    single_copy.wait()


def pair_part(blocks, queries, first, right, minus, single):
    tok_count = first.shape[0]
    vmem = pl.BlockSpec(memory_space=pltpu.VMEM)
    return pl.pallas_call(
        pair_kernel,
        out_shape=(
            jax.ShapeDtypeStruct(single.shape, BF16),
            jax.ShapeDtypeStruct(first.shape, BF16),
        ),
        in_specs=[vmem] * 6,
        out_specs=(pl.BlockSpec(memory_space=pltpu.HBM),) * 2,
        scratch_shapes=[
            pltpu.VMEM(first.shape, BF16),
            pltpu.SemaphoreType.DMA((tok_count,)),
            pltpu.SemaphoreType.DMA,
        ],
        compiler_params=pltpu.CompilerParams(vmem_limit_bytes=32 * 2**20),
        cost_estimate=pl.CostEstimate(
            flops=2 * first.size * right.shape[0],
            bytes_accessed=6 * first.size,
            transcendentals=0,
        ),
        name="pair_rows",
    )(blocks, queries, first, right, minus, single)


def shards(
    hidden_states,
    layer_mix,
    norm_gain,
    norm_bias,
    proj_in,
    proj_in_bias,
    proj_out,
    proj_out_bias,
    residue_tokens,
    residue_table,
    pair_norm_gain,
    pair_norm_bias,
    qk_weight,
    qk_bias,
    pair_weight,
    relpos_bins,
    relpos_table,
    chain_ids,
    chain_table,
):
    device_count = lax.axis_size("seq")
    single, queries, copies, first, right, minus = single_part(
        device_count,
        (
            hidden_states, layer_mix, norm_gain, norm_bias, proj_in, proj_in_bias, proj_out,
            proj_out_bias, residue_tokens, residue_table, pair_norm_gain, pair_norm_bias,
            qk_weight, qk_bias, chain_ids, relpos_bins, pair_weight, relpos_table, chain_table,
        ),
    )
    falling = list(reversed(range(device_count)))
    blocks = lax.all_to_all(
        copies, "seq", split_axis=0, concat_axis=0, axis_index_groups=[falling]
    )
    return pair_part(blocks, queries, first, right, minus, single)


def solution(mesh):
    in_specs = (
        P(None, ("groups", "seq"), None),
        P(),
        P(),
        P(),
        P(),
        P(),
        P(),
        P(),
        P(("groups", "seq")),
        P(),
        P(),
        P(),
        P(),
        P(),
        P(),
        P(("groups", "seq"), None),
        P(),
        P(("groups", "seq")),
        P(),
    )
    out_specs = (P(("groups", "seq"), None), P(("groups", "seq"), None, None))
    return jax.shard_map(shards, mesh=mesh, in_specs=in_specs, out_specs=out_specs, check_vma=False)
```

```python
import functools

import jax
import jax.numpy as jnp
from jax import lax
from jax.experimental import pallas as pl
from jax.experimental.pallas import tpu as pltpu
from jax.sharding import PartitionSpec as P

epsilon = 1e-05
BF16 = jnp.bfloat16
F32 = jnp.float32


def pieces(total, count):
    count = max(1, min(count, total))
    ends = [total * step // count for step in range(count + 1)]
    return [(low, high - low) for low, high in zip(ends[:-1], ends[1:])]


def row_norm(values, gain, bias):
    center = values - jnp.mean(values, axis=-1, keepdims=True)
    spread = jnp.mean(center * center, axis=-1, keepdims=True)
    return center * lax.rsqrt(spread + epsilon) * gain + bias


def chain_flags(chain, tok_count, inner_dim):
    lanes = lax.broadcasted_iota(jnp.int32, (tok_count, 2 * inner_dim), 1)
    flag = lax.rem(lanes, inner_dim // 2).astype(F32)
    square = (tok_count, tok_count)
    own = lax.broadcasted_iota(jnp.int32, square, 0) == lax.broadcasted_iota(jnp.int32, square, 1)
    chain_col = jnp.sum(jnp.where(own, chain[...].astype(F32), 0.0), axis=1, keepdims=True)
    return jnp.where(flag == chain_col, 1.0, 0.0)


def operand_rows(bins, pair_weight, relpos, chain_table, bin_rows, right, minus, tok_count):
    bin_count = relpos.shape[0]
    inner_dim = pair_weight.shape[0] // 2
    flag_count = inner_dim // 2
    step = chain_table[1:2, :] - chain_table[0:1, :]
    step_high = step.astype(BF16).astype(F32)
    shape = (flag_count, step.shape[1])
    right[0:inner_dim, :] = pair_weight[0:inner_dim, :]
    right[inner_dim:inner_dim + flag_count, :] = jnp.broadcast_to(step_high, shape).astype(BF16)
    right[inner_dim + flag_count:, :] = jnp.broadcast_to(step - step_high, shape).astype(BF16)
    minus[0:inner_dim, :] = pair_weight[inner_dim:, :]
    minus[inner_dim:, :] = jnp.zeros((inner_dim, step.shape[1]), BF16)
    bin_rows[...] = jnp.zeros(bin_rows.shape, F32)
    bin_rows[0:bin_count, :] = relpos[...] + chain_table[0:1, :]
    padded = jnp.concatenate(
        [bins[...], jnp.zeros((128 - tok_count, bins.shape[1]), jnp.int32)], axis=0
    )
    return padded.T


def single_kernel(
    plan,
    hidden_hbm, mix_hbm, norm_gain_hbm, norm_bias_hbm, proj_in_hbm, proj_in_bias_hbm,
    proj_out_hbm, proj_out_bias_hbm, tokens_hbm, residue_hbm, pair_gain_hbm, pair_bias_hbm,
    qk_hbm, qk_bias_hbm, chain_hbm, bins_hbm, pair_weight_hbm, relpos_hbm, chain_table_hbm,
    single, query_ref, copies_ref, first, right, minus,
    hidden, mix, norm_gain, norm_bias, proj_in, proj_in_bias, proj_out, proj_out_bias, tokens,
    residue, pair_gain, pair_bias, qk, qk_bias, chain, bins, pair_weight, relpos, chain_table,
    mixture, residue_rows, bin_rows, sem_hidden, sem_in, sem_out, sem_small,
):
    state_pieces, in_pieces, out_pieces, lane_step = plan
    tok_count = mixture.shape[0]
    inner_dim = qk.shape[1] // 2

    small = [
        (mix_hbm, mix), (tokens_hbm, tokens), (residue_hbm, residue),
        (norm_gain_hbm, norm_gain), (norm_bias_hbm, norm_bias),
        (proj_in_bias_hbm, proj_in_bias), (proj_out_bias_hbm, proj_out_bias),
        (pair_gain_hbm, pair_gain), (pair_bias_hbm, pair_bias),
        (qk_hbm, qk), (qk_bias_hbm, qk_bias), (chain_hbm, chain), (bins_hbm, bins),
        (pair_weight_hbm, pair_weight), (relpos_hbm, relpos), (chain_table_hbm, chain_table),
    ]
    small = [
        pltpu.make_async_copy(source, target, sem_small.at[at])
        for at, (source, target) in enumerate(small)
    ]
    states = [
        pltpu.make_async_copy(
            hidden_hbm.at[pl.ds(low, size)], hidden.at[pl.ds(low, size)], sem_hidden.at[at]
        )
        for at, (low, size) in enumerate(state_pieces)
    ]
    firsts = [
        pltpu.make_async_copy(
            proj_in_hbm.at[pl.ds(low, size)], proj_in.at[pl.ds(low, size)], sem_in.at[at]
        )
        for at, (low, size) in enumerate(in_pieces)
    ]
    seconds = [
        pltpu.make_async_copy(
            proj_out_hbm.at[pl.ds(low, size)], proj_out.at[pl.ds(low, size)], sem_out.at[at]
        )
        for at, (low, size) in enumerate(out_pieces)
    ]
    small[0].start()
    for copy in states:
        copy.start()
    firsts[0].start()
    for copy in small[1:]:
        copy.start()
    later = firsts[1:] + seconds

    small[0].wait()
    width = mixture.shape[1]
    for at, (low, size) in enumerate(state_pieces):
        states[at].wait()
        last = at == len(state_pieces) - 1
        for copy in later if last else later[:1]:
            copy.start()
        later = later[1:]
        for lane in range(0, width, lane_step):
            span = slice(lane, min(lane + lane_step, width))
            total = mixture[:, span] if at else None
            for state in range(low, low + size):
                term = mix[state] * hidden[state, :, span].astype(F32)
                total = term if total is None else total + term
            mixture[:, span] = total

    for copy in small[1:]:
        copy.wait()
    normed = row_norm(
        mixture[...], norm_gain[...].reshape(1, width), norm_bias[...].reshape(1, width)
    ).astype(BF16)
    bins_col = operand_rows(
        bins, pair_weight, relpos, chain_table, bin_rows, right, minus, tok_count
    )
    flags = chain_flags(chain, tok_count, inner_dim)
    bin_table = bin_rows[...].astype(BF16)
    lanes = lax.broadcasted_iota(jnp.int32, (bins_col.shape[0], bin_table.shape[0]), 1)
    row_pieces = pieces(tok_count, max(1, len(in_pieces) - 1))
    total = None
    for at, (low, size) in enumerate(in_pieces):
        firsts[at].wait()
        term = jnp.dot(
            normed[:, low:low + size], proj_in[pl.ds(low, size), :], preferred_element_type=F32
        )
        total = term if total is None else total + term
        if at < len(row_pieces):
            for row in range(row_pieces[at][0], sum(row_pieces[at])):
                onehot = jnp.where(bins_col[:, row:row + 1] == lanes, 1.0, 0.0).astype(BF16)
                first[row] = jnp.dot(onehot, bin_table, preferred_element_type=F32)
    for row in range(tok_count):
        residue_rows[pl.ds(row, 1), :] = residue[pl.ds(tokens[row], 1), :]
    middle = jnp.maximum(total + proj_in_bias[...], 0.0).astype(BF16)

    total = None
    for at, (low, size) in enumerate(out_pieces):
        seconds[at].wait()
        term = jnp.dot(
            middle[:, low:low + size], proj_out[pl.ds(low, size), :], preferred_element_type=F32
        )
        total = term if total is None else total + term
    single_f = total + proj_out_bias[...] + residue_rows[...]
    single[...] = single_f.astype(BF16)

    pair_in = row_norm(single_f, pair_gain[...], pair_bias[...]).astype(BF16)
    query_key = jnp.dot(pair_in, qk[...], preferred_element_type=F32) + qk_bias[...]

    front = lax.broadcasted_iota(jnp.int32, flags.shape, 1) < inner_dim
    query_ref[...] = jnp.where(front, query_key, flags).astype(BF16)
    block = jnp.where(front, pltpu.roll(query_key, inner_dim, 1), flags).astype(BF16)
    for peer in range(copies_ref.shape[0]):
        copies_ref[peer] = block


def single_part(device_count, operands):
    (hidden, mix, norm_gain, norm_bias, proj_in, proj_in_bias, proj_out, proj_out_bias, tokens,
     residue, pair_gain, pair_bias, qk, qk_bias, chain, bins, pair_weight, relpos,
     chain_table) = operands
    state_count, tok_count, width = hidden.shape
    channels = proj_out.shape[1]
    lanes = qk.shape[1]
    table_rows = -(-relpos.shape[0] // 128) * 128
    vmem = pl.BlockSpec(memory_space=pltpu.VMEM)
    plan = (pieces(state_count, 6), pieces(width, 5), pieces(channels, 2), 512)
    args = (
        hidden, mix, norm_gain, norm_bias, proj_in, proj_in_bias[None],
        proj_out, proj_out_bias[None], tokens, residue, pair_gain[None], pair_bias[None],
        qk, qk_bias[None], chain[None], bins, pair_weight, relpos, chain_table,
    )
    args = [pltpu.with_memory_space_constraint(arg, pltpu.HBM) for arg in args]
    in_smem = (1, 8)
    scratch = [
        (pltpu.SMEM if at in in_smem else pltpu.VMEM)(arg.shape, arg.dtype)
        for at, arg in enumerate(args)
    ]
    scratch += [
        pltpu.VMEM((tok_count, width), F32),
        pltpu.VMEM((tok_count, channels), F32),
        pltpu.VMEM((table_rows, pair_weight.shape[1]), F32),
        pltpu.SemaphoreType.DMA((len(plan[0]),)),
        pltpu.SemaphoreType.DMA((len(plan[1]),)),
        pltpu.SemaphoreType.DMA((len(plan[2]),)),
        pltpu.SemaphoreType.DMA((16,)),
    ]
    moved = sum(arg.size * arg.dtype.itemsize for arg in args)
    return pl.pallas_call(
        functools.partial(single_kernel, plan),
        out_shape=(
            jax.ShapeDtypeStruct((tok_count, channels), BF16),
            jax.ShapeDtypeStruct((tok_count, lanes), BF16),
            jax.ShapeDtypeStruct((device_count, tok_count, lanes), BF16),
            jax.ShapeDtypeStruct(bins.shape + pair_weight.shape[1:], F32),
            jax.ShapeDtypeStruct(pair_weight.shape, BF16),
            jax.ShapeDtypeStruct(pair_weight.shape, BF16),
        ),
        in_specs=[pl.BlockSpec(memory_space=pltpu.HBM)] * len(args),
        out_specs=(vmem,) * 6,
        scratch_shapes=scratch,
        compiler_params=pltpu.CompilerParams(vmem_limit_bytes=32 * 2**20),
        cost_estimate=pl.CostEstimate(
            flops=2 * tok_count * channels * (width + channels + lanes),
            bytes_accessed=moved,
            transcendentals=0,
        ),
        name="single_path",
    )(*args)


def pair_kernel(
    blocks, queries, first, right, minus, single, single_hbm, pair_hbm, pair, sem, sem_single
):
    single_copy = pltpu.make_async_copy(single, single_hbm, sem_single)
    single_copy.start()
    keys = jnp.concatenate([blocks[1:].reshape(-1, blocks.shape[2]), blocks[0]], axis=0)
    row_diff = jnp.dot(queries[...], minus[...], preferred_element_type=F32)
    col_diff = jnp.dot(keys, minus[...], preferred_element_type=F32)
    copies = []
    for row in range(first.shape[0]):
        products = keys * queries[row:row + 1, :]
        value = jnp.dot(products, right[...], preferred_element_type=F32)
        value = value + first[row] + (row_diff[row:row + 1, :] - col_diff)
        pair[row] = value.astype(BF16)
        copy = pltpu.make_async_copy(pair.at[row], pair_hbm.at[row], sem.at[row])
        copy.start()
        copies.append(copy)
    for copy in copies:
        copy.wait()
    single_copy.wait()


def pair_part(blocks, queries, first, right, minus, single):
    tok_count = first.shape[0]
    vmem = pl.BlockSpec(memory_space=pltpu.VMEM)
    return pl.pallas_call(
        pair_kernel,
        out_shape=(
            jax.ShapeDtypeStruct(single.shape, BF16),
            jax.ShapeDtypeStruct(first.shape, BF16),
        ),
        in_specs=[vmem] * 6,
        out_specs=(pl.BlockSpec(memory_space=pltpu.HBM),) * 2,
        scratch_shapes=[
            pltpu.VMEM(first.shape, BF16),
            pltpu.SemaphoreType.DMA((tok_count,)),
            pltpu.SemaphoreType.DMA,
        ],
        compiler_params=pltpu.CompilerParams(vmem_limit_bytes=32 * 2**20),
        cost_estimate=pl.CostEstimate(
            flops=2 * first.size * right.shape[0],
            bytes_accessed=6 * first.size,
            transcendentals=0,
        ),
        name="pair_rows",
    )(blocks, queries, first, right, minus, single)


def shards(
    hidden_states,
    layer_mix,
    norm_gain,
    norm_bias,
    proj_in,
    proj_in_bias,
    proj_out,
    proj_out_bias,
    residue_tokens,
    residue_table,
    pair_norm_gain,
    pair_norm_bias,
    qk_weight,
    qk_bias,
    pair_weight,
    relpos_bins,
    relpos_table,
    chain_ids,
    chain_table,
):
    device_count = lax.axis_size("seq")
    single, queries, copies, first, right, minus = single_part(
        device_count,
        (
            hidden_states, layer_mix, norm_gain, norm_bias, proj_in, proj_in_bias, proj_out,
            proj_out_bias, residue_tokens, residue_table, pair_norm_gain, pair_norm_bias,
            qk_weight, qk_bias, chain_ids, relpos_bins, pair_weight, relpos_table, chain_table,
        ),
    )
    order = [device_count - 1] + list(range(device_count - 1))
    blocks = lax.all_to_all(
        copies, "seq", split_axis=0, concat_axis=0, axis_index_groups=[order]
    )
    return pair_part(blocks, queries, first, right, minus, single)


def solution(mesh):
    in_specs = (
        P(None, ("groups", "seq"), None),
        P(),
        P(),
        P(),
        P(),
        P(),
        P(),
        P(),
        P(("groups", "seq")),
        P(),
        P(),
        P(),
        P(),
        P(),
        P(),
        P(("groups", "seq"), None),
        P(),
        P(("groups", "seq")),
        P(),
    )
    out_specs = (P(("groups", "seq"), None), P(("groups", "seq"), None, None))
    return jax.shard_map(shards, mesh=mesh, in_specs=in_specs, out_specs=out_specs, check_vma=False)
```

```python
import functools

import jax
import jax.numpy as jnp
from jax import lax
from jax.experimental import pallas as pl
from jax.experimental.pallas import tpu as pltpu
from jax.sharding import PartitionSpec as P

epsilon = 1e-05
BF16 = jnp.bfloat16
F32 = jnp.float32


def pieces(total, count):
    count = max(1, min(count, total))
    ends = [total * step // count for step in range(count + 1)]
    return [(low, high - low) for low, high in zip(ends[:-1], ends[1:])]


def row_norm(values, gain, bias):
    center = values - jnp.mean(values, axis=-1, keepdims=True)
    spread = jnp.mean(center * center, axis=-1, keepdims=True)
    return center * lax.rsqrt(spread + epsilon) * gain + bias


def chain_flags(chain, tok_count, inner_dim):
    lanes = lax.broadcasted_iota(jnp.int32, (tok_count, 2 * inner_dim), 1)
    flag = lax.rem(lanes, inner_dim // 2).astype(F32)
    square = (tok_count, tok_count)
    own = lax.broadcasted_iota(jnp.int32, square, 0) == lax.broadcasted_iota(jnp.int32, square, 1)
    chain_col = jnp.sum(jnp.where(own, chain[...].astype(F32), 0.0), axis=1, keepdims=True)
    return jnp.where(flag == chain_col, 1.0, 0.0)


def operand_rows(bins, pair_weight, relpos, chain_table, bin_rows, right, minus, tok_count):
    bin_count = relpos.shape[0]
    inner_dim = pair_weight.shape[0] // 2
    flag_count = inner_dim // 2
    step = chain_table[1:2, :] - chain_table[0:1, :]
    step_high = step.astype(BF16).astype(F32)
    shape = (flag_count, step.shape[1])
    right[0:inner_dim, :] = pair_weight[0:inner_dim, :]
    right[inner_dim:inner_dim + flag_count, :] = jnp.broadcast_to(step_high, shape).astype(BF16)
    right[inner_dim + flag_count:, :] = jnp.broadcast_to(step - step_high, shape).astype(BF16)
    minus[0:inner_dim, :] = pair_weight[inner_dim:, :]
    minus[inner_dim:, :] = jnp.zeros((inner_dim, step.shape[1]), BF16)
    bin_rows[...] = jnp.zeros(bin_rows.shape, F32)
    bin_rows[0:bin_count, :] = relpos[...] + chain_table[0:1, :]
    padded = jnp.concatenate(
        [bins[...], jnp.zeros((128 - tok_count, bins.shape[1]), jnp.int32)], axis=0
    )
    return padded.T


def single_kernel(
    plan,
    hidden_hbm, mix_hbm, norm_gain_hbm, norm_bias_hbm, proj_in_hbm, proj_in_bias_hbm,
    proj_out_hbm, proj_out_bias_hbm, tokens_hbm, residue_hbm, pair_gain_hbm, pair_bias_hbm,
    qk_hbm, qk_bias_hbm, chain_hbm, bins_hbm, pair_weight_hbm, relpos_hbm, chain_table_hbm,
    single, query_ref, copies_ref, first, right, minus,
    hidden, mix, norm_gain, norm_bias, proj_in, proj_in_bias, proj_out, proj_out_bias, tokens,
    residue, pair_gain, pair_bias, qk, qk_bias, chain, bins, pair_weight, relpos, chain_table,
    mixture, residue_rows, bin_rows, sem_hidden, sem_in, sem_out, sem_small,
):
    state_pieces, in_pieces, out_pieces, lane_step = plan
    tok_count = mixture.shape[0]
    inner_dim = qk.shape[1] // 2

    small = [
        (mix_hbm, mix), (bins_hbm, bins), (relpos_hbm, relpos), (chain_table_hbm, chain_table),
        (pair_weight_hbm, pair_weight), (chain_hbm, chain), (norm_gain_hbm, norm_gain),
        (norm_bias_hbm, norm_bias), (tokens_hbm, tokens), (residue_hbm, residue),
        (proj_in_bias_hbm, proj_in_bias), (proj_out_bias_hbm, proj_out_bias),
        (pair_gain_hbm, pair_gain), (pair_bias_hbm, pair_bias),
        (qk_hbm, qk), (qk_bias_hbm, qk_bias),
    ]
    first_small = 6
    small = [
        pltpu.make_async_copy(source, target, sem_small.at[at])
        for at, (source, target) in enumerate(small)
    ]
    states = [
        pltpu.make_async_copy(
            hidden_hbm.at[pl.ds(low, size)], hidden.at[pl.ds(low, size)], sem_hidden.at[at]
        )
        for at, (low, size) in enumerate(state_pieces)
    ]
    firsts = [
        pltpu.make_async_copy(
            proj_in_hbm.at[pl.ds(low, size)], proj_in.at[pl.ds(low, size)], sem_in.at[at]
        )
        for at, (low, size) in enumerate(in_pieces)
    ]
    seconds = [
        pltpu.make_async_copy(
            proj_out_hbm.at[pl.ds(low, size)], proj_out.at[pl.ds(low, size)], sem_out.at[at]
        )
        for at, (low, size) in enumerate(out_pieces)
    ]
    small[0].start()
    states[0].start()
    for copy in small[1:first_small] + states[1:] + firsts[:2] + small[first_small:]:
        copy.start()
    later = firsts[2:] + seconds
    per_piece = -(-len(later) // len(states))

    width = mixture.shape[1]
    row_pieces = pieces(tok_count, len(states) + len(in_pieces) - 2)

    def bins_rows(at):
        if at < len(row_pieces):
            for row in range(row_pieces[at][0], sum(row_pieces[at])):
                onehot = jnp.where(bins_col[:, row:row + 1] == lanes, 1.0, 0.0).astype(BF16)
                first[row] = jnp.dot(onehot, bin_table, preferred_element_type=F32)

    small[0].wait()
    for at, (low, size) in enumerate(state_pieces):
        states[at].wait()
        for copy in later[:per_piece]:
            copy.start()
        later = later[per_piece:]
        for lane in range(0, width, lane_step):
            span = slice(lane, min(lane + lane_step, width))
            total = mixture[:, span] if at else None
            for state in range(low, low + size):
                term = mix[state] * hidden[state, :, span].astype(F32)
                total = term if total is None else total + term
            mixture[:, span] = total
        if at == 0:
            for copy in small[1:first_small]:
                copy.wait()
            bins_col = operand_rows(
                bins, pair_weight, relpos, chain_table, bin_rows, right, minus, tok_count
            )
            flags = chain_flags(chain, tok_count, inner_dim)
            bin_table = bin_rows[...].astype(BF16)
            lanes = lax.broadcasted_iota(jnp.int32, (bins_col.shape[0], bin_table.shape[0]), 1)
        if at < len(states) - 1:
            bins_rows(at)

    for copy in small[first_small:]:
        copy.wait()
    normed = row_norm(
        mixture[...], norm_gain[...].reshape(1, width), norm_bias[...].reshape(1, width)
    ).astype(BF16)
    total = None
    for at, (low, size) in enumerate(in_pieces):
        firsts[at].wait()
        term = jnp.dot(
            normed[:, low:low + size], proj_in[pl.ds(low, size), :], preferred_element_type=F32
        )
        total = term if total is None else total + term
        bins_rows(len(states) - 1 + at)
    for row in range(tok_count):
        residue_rows[pl.ds(row, 1), :] = residue[pl.ds(tokens[row], 1), :]
    middle = jnp.maximum(total + proj_in_bias[...], 0.0).astype(BF16)

    total = None
    for at, (low, size) in enumerate(out_pieces):
        seconds[at].wait()
        term = jnp.dot(
            middle[:, low:low + size], proj_out[pl.ds(low, size), :], preferred_element_type=F32
        )
        total = term if total is None else total + term
    single_f = total + proj_out_bias[...] + residue_rows[...]
    single[...] = single_f.astype(BF16)

    pair_in = row_norm(single_f, pair_gain[...], pair_bias[...]).astype(BF16)
    query_key = jnp.dot(pair_in, qk[...], preferred_element_type=F32) + qk_bias[...]

    front = lax.broadcasted_iota(jnp.int32, flags.shape, 1) < inner_dim
    query_ref[...] = jnp.where(front, query_key, flags).astype(BF16)
    block = jnp.where(front, pltpu.roll(query_key, inner_dim, 1), flags).astype(BF16)
    for peer in range(copies_ref.shape[0]):
        copies_ref[peer] = block


def single_part(device_count, operands):
    (hidden, mix, norm_gain, norm_bias, proj_in, proj_in_bias, proj_out, proj_out_bias, tokens,
     residue, pair_gain, pair_bias, qk, qk_bias, chain, bins, pair_weight, relpos,
     chain_table) = operands
    state_count, tok_count, width = hidden.shape
    channels = proj_out.shape[1]
    lanes = qk.shape[1]
    table_rows = -(-relpos.shape[0] // 128) * 128
    vmem = pl.BlockSpec(memory_space=pltpu.VMEM)
    plan = (pieces(state_count, 6), pieces(width, 10), pieces(channels, 4), 512)
    args = (
        hidden, mix, norm_gain, norm_bias, proj_in, proj_in_bias[None],
        proj_out, proj_out_bias[None], tokens, residue, pair_gain[None], pair_bias[None],
        qk, qk_bias[None], chain[None], bins, pair_weight, relpos, chain_table,
    )
    args = [pltpu.with_memory_space_constraint(arg, pltpu.HBM) for arg in args]
    in_smem = (1, 8)
    scratch = [
        (pltpu.SMEM if at in in_smem else pltpu.VMEM)(arg.shape, arg.dtype)
        for at, arg in enumerate(args)
    ]
    scratch += [
        pltpu.VMEM((tok_count, width), F32),
        pltpu.VMEM((tok_count, channels), F32),
        pltpu.VMEM((table_rows, pair_weight.shape[1]), F32),
        pltpu.SemaphoreType.DMA((len(plan[0]),)),
        pltpu.SemaphoreType.DMA((len(plan[1]),)),
        pltpu.SemaphoreType.DMA((len(plan[2]),)),
        pltpu.SemaphoreType.DMA((16,)),
    ]
    moved = sum(arg.size * arg.dtype.itemsize for arg in args)
    return pl.pallas_call(
        functools.partial(single_kernel, plan),
        out_shape=(
            jax.ShapeDtypeStruct((tok_count, channels), BF16),
            jax.ShapeDtypeStruct((tok_count, lanes), BF16),
            jax.ShapeDtypeStruct((device_count, tok_count, lanes), BF16),
            jax.ShapeDtypeStruct(bins.shape + pair_weight.shape[1:], F32),
            jax.ShapeDtypeStruct(pair_weight.shape, BF16),
            jax.ShapeDtypeStruct(pair_weight.shape, BF16),
        ),
        in_specs=[pl.BlockSpec(memory_space=pltpu.HBM)] * len(args),
        out_specs=(vmem,) * 6,
        scratch_shapes=scratch,
        compiler_params=pltpu.CompilerParams(vmem_limit_bytes=32 * 2**20),
        cost_estimate=pl.CostEstimate(
            flops=2 * tok_count * channels * (width + channels + lanes),
            bytes_accessed=moved,
            transcendentals=0,
        ),
        name="single_path",
    )(*args)


def pair_kernel(
    blocks, queries, first, right, minus, single, single_hbm, pair_hbm, pair, sem, sem_single
):
    single_copy = pltpu.make_async_copy(single, single_hbm, sem_single)
    single_copy.start()
    keys = jnp.concatenate([blocks[1:].reshape(-1, blocks.shape[2]), blocks[0]], axis=0)
    row_diff = jnp.dot(queries[...], minus[...], preferred_element_type=F32)
    col_diff = jnp.dot(keys, minus[...], preferred_element_type=F32)
    copies = []
    for row in range(first.shape[0]):
        products = keys * queries[row:row + 1, :]
        value = jnp.dot(products, right[...], preferred_element_type=F32)
        value = value + first[row] + (row_diff[row:row + 1, :] - col_diff)
        pair[row] = value.astype(BF16)
        copy = pltpu.make_async_copy(pair.at[row], pair_hbm.at[row], sem.at[row])
        copy.start()
        copies.append(copy)
    for copy in copies:
        copy.wait()
    single_copy.wait()


def pair_part(blocks, queries, first, right, minus, single):
    tok_count = first.shape[0]
    vmem = pl.BlockSpec(memory_space=pltpu.VMEM)
    return pl.pallas_call(
        pair_kernel,
        out_shape=(
            jax.ShapeDtypeStruct(single.shape, BF16),
            jax.ShapeDtypeStruct(first.shape, BF16),
        ),
        in_specs=[vmem] * 6,
        out_specs=(pl.BlockSpec(memory_space=pltpu.HBM),) * 2,
        scratch_shapes=[
            pltpu.VMEM(first.shape, BF16),
            pltpu.SemaphoreType.DMA((tok_count,)),
            pltpu.SemaphoreType.DMA,
        ],
        compiler_params=pltpu.CompilerParams(vmem_limit_bytes=32 * 2**20),
        cost_estimate=pl.CostEstimate(
            flops=2 * first.size * right.shape[0],
            bytes_accessed=6 * first.size,
            transcendentals=0,
        ),
        name="pair_rows",
    )(blocks, queries, first, right, minus, single)


def shards(
    hidden_states,
    layer_mix,
    norm_gain,
    norm_bias,
    proj_in,
    proj_in_bias,
    proj_out,
    proj_out_bias,
    residue_tokens,
    residue_table,
    pair_norm_gain,
    pair_norm_bias,
    qk_weight,
    qk_bias,
    pair_weight,
    relpos_bins,
    relpos_table,
    chain_ids,
    chain_table,
):
    device_count = lax.axis_size("seq")
    single, queries, copies, first, right, minus = single_part(
        device_count,
        (
            hidden_states, layer_mix, norm_gain, norm_bias, proj_in, proj_in_bias, proj_out,
            proj_out_bias, residue_tokens, residue_table, pair_norm_gain, pair_norm_bias,
            qk_weight, qk_bias, chain_ids, relpos_bins, pair_weight, relpos_table, chain_table,
        ),
    )
    order = [device_count - 1] + list(range(device_count - 1))
    blocks = lax.all_to_all(
        copies, "seq", split_axis=0, concat_axis=0, axis_index_groups=[order]
    )
    return pair_part(blocks, queries, first, right, minus, single)


def solution(mesh):
    in_specs = (
        P(None, ("groups", "seq"), None),
        P(),
        P(),
        P(),
        P(),
        P(),
        P(),
        P(),
        P(("groups", "seq")),
        P(),
        P(),
        P(),
        P(),
        P(),
        P(),
        P(("groups", "seq"), None),
        P(),
        P(("groups", "seq")),
        P(),
    )
    out_specs = (P(("groups", "seq"), None), P(("groups", "seq"), None, None))
    return jax.shard_map(shards, mesh=mesh, in_specs=in_specs, out_specs=out_specs, check_vma=False)
```

```python
import functools

import jax
import jax.numpy as jnp
from jax import lax
from jax.experimental import pallas as pl
from jax.experimental.pallas import tpu as pltpu
from jax.sharding import PartitionSpec as P

epsilon = 1e-05
BF16 = jnp.bfloat16
F32 = jnp.float32


def pieces(total, count):
    count = max(1, min(count, total))
    ends = [total * step // count for step in range(count + 1)]
    return [(low, high - low) for low, high in zip(ends[:-1], ends[1:])]


def row_norm(values, gain, bias):
    center = values - jnp.mean(values, axis=-1, keepdims=True)
    spread = jnp.mean(center * center, axis=-1, keepdims=True)
    return center * lax.rsqrt(spread + epsilon) * gain + bias


def chain_flags(chain, tok_count, inner_dim):
    lanes = lax.broadcasted_iota(jnp.int32, (tok_count, 2 * inner_dim), 1)
    flag = lax.rem(lanes, inner_dim // 2).astype(F32)
    square = (tok_count, tok_count)
    own = lax.broadcasted_iota(jnp.int32, square, 0) == lax.broadcasted_iota(jnp.int32, square, 1)
    chain_col = jnp.sum(jnp.where(own, chain[...].astype(F32), 0.0), axis=1, keepdims=True)
    return jnp.where(flag == chain_col, 1.0, 0.0)


def operand_rows(bins, pair_weight, relpos, chain_table, bin_rows, right, minus, tok_count):
    bin_count = relpos.shape[0]
    inner_dim = pair_weight.shape[0] // 2
    flag_count = inner_dim // 2
    step = chain_table[1:2, :] - chain_table[0:1, :]
    step_high = step.astype(BF16).astype(F32)
    shape = (flag_count, step.shape[1])
    right[0:inner_dim, :] = pair_weight[0:inner_dim, :]
    right[inner_dim:inner_dim + flag_count, :] = jnp.broadcast_to(step_high, shape).astype(BF16)
    right[inner_dim + flag_count:, :] = jnp.broadcast_to(step - step_high, shape).astype(BF16)
    minus[0:inner_dim, :] = pair_weight[inner_dim:, :]
    minus[inner_dim:, :] = jnp.zeros((inner_dim, step.shape[1]), BF16)
    bin_rows[...] = jnp.zeros(bin_rows.shape, F32)
    bin_rows[0:bin_count, :] = relpos[...] + chain_table[0:1, :]
    padded = jnp.concatenate(
        [bins[...], jnp.zeros((128 - tok_count, bins.shape[1]), jnp.int32)], axis=0
    )
    return padded.T


def single_kernel(
    plan,
    hidden_hbm, mix_hbm, norm_gain_hbm, norm_bias_hbm, proj_in_hbm, proj_in_bias_hbm,
    proj_out_hbm, proj_out_bias_hbm, tokens_hbm, residue_hbm, pair_gain_hbm, pair_bias_hbm,
    qk_hbm, qk_bias_hbm, chain_hbm, bins_hbm, pair_weight_hbm, relpos_hbm, chain_table_hbm,
    single, query_ref, copies_ref, first, right, minus,
    hidden, mix, norm_gain, norm_bias, proj_in, proj_in_bias, proj_out, proj_out_bias, tokens,
    residue, pair_gain, pair_bias, qk, qk_bias, chain, bins, pair_weight, relpos, chain_table,
    mixture, residue_rows, bin_rows, sem_hidden, sem_in, sem_out, sem_small,
):
    state_pieces, in_pieces, out_pieces, lane_step = plan
    tok_count = mixture.shape[0]
    inner_dim = qk.shape[1] // 2

    small = [
        (mix_hbm, mix), (bins_hbm, bins), (relpos_hbm, relpos), (chain_table_hbm, chain_table),
        (pair_weight_hbm, pair_weight), (chain_hbm, chain), (norm_gain_hbm, norm_gain),
        (norm_bias_hbm, norm_bias), (tokens_hbm, tokens), (residue_hbm, residue),
        (proj_in_bias_hbm, proj_in_bias), (proj_out_bias_hbm, proj_out_bias),
        (pair_gain_hbm, pair_gain), (pair_bias_hbm, pair_bias),
        (qk_hbm, qk), (qk_bias_hbm, qk_bias),
    ]
    first_small = 6
    small = [
        pltpu.make_async_copy(source, target, sem_small.at[at])
        for at, (source, target) in enumerate(small)
    ]
    states = [
        pltpu.make_async_copy(
            hidden_hbm.at[pl.ds(low, size)], hidden.at[pl.ds(low, size)], sem_hidden.at[at]
        )
        for at, (low, size) in enumerate(state_pieces)
    ]
    firsts = [
        pltpu.make_async_copy(
            proj_in_hbm.at[pl.ds(low, size)], proj_in.at[pl.ds(low, size)], sem_in.at[at]
        )
        for at, (low, size) in enumerate(in_pieces)
    ]
    seconds = [
        pltpu.make_async_copy(
            proj_out_hbm.at[pl.ds(low, size)], proj_out.at[pl.ds(low, size)], sem_out.at[at]
        )
        for at, (low, size) in enumerate(out_pieces)
    ]
    for copy in small[:first_small] + states + firsts[:1] + small[first_small:]:
        copy.start()
    later = firsts[1:] + seconds

    for copy in small[:first_small]:
        copy.wait()
    bins_col = operand_rows(
        bins, pair_weight, relpos, chain_table, bin_rows, right, minus, tok_count
    )
    bin_table = bin_rows[...].astype(BF16)
    lanes = lax.broadcasted_iota(jnp.int32, (bins_col.shape[0], bin_table.shape[0]), 1)
    for row in range(tok_count):
        onehot = jnp.where(bins_col[:, row:row + 1] == lanes, 1.0, 0.0).astype(BF16)
        first[row] = jnp.dot(onehot, bin_table, preferred_element_type=F32)
    flags = chain_flags(chain, tok_count, inner_dim)

    width = mixture.shape[1]
    for at, (low, size) in enumerate(state_pieces):
        states[at].wait()
        for copy in later if at else later[:1]:
            copy.start()
        later = later[1:]
        for lane in range(0, width, lane_step):
            span = slice(lane, min(lane + lane_step, width))
            total = mixture[:, span] if at else None
            for state in range(low, low + size):
                term = mix[state] * hidden[state, :, span].astype(F32)
                total = term if total is None else total + term
            mixture[:, span] = total

    for copy in small[first_small:]:
        copy.wait()
    normed = row_norm(
        mixture[...], norm_gain[...].reshape(1, width), norm_bias[...].reshape(1, width)
    ).astype(BF16)
    total = None
    for at, (low, size) in enumerate(in_pieces):
        firsts[at].wait()
        term = jnp.dot(
            normed[:, low:low + size], proj_in[pl.ds(low, size), :], preferred_element_type=F32
        )
        total = term if total is None else total + term
    for row in range(tok_count):
        residue_rows[pl.ds(row, 1), :] = residue[pl.ds(tokens[row], 1), :]
    middle = jnp.maximum(total + proj_in_bias[...], 0.0).astype(BF16)

    total = None
    for at, (low, size) in enumerate(out_pieces):
        seconds[at].wait()
        term = jnp.dot(
            middle[:, low:low + size], proj_out[pl.ds(low, size), :], preferred_element_type=F32
        )
        total = term if total is None else total + term
    single_f = total + proj_out_bias[...] + residue_rows[...]
    single[...] = single_f.astype(BF16)

    pair_in = row_norm(single_f, pair_gain[...], pair_bias[...]).astype(BF16)
    query_key = jnp.dot(pair_in, qk[...], preferred_element_type=F32) + qk_bias[...]

    front = lax.broadcasted_iota(jnp.int32, flags.shape, 1) < inner_dim
    query_ref[...] = jnp.where(front, query_key, flags).astype(BF16)
    block = jnp.where(front, pltpu.roll(query_key, inner_dim, 1), flags).astype(BF16)
    for peer in range(copies_ref.shape[0]):
        copies_ref[peer] = block


def single_part(device_count, operands):
    (hidden, mix, norm_gain, norm_bias, proj_in, proj_in_bias, proj_out, proj_out_bias, tokens,
     residue, pair_gain, pair_bias, qk, qk_bias, chain, bins, pair_weight, relpos,
     chain_table) = operands
    state_count, tok_count, width = hidden.shape
    channels = proj_out.shape[1]
    lanes = qk.shape[1]
    table_rows = -(-relpos.shape[0] // 128) * 128
    vmem = pl.BlockSpec(memory_space=pltpu.VMEM)
    plan = (pieces(state_count, 2), pieces(width, 2), pieces(channels, 2), 512)
    args = (
        hidden, mix, norm_gain, norm_bias, proj_in, proj_in_bias[None],
        proj_out, proj_out_bias[None], tokens, residue, pair_gain[None], pair_bias[None],
        qk, qk_bias[None], chain[None], bins, pair_weight, relpos, chain_table,
    )
    args = [pltpu.with_memory_space_constraint(arg, pltpu.HBM) for arg in args]
    in_smem = (1, 8)
    scratch = [
        (pltpu.SMEM if at in in_smem else pltpu.VMEM)(arg.shape, arg.dtype)
        for at, arg in enumerate(args)
    ]
    scratch += [
        pltpu.VMEM((tok_count, width), F32),
        pltpu.VMEM((tok_count, channels), F32),
        pltpu.VMEM((table_rows, pair_weight.shape[1]), F32),
        pltpu.SemaphoreType.DMA((len(plan[0]),)),
        pltpu.SemaphoreType.DMA((len(plan[1]),)),
        pltpu.SemaphoreType.DMA((len(plan[2]),)),
        pltpu.SemaphoreType.DMA((16,)),
    ]
    moved = sum(arg.size * arg.dtype.itemsize for arg in args)
    return pl.pallas_call(
        functools.partial(single_kernel, plan),
        out_shape=(
            jax.ShapeDtypeStruct((tok_count, channels), BF16),
            jax.ShapeDtypeStruct((tok_count, lanes), BF16),
            jax.ShapeDtypeStruct((device_count, tok_count, lanes), BF16),
            jax.ShapeDtypeStruct(bins.shape + pair_weight.shape[1:], F32),
            jax.ShapeDtypeStruct(pair_weight.shape, BF16),
            jax.ShapeDtypeStruct(pair_weight.shape, BF16),
        ),
        in_specs=[pl.BlockSpec(memory_space=pltpu.HBM)] * len(args),
        out_specs=(vmem,) * 6,
        scratch_shapes=scratch,
        compiler_params=pltpu.CompilerParams(vmem_limit_bytes=32 * 2**20),
        cost_estimate=pl.CostEstimate(
            flops=2 * tok_count * channels * (width + channels + lanes),
            bytes_accessed=moved,
            transcendentals=0,
        ),
        name="single_path",
    )(*args)


def pair_kernel(
    blocks, queries, first, right, minus, single, single_hbm, pair_hbm, pair, sem, sem_single
):
    single_copy = pltpu.make_async_copy(single, single_hbm, sem_single)
    single_copy.start()
    keys = jnp.concatenate([blocks[1:].reshape(-1, blocks.shape[2]), blocks[0]], axis=0)
    row_diff = jnp.dot(queries[...], minus[...], preferred_element_type=F32)
    col_diff = jnp.dot(keys, minus[...], preferred_element_type=F32)
    copies = []
    for row in range(first.shape[0]):
        products = keys * queries[row:row + 1, :]
        value = jnp.dot(products, right[...], preferred_element_type=F32)
        value = value + first[row] + (row_diff[row:row + 1, :] - col_diff)
        pair[row] = value.astype(BF16)
        copy = pltpu.make_async_copy(pair.at[row], pair_hbm.at[row], sem.at[row])
        copy.start()
        copies.append(copy)
    for copy in copies:
        copy.wait()
    single_copy.wait()


def pair_part(blocks, queries, first, right, minus, single):
    tok_count = first.shape[0]
    vmem = pl.BlockSpec(memory_space=pltpu.VMEM)
    return pl.pallas_call(
        pair_kernel,
        out_shape=(
            jax.ShapeDtypeStruct(single.shape, BF16),
            jax.ShapeDtypeStruct(first.shape, BF16),
        ),
        in_specs=[vmem] * 6,
        out_specs=(pl.BlockSpec(memory_space=pltpu.HBM),) * 2,
        scratch_shapes=[
            pltpu.VMEM(first.shape, BF16),
            pltpu.SemaphoreType.DMA((tok_count,)),
            pltpu.SemaphoreType.DMA,
        ],
        compiler_params=pltpu.CompilerParams(vmem_limit_bytes=32 * 2**20),
        cost_estimate=pl.CostEstimate(
            flops=2 * first.size * right.shape[0],
            bytes_accessed=6 * first.size,
            transcendentals=0,
        ),
        name="pair_rows",
    )(blocks, queries, first, right, minus, single)


def shards(
    hidden_states,
    layer_mix,
    norm_gain,
    norm_bias,
    proj_in,
    proj_in_bias,
    proj_out,
    proj_out_bias,
    residue_tokens,
    residue_table,
    pair_norm_gain,
    pair_norm_bias,
    qk_weight,
    qk_bias,
    pair_weight,
    relpos_bins,
    relpos_table,
    chain_ids,
    chain_table,
):
    device_count = lax.axis_size("seq")
    single, queries, copies, first, right, minus = single_part(
        device_count,
        (
            hidden_states, layer_mix, norm_gain, norm_bias, proj_in, proj_in_bias, proj_out,
            proj_out_bias, residue_tokens, residue_table, pair_norm_gain, pair_norm_bias,
            qk_weight, qk_bias, chain_ids, relpos_bins, pair_weight, relpos_table, chain_table,
        ),
    )
    order = [device_count - 1] + list(range(device_count - 1))
    blocks = lax.all_to_all(
        copies, "seq", split_axis=0, concat_axis=0, axis_index_groups=[order]
    )
    return pair_part(blocks, queries, first, right, minus, single)


def solution(mesh):
    in_specs = (
        P(None, ("groups", "seq"), None),
        P(),
        P(),
        P(),
        P(),
        P(),
        P(),
        P(),
        P(("groups", "seq")),
        P(),
        P(),
        P(),
        P(),
        P(),
        P(),
        P(("groups", "seq"), None),
        P(),
        P(("groups", "seq")),
        P(),
    )
    out_specs = (P(("groups", "seq"), None), P(("groups", "seq"), None, None))
    return jax.shard_map(shards, mesh=mesh, in_specs=in_specs, out_specs=out_specs, check_vma=False)
```

```python
import functools

import jax
import jax.numpy as jnp
from jax import lax
from jax.experimental import pallas as pl
from jax.experimental.pallas import tpu as pltpu
from jax.sharding import PartitionSpec as P

epsilon = 1e-05
BF16 = jnp.bfloat16
F32 = jnp.float32


def pieces(total, count):
    count = max(1, min(count, total))
    ends = [total * step // count for step in range(count + 1)]
    return [(low, high - low) for low, high in zip(ends[:-1], ends[1:])]


def row_norm(values, gain, bias):
    center = values - jnp.mean(values, axis=-1, keepdims=True)
    spread = jnp.mean(center * center, axis=-1, keepdims=True)
    return center * lax.rsqrt(spread + epsilon) * gain + bias


def chain_flags(chain, tok_count, inner_dim):
    lanes = lax.broadcasted_iota(jnp.int32, (tok_count, 2 * inner_dim), 1)
    flag = lax.rem(lanes, inner_dim // 2).astype(F32)
    square = (tok_count, tok_count)
    own = lax.broadcasted_iota(jnp.int32, square, 0) == lax.broadcasted_iota(jnp.int32, square, 1)
    chain_col = jnp.sum(jnp.where(own, chain[...].astype(F32), 0.0), axis=1, keepdims=True)
    return jnp.where(flag == chain_col, 1.0, 0.0)


def operand_rows(bins, pair_weight, relpos, chain_table, bin_rows, right, minus, tok_count):
    bin_count = relpos.shape[0]
    inner_dim = pair_weight.shape[0] // 2
    flag_count = inner_dim // 2
    step = chain_table[1:2, :] - chain_table[0:1, :]
    step_high = step.astype(BF16).astype(F32)
    shape = (flag_count, step.shape[1])
    right[0:inner_dim, :] = pair_weight[0:inner_dim, :]
    right[inner_dim:inner_dim + flag_count, :] = jnp.broadcast_to(step_high, shape).astype(BF16)
    right[inner_dim + flag_count:, :] = jnp.broadcast_to(step - step_high, shape).astype(BF16)
    minus[0:inner_dim, :] = pair_weight[inner_dim:, :]
    minus[inner_dim:, :] = jnp.zeros((inner_dim, step.shape[1]), BF16)
    bin_rows[...] = jnp.zeros(bin_rows.shape, F32)
    bin_rows[0:bin_count, :] = relpos[...] + chain_table[0:1, :]
    padded = jnp.concatenate(
        [bins[...], jnp.zeros((128 - tok_count, bins.shape[1]), jnp.int32)], axis=0
    )
    return padded.T


def single_kernel(
    plan,
    hidden_hbm, mix_hbm, norm_gain_hbm, norm_bias_hbm, proj_in_hbm, proj_in_bias_hbm,
    proj_out_hbm, proj_out_bias_hbm, tokens_hbm, residue_hbm, pair_gain_hbm, pair_bias_hbm,
    qk_hbm, qk_bias_hbm, chain_hbm, bins_hbm, pair_weight_hbm, relpos_hbm, chain_table_hbm,
    single, query_ref, copies_ref, first, right, minus,
    hidden, mix, norm_gain, norm_bias, proj_in, proj_in_bias, proj_out, proj_out_bias, tokens,
    residue, pair_gain, pair_bias, qk, qk_bias, chain, bins, pair_weight, relpos, chain_table,
    mixture, residue_rows, bin_rows, sem_hidden, sem_in, sem_out, sem_small,
):
    state_pieces, in_pieces, out_pieces = plan
    tok_count = mixture.shape[0]
    inner_dim = qk.shape[1] // 2

    small = [
        (mix_hbm, mix), (tokens_hbm, tokens), (residue_hbm, residue),
        (norm_gain_hbm, norm_gain), (norm_bias_hbm, norm_bias),
        (proj_in_bias_hbm, proj_in_bias), (proj_out_bias_hbm, proj_out_bias),
        (pair_gain_hbm, pair_gain), (pair_bias_hbm, pair_bias),
        (qk_hbm, qk), (qk_bias_hbm, qk_bias), (chain_hbm, chain), (bins_hbm, bins),
        (pair_weight_hbm, pair_weight), (relpos_hbm, relpos), (chain_table_hbm, chain_table),
    ]
    small = [
        pltpu.make_async_copy(source, target, sem_small.at[at])
        for at, (source, target) in enumerate(small)
    ]
    states = [
        pltpu.make_async_copy(
            hidden_hbm.at[pl.ds(low, size)], hidden.at[pl.ds(low, size)], sem_hidden.at[at]
        )
        for at, (low, size) in enumerate(state_pieces)
    ]
    firsts = [
        pltpu.make_async_copy(
            proj_in_hbm.at[pl.ds(low, size)], proj_in.at[pl.ds(low, size)], sem_in.at[at]
        )
        for at, (low, size) in enumerate(in_pieces)
    ]
    seconds = [
        pltpu.make_async_copy(
            proj_out_hbm.at[pl.ds(low, size)], proj_out.at[pl.ds(low, size)], sem_out.at[at]
        )
        for at, (low, size) in enumerate(out_pieces)
    ]
    small[0].start()
    for copy in states:
        copy.start()
    firsts[0].start()
    for copy in small[1:]:
        copy.start()
    later = firsts[1:] + seconds

    small[0].wait()
    width = mixture.shape[1]
    state_count = hidden.shape[0]
    shape = (tok_count, state_count * tok_count)
    lanes = lax.broadcasted_iota(jnp.int32, shape, 1)
    state_of = lanes // tok_count
    weights = jnp.zeros(shape, F32)
    for state in range(state_count):
        weights = jnp.where(state_of == state, mix[state], weights)
    own = lanes - state_of * tok_count == lax.broadcasted_iota(jnp.int32, shape, 0)
    weights = jnp.where(own, weights, 0.0)
    high = weights.astype(BF16)
    middle = (weights - high.astype(F32)).astype(BF16)
    low_part = (weights - high.astype(F32) - middle.astype(F32)).astype(BF16)
    weights = jnp.concatenate([high, middle, low_part], axis=0)

    mixed = None
    for at, (low, size) in enumerate(state_pieces):
        states[at].wait()
        last = at == len(state_pieces) - 1
        for copy in later if last else later[:2]:
            copy.start()
        later = later[2:]
        term = jnp.dot(
            weights[:, low * tok_count:(low + size) * tok_count],
            hidden[pl.ds(low, size)].reshape(size * tok_count, width),
            preferred_element_type=F32,
        )
        mixed = term if mixed is None else mixed + term
    mixture[...] = (
        mixed[0:tok_count] + (mixed[tok_count:2 * tok_count] + mixed[2 * tok_count:])
    )

    for copy in small[1:]:
        copy.wait()
    normed = row_norm(
        mixture[...], norm_gain[...].reshape(1, width), norm_bias[...].reshape(1, width)
    ).astype(BF16)
    bins_col = operand_rows(
        bins, pair_weight, relpos, chain_table, bin_rows, right, minus, tok_count
    )
    flags = chain_flags(chain, tok_count, inner_dim)
    bin_table = bin_rows[...].astype(BF16)
    lanes = lax.broadcasted_iota(jnp.int32, (bins_col.shape[0], bin_table.shape[0]), 1)
    row_pieces = pieces(tok_count, max(1, len(in_pieces) - 1))
    total = None
    for at, (low, size) in enumerate(in_pieces):
        firsts[at].wait()
        term = jnp.dot(
            normed[:, low:low + size], proj_in[pl.ds(low, size), :], preferred_element_type=F32
        )
        total = term if total is None else total + term
        if at < len(row_pieces):
            for row in range(row_pieces[at][0], sum(row_pieces[at])):
                onehot = jnp.where(bins_col[:, row:row + 1] == lanes, 1.0, 0.0).astype(BF16)
                first[row] = jnp.dot(onehot, bin_table, preferred_element_type=F32)
    for row in range(tok_count):
        residue_rows[pl.ds(row, 1), :] = residue[pl.ds(tokens[row], 1), :]
    middle = jnp.maximum(total + proj_in_bias[...], 0.0).astype(BF16)

    total = None
    for at, (low, size) in enumerate(out_pieces):
        seconds[at].wait()
        term = jnp.dot(
            middle[:, low:low + size], proj_out[pl.ds(low, size), :], preferred_element_type=F32
        )
        total = term if total is None else total + term
    single_f = total + proj_out_bias[...] + residue_rows[...]
    single[...] = single_f.astype(BF16)

    pair_in = row_norm(single_f, pair_gain[...], pair_bias[...]).astype(BF16)
    query_key = jnp.dot(pair_in, qk[...], preferred_element_type=F32) + qk_bias[...]

    front = lax.broadcasted_iota(jnp.int32, flags.shape, 1) < inner_dim
    query_ref[...] = jnp.where(front, query_key, flags).astype(BF16)
    block = jnp.where(front, pltpu.roll(query_key, inner_dim, 1), flags).astype(BF16)
    for peer in range(copies_ref.shape[0]):
        copies_ref[peer] = block


def single_part(device_count, operands):
    (hidden, mix, norm_gain, norm_bias, proj_in, proj_in_bias, proj_out, proj_out_bias, tokens,
     residue, pair_gain, pair_bias, qk, qk_bias, chain, bins, pair_weight, relpos,
     chain_table) = operands
    state_count, tok_count, width = hidden.shape
    channels = proj_out.shape[1]
    lanes = qk.shape[1]
    table_rows = -(-relpos.shape[0] // 128) * 128
    vmem = pl.BlockSpec(memory_space=pltpu.VMEM)
    states_step = max(1, 256 // tok_count)
    state_pieces = [
        (low, min(states_step, state_count - low)) for low in range(0, state_count, states_step)
    ]
    plan = (state_pieces, pieces(width, 5), pieces(channels, 2))
    args = (
        hidden, mix, norm_gain, norm_bias, proj_in, proj_in_bias[None],
        proj_out, proj_out_bias[None], tokens, residue, pair_gain[None], pair_bias[None],
        qk, qk_bias[None], chain[None], bins, pair_weight, relpos, chain_table,
    )
    args = [pltpu.with_memory_space_constraint(arg, pltpu.HBM) for arg in args]
    in_smem = (1, 8)
    scratch = [
        (pltpu.SMEM if at in in_smem else pltpu.VMEM)(arg.shape, arg.dtype)
        for at, arg in enumerate(args)
    ]
    scratch += [
        pltpu.VMEM((tok_count, width), F32),
        pltpu.VMEM((tok_count, channels), F32),
        pltpu.VMEM((table_rows, pair_weight.shape[1]), F32),
        pltpu.SemaphoreType.DMA((len(plan[0]),)),
        pltpu.SemaphoreType.DMA((len(plan[1]),)),
        pltpu.SemaphoreType.DMA((len(plan[2]),)),
        pltpu.SemaphoreType.DMA((16,)),
    ]
    moved = sum(arg.size * arg.dtype.itemsize for arg in args)
    return pl.pallas_call(
        functools.partial(single_kernel, plan),
        out_shape=(
            jax.ShapeDtypeStruct((tok_count, channels), BF16),
            jax.ShapeDtypeStruct((tok_count, lanes), BF16),
            jax.ShapeDtypeStruct((device_count, tok_count, lanes), BF16),
            jax.ShapeDtypeStruct(bins.shape + pair_weight.shape[1:], F32),
            jax.ShapeDtypeStruct(pair_weight.shape, BF16),
            jax.ShapeDtypeStruct(pair_weight.shape, BF16),
        ),
        in_specs=[pl.BlockSpec(memory_space=pltpu.HBM)] * len(args),
        out_specs=(vmem,) * 6,
        scratch_shapes=scratch,
        compiler_params=pltpu.CompilerParams(vmem_limit_bytes=32 * 2**20),
        cost_estimate=pl.CostEstimate(
            flops=2 * tok_count * channels * (width + channels + lanes),
            bytes_accessed=moved,
            transcendentals=0,
        ),
        name="single_path",
    )(*args)


def pair_kernel(
    blocks, queries, first, right, minus, single, single_hbm, pair_hbm, pair, sem, sem_single
):
    single_copy = pltpu.make_async_copy(single, single_hbm, sem_single)
    single_copy.start()
    keys = jnp.concatenate([blocks[1:].reshape(-1, blocks.shape[2]), blocks[0]], axis=0)
    row_diff = jnp.dot(queries[...], minus[...], preferred_element_type=F32)
    col_diff = jnp.dot(keys, minus[...], preferred_element_type=F32)
    copies = []
    for row in range(first.shape[0]):
        products = keys * queries[row:row + 1, :]
        value = jnp.dot(products, right[...], preferred_element_type=F32)
        value = value + first[row] + (row_diff[row:row + 1, :] - col_diff)
        pair[row] = value.astype(BF16)
        copy = pltpu.make_async_copy(pair.at[row], pair_hbm.at[row], sem.at[row])
        copy.start()
        copies.append(copy)
    for copy in copies:
        copy.wait()
    single_copy.wait()


def pair_part(blocks, queries, first, right, minus, single):
    tok_count = first.shape[0]
    vmem = pl.BlockSpec(memory_space=pltpu.VMEM)
    return pl.pallas_call(
        pair_kernel,
        out_shape=(
            jax.ShapeDtypeStruct(single.shape, BF16),
            jax.ShapeDtypeStruct(first.shape, BF16),
        ),
        in_specs=[vmem] * 6,
        out_specs=(pl.BlockSpec(memory_space=pltpu.HBM),) * 2,
        scratch_shapes=[
            pltpu.VMEM(first.shape, BF16),
            pltpu.SemaphoreType.DMA((tok_count,)),
            pltpu.SemaphoreType.DMA,
        ],
        compiler_params=pltpu.CompilerParams(vmem_limit_bytes=32 * 2**20),
        cost_estimate=pl.CostEstimate(
            flops=2 * first.size * right.shape[0],
            bytes_accessed=6 * first.size,
            transcendentals=0,
        ),
        name="pair_rows",
    )(blocks, queries, first, right, minus, single)


def shards(
    hidden_states,
    layer_mix,
    norm_gain,
    norm_bias,
    proj_in,
    proj_in_bias,
    proj_out,
    proj_out_bias,
    residue_tokens,
    residue_table,
    pair_norm_gain,
    pair_norm_bias,
    qk_weight,
    qk_bias,
    pair_weight,
    relpos_bins,
    relpos_table,
    chain_ids,
    chain_table,
):
    device_count = lax.axis_size("seq")
    single, queries, copies, first, right, minus = single_part(
        device_count,
        (
            hidden_states, layer_mix, norm_gain, norm_bias, proj_in, proj_in_bias, proj_out,
            proj_out_bias, residue_tokens, residue_table, pair_norm_gain, pair_norm_bias,
            qk_weight, qk_bias, chain_ids, relpos_bins, pair_weight, relpos_table, chain_table,
        ),
    )
    order = [device_count - 1] + list(range(device_count - 1))
    blocks = lax.all_to_all(
        copies, "seq", split_axis=0, concat_axis=0, axis_index_groups=[order]
    )
    return pair_part(blocks, queries, first, right, minus, single)


def solution(mesh):
    in_specs = (
        P(None, ("groups", "seq"), None),
        P(),
        P(),
        P(),
        P(),
        P(),
        P(),
        P(),
        P(("groups", "seq")),
        P(),
        P(),
        P(),
        P(),
        P(),
        P(),
        P(("groups", "seq"), None),
        P(),
        P(("groups", "seq")),
        P(),
    )
    out_specs = (P(("groups", "seq"), None), P(("groups", "seq"), None, None))
    return jax.shard_map(shards, mesh=mesh, in_specs=in_specs, out_specs=out_specs, check_vma=False)
```

```python
import functools

import jax
import jax.numpy as jnp
from jax import lax
from jax.experimental import pallas as pl
from jax.experimental.pallas import tpu as pltpu
from jax.sharding import PartitionSpec as P

epsilon = 1e-05
BF16 = jnp.bfloat16
F32 = jnp.float32


def pieces(total, count):
    count = max(1, min(count, total))
    ends = [total * step // count for step in range(count + 1)]
    return [(low, high - low) for low, high in zip(ends[:-1], ends[1:])]


def row_norm(values, gain, bias):
    center = values - jnp.mean(values, axis=-1, keepdims=True)
    spread = jnp.mean(center * center, axis=-1, keepdims=True)
    return center * lax.rsqrt(spread + epsilon) * gain + bias


def chain_flags(chain, tok_count, inner_dim):
    lanes = lax.broadcasted_iota(jnp.int32, (tok_count, 2 * inner_dim), 1)
    flag = lax.rem(lanes, inner_dim // 2).astype(F32)
    square = (tok_count, tok_count)
    own = lax.broadcasted_iota(jnp.int32, square, 0) == lax.broadcasted_iota(jnp.int32, square, 1)
    chain_col = jnp.sum(jnp.where(own, chain[...].astype(F32), 0.0), axis=1, keepdims=True)
    return jnp.where(flag == chain_col, 1.0, 0.0)


def operand_rows(bins, pair_weight, relpos, chain_table, bin_rows, right, minus, tok_count):
    bin_count = relpos.shape[0]
    inner_dim = pair_weight.shape[0] // 2
    flag_count = inner_dim // 2
    step = chain_table[1:2, :] - chain_table[0:1, :]
    step_high = step.astype(BF16).astype(F32)
    shape = (flag_count, step.shape[1])
    right[0:inner_dim, :] = pair_weight[0:inner_dim, :]
    right[inner_dim:inner_dim + flag_count, :] = jnp.broadcast_to(step_high, shape).astype(BF16)
    right[inner_dim + flag_count:, :] = jnp.broadcast_to(step - step_high, shape).astype(BF16)
    minus[0:inner_dim, :] = pair_weight[inner_dim:, :]
    minus[inner_dim:, :] = jnp.zeros((inner_dim, step.shape[1]), BF16)
    bin_rows[...] = jnp.zeros(bin_rows.shape, F32)
    bin_rows[0:bin_count, :] = relpos[...] + chain_table[0:1, :]
    padded = jnp.concatenate(
        [bins[...], jnp.zeros((128 - tok_count, bins.shape[1]), jnp.int32)], axis=0
    )
    return padded.T


def single_kernel(
    plan,
    hidden_hbm, mix_hbm, norm_gain_hbm, norm_bias_hbm, proj_in_hbm, proj_in_bias_hbm,
    proj_out_hbm, proj_out_bias_hbm, tokens_hbm, residue_hbm, pair_gain_hbm, pair_bias_hbm,
    qk_hbm, qk_bias_hbm, chain_hbm, bins_hbm, pair_weight_hbm, relpos_hbm, chain_table_hbm,
    single, query_ref, copies_ref, first, right, minus,
    hidden, mix, norm_gain, norm_bias, proj_in, proj_in_bias, proj_out, proj_out_bias, tokens,
    residue, pair_gain, pair_bias, qk, qk_bias, chain, bins, pair_weight, relpos, chain_table,
    mixture, residue_rows, bin_rows, sem_hidden, sem_in, sem_out, sem_small,
):
    in_pieces, out_pieces = plan
    tok_count = mixture.shape[0]
    inner_dim = qk.shape[1] // 2

    small = [
        (mix_hbm, mix), (tokens_hbm, tokens), (residue_hbm, residue),
        (norm_gain_hbm, norm_gain), (norm_bias_hbm, norm_bias),
        (proj_in_bias_hbm, proj_in_bias), (proj_out_bias_hbm, proj_out_bias),
        (pair_gain_hbm, pair_gain), (pair_bias_hbm, pair_bias),
        (qk_hbm, qk), (qk_bias_hbm, qk_bias), (chain_hbm, chain), (bins_hbm, bins),
        (pair_weight_hbm, pair_weight), (relpos_hbm, relpos), (chain_table_hbm, chain_table),
    ]
    small = [
        pltpu.make_async_copy(source, target, sem_small.at[at])
        for at, (source, target) in enumerate(small)
    ]
    states = [
        pltpu.make_async_copy(
            hidden_hbm.at[:, :, pl.ds(low, size)],
            hidden.at[:, :, pl.ds(low, size)],
            sem_hidden.at[at],
        )
        for at, (low, size) in enumerate(in_pieces)
    ]
    firsts = [
        pltpu.make_async_copy(
            proj_in_hbm.at[pl.ds(low, size)], proj_in.at[pl.ds(low, size)], sem_in.at[at]
        )
        for at, (low, size) in enumerate(in_pieces)
    ]
    seconds = [
        pltpu.make_async_copy(
            proj_out_hbm.at[pl.ds(low, size)], proj_out.at[pl.ds(low, size)], sem_out.at[at]
        )
        for at, (low, size) in enumerate(out_pieces)
    ]
    small[0].start()
    states[0].start()
    for copy in small[1:] + states[1:] + firsts[:1]:
        copy.start()
    later = firsts[1:] + seconds

    width = mixture.shape[1]
    small[0].wait()
    shift = sums = squares = None
    for at, (low, size) in enumerate(in_pieces):
        states[at].wait()
        for copy in later if at == len(in_pieces) - 1 else later[:1]:
            copy.start()
        later = later[1:]
        total = None
        for state in range(hidden.shape[0]):
            term = mix[state] * hidden[state, :, low:low + size].astype(F32)
            total = term if total is None else total + term
        mixture[:, low:low + size] = total
        if shift is None:
            shift = jnp.mean(total, axis=1, keepdims=True)
        total = total - shift
        for lane in range(0, size, 128):
            part = total[:, lane:lane + 128]
            sums = part if sums is None else sums + part
            squares = part * part if squares is None else squares + part * part
        if at == min(1, len(in_pieces) - 1):
            for copy in small[1:]:
                copy.wait()
            bins_col = operand_rows(
                bins, pair_weight, relpos, chain_table, bin_rows, right, minus, tok_count
            )
            flags = chain_flags(chain, tok_count, inner_dim)
            for row in range(tok_count):
                residue_rows[pl.ds(row, 1), :] = residue[pl.ds(tokens[row], 1), :]

    offset = jnp.sum(sums, axis=1, keepdims=True) / width
    spread = jnp.sum(squares, axis=1, keepdims=True) / width - offset * offset
    mean = shift + offset
    scale = lax.rsqrt(jnp.maximum(spread, 0.0) + epsilon)
    gain, bias = norm_gain[...].reshape(1, width), norm_bias[...].reshape(1, width)
    bin_table = bin_rows[...].astype(BF16)
    lanes = lax.broadcasted_iota(jnp.int32, (bins_col.shape[0], bin_table.shape[0]), 1)
    row_pieces = pieces(tok_count, max(1, len(in_pieces) - 1))
    total = None
    for at, (low, size) in enumerate(in_pieces):
        span = slice(low, low + size)
        normed = ((mixture[:, span] - mean) * scale * gain[:, span] + bias[:, span]).astype(BF16)
        firsts[at].wait()
        term = jnp.dot(normed, proj_in[pl.ds(low, size), :], preferred_element_type=F32)
        total = term if total is None else total + term
        if at < len(row_pieces):
            for row in range(row_pieces[at][0], sum(row_pieces[at])):
                onehot = jnp.where(bins_col[:, row:row + 1] == lanes, 1.0, 0.0).astype(BF16)
                first[row] = jnp.dot(onehot, bin_table, preferred_element_type=F32)
    middle = jnp.maximum(total + proj_in_bias[...], 0.0).astype(BF16)

    total = None
    for at, (low, size) in enumerate(out_pieces):
        seconds[at].wait()
        term = jnp.dot(
            middle[:, low:low + size], proj_out[pl.ds(low, size), :], preferred_element_type=F32
        )
        total = term if total is None else total + term
    single_f = total + proj_out_bias[...] + residue_rows[...]
    single[...] = single_f.astype(BF16)

    pair_in = row_norm(single_f, pair_gain[...], pair_bias[...]).astype(BF16)
    query_key = jnp.dot(pair_in, qk[...], preferred_element_type=F32) + qk_bias[...]

    front = lax.broadcasted_iota(jnp.int32, flags.shape, 1) < inner_dim
    query_ref[...] = jnp.where(front, query_key, flags).astype(BF16)
    block = jnp.where(front, pltpu.roll(query_key, inner_dim, 1), flags).astype(BF16)
    for peer in range(copies_ref.shape[0]):
        copies_ref[peer] = block


def single_part(device_count, operands):
    (hidden, mix, norm_gain, norm_bias, proj_in, proj_in_bias, proj_out, proj_out_bias, tokens,
     residue, pair_gain, pair_bias, qk, qk_bias, chain, bins, pair_weight, relpos,
     chain_table) = operands
    tok_count, width = hidden.shape[1:]
    channels = proj_out.shape[1]
    lanes = qk.shape[1]
    table_rows = -(-relpos.shape[0] // 128) * 128
    vmem = pl.BlockSpec(memory_space=pltpu.VMEM)
    plan = (pieces(width, 5), pieces(channels, 2))
    args = (
        hidden, mix, norm_gain, norm_bias, proj_in, proj_in_bias[None],
        proj_out, proj_out_bias[None], tokens, residue, pair_gain[None], pair_bias[None],
        qk, qk_bias[None], chain[None], bins, pair_weight, relpos, chain_table,
    )
    args = [pltpu.with_memory_space_constraint(arg, pltpu.HBM) for arg in args]
    in_smem = (1, 8)
    scratch = [
        (pltpu.SMEM if at in in_smem else pltpu.VMEM)(arg.shape, arg.dtype)
        for at, arg in enumerate(args)
    ]
    scratch += [
        pltpu.VMEM((tok_count, width), F32),
        pltpu.VMEM((tok_count, channels), F32),
        pltpu.VMEM((table_rows, pair_weight.shape[1]), F32),
        pltpu.SemaphoreType.DMA((len(plan[0]),)),
        pltpu.SemaphoreType.DMA((len(plan[0]),)),
        pltpu.SemaphoreType.DMA((len(plan[1]),)),
        pltpu.SemaphoreType.DMA((16,)),
    ]
    moved = sum(arg.size * arg.dtype.itemsize for arg in args)
    return pl.pallas_call(
        functools.partial(single_kernel, plan),
        out_shape=(
            jax.ShapeDtypeStruct((tok_count, channels), BF16),
            jax.ShapeDtypeStruct((tok_count, lanes), BF16),
            jax.ShapeDtypeStruct((device_count, tok_count, lanes), BF16),
            jax.ShapeDtypeStruct(bins.shape + pair_weight.shape[1:], F32),
            jax.ShapeDtypeStruct(pair_weight.shape, BF16),
            jax.ShapeDtypeStruct(pair_weight.shape, BF16),
        ),
        in_specs=[pl.BlockSpec(memory_space=pltpu.HBM)] * len(args),
        out_specs=(vmem,) * 6,
        scratch_shapes=scratch,
        compiler_params=pltpu.CompilerParams(vmem_limit_bytes=32 * 2**20),
        cost_estimate=pl.CostEstimate(
            flops=2 * tok_count * channels * (width + channels + lanes),
            bytes_accessed=moved,
            transcendentals=0,
        ),
        name="single_path",
    )(*args)


def pair_kernel(
    blocks, queries, first, right, minus, single, single_hbm, pair_hbm, pair, sem, sem_single
):
    single_copy = pltpu.make_async_copy(single, single_hbm, sem_single)
    single_copy.start()
    keys = jnp.concatenate([blocks[1:].reshape(-1, blocks.shape[2]), blocks[0]], axis=0)
    row_diff = jnp.dot(queries[...], minus[...], preferred_element_type=F32)
    col_diff = jnp.dot(keys, minus[...], preferred_element_type=F32)
    copies = []
    for row in range(first.shape[0]):
        products = keys * queries[row:row + 1, :]
        value = jnp.dot(products, right[...], preferred_element_type=F32)
        value = value + first[row] + (row_diff[row:row + 1, :] - col_diff)
        pair[row] = value.astype(BF16)
        copy = pltpu.make_async_copy(pair.at[row], pair_hbm.at[row], sem.at[row])
        copy.start()
        copies.append(copy)
    for copy in copies:
        copy.wait()
    single_copy.wait()


def pair_part(blocks, queries, first, right, minus, single):
    tok_count = first.shape[0]
    vmem = pl.BlockSpec(memory_space=pltpu.VMEM)
    return pl.pallas_call(
        pair_kernel,
        out_shape=(
            jax.ShapeDtypeStruct(single.shape, BF16),
            jax.ShapeDtypeStruct(first.shape, BF16),
        ),
        in_specs=[vmem] * 6,
        out_specs=(pl.BlockSpec(memory_space=pltpu.HBM),) * 2,
        scratch_shapes=[
            pltpu.VMEM(first.shape, BF16),
            pltpu.SemaphoreType.DMA((tok_count,)),
            pltpu.SemaphoreType.DMA,
        ],
        compiler_params=pltpu.CompilerParams(vmem_limit_bytes=32 * 2**20),
        cost_estimate=pl.CostEstimate(
            flops=2 * first.size * right.shape[0],
            bytes_accessed=6 * first.size,
            transcendentals=0,
        ),
        name="pair_rows",
    )(blocks, queries, first, right, minus, single)


def shards(
    hidden_states,
    layer_mix,
    norm_gain,
    norm_bias,
    proj_in,
    proj_in_bias,
    proj_out,
    proj_out_bias,
    residue_tokens,
    residue_table,
    pair_norm_gain,
    pair_norm_bias,
    qk_weight,
    qk_bias,
    pair_weight,
    relpos_bins,
    relpos_table,
    chain_ids,
    chain_table,
):
    device_count = lax.axis_size("seq")
    single, queries, copies, first, right, minus = single_part(
        device_count,
        (
            hidden_states, layer_mix, norm_gain, norm_bias, proj_in, proj_in_bias, proj_out,
            proj_out_bias, residue_tokens, residue_table, pair_norm_gain, pair_norm_bias,
            qk_weight, qk_bias, chain_ids, relpos_bins, pair_weight, relpos_table, chain_table,
        ),
    )
    order = [device_count - 1] + list(range(device_count - 1))
    blocks = lax.all_to_all(
        copies, "seq", split_axis=0, concat_axis=0, axis_index_groups=[order]
    )
    return pair_part(blocks, queries, first, right, minus, single)


def solution(mesh):
    in_specs = (
        P(None, ("groups", "seq"), None),
        P(),
        P(),
        P(),
        P(),
        P(),
        P(),
        P(),
        P(("groups", "seq")),
        P(),
        P(),
        P(),
        P(),
        P(),
        P(),
        P(("groups", "seq"), None),
        P(),
        P(("groups", "seq")),
        P(),
    )
    out_specs = (P(("groups", "seq"), None), P(("groups", "seq"), None, None))
    return jax.shard_map(shards, mesh=mesh, in_specs=in_specs, out_specs=out_specs, check_vma=False)
```

```python
import functools

import jax
import jax.numpy as jnp
from jax import lax
from jax.experimental import pallas as pl
from jax.experimental.pallas import tpu as pltpu
from jax.sharding import PartitionSpec as P

epsilon = 1e-05
BF16 = jnp.bfloat16
F32 = jnp.float32


def pieces(total, count):
    count = max(1, min(count, total))
    ends = [total * step // count for step in range(count + 1)]
    return [(low, high - low) for low, high in zip(ends[:-1], ends[1:])]


def row_norm(values, gain, bias):
    center = values - jnp.mean(values, axis=-1, keepdims=True)
    spread = jnp.mean(center * center, axis=-1, keepdims=True)
    return center * lax.rsqrt(spread + epsilon) * gain + bias


def chain_flags(chain, tok_count, inner_dim):
    lanes = lax.broadcasted_iota(jnp.int32, (tok_count, 2 * inner_dim), 1)
    flag = lax.rem(lanes, inner_dim // 2).astype(F32)
    square = (tok_count, tok_count)
    own = lax.broadcasted_iota(jnp.int32, square, 0) == lax.broadcasted_iota(jnp.int32, square, 1)
    chain_col = jnp.sum(jnp.where(own, chain[...].astype(F32), 0.0), axis=1, keepdims=True)
    return jnp.where(flag == chain_col, 1.0, 0.0)


def operand_rows(bins, pair_weight, relpos, chain_table, bin_rows, right, minus, tok_count):
    bin_count = relpos.shape[0]
    inner_dim = pair_weight.shape[0] // 2
    flag_count = inner_dim // 2
    step = chain_table[1:2, :] - chain_table[0:1, :]
    step_high = step.astype(BF16).astype(F32)
    shape = (flag_count, step.shape[1])
    right[0:inner_dim, :] = pair_weight[0:inner_dim, :]
    right[inner_dim:inner_dim + flag_count, :] = jnp.broadcast_to(step_high, shape).astype(BF16)
    right[inner_dim + flag_count:, :] = jnp.broadcast_to(step - step_high, shape).astype(BF16)
    minus[0:inner_dim, :] = pair_weight[inner_dim:, :]
    minus[inner_dim:, :] = jnp.zeros((inner_dim, step.shape[1]), BF16)
    bin_rows[...] = jnp.zeros(bin_rows.shape, F32)
    bin_rows[0:bin_count, :] = relpos[...] + chain_table[0:1, :]
    padded = jnp.concatenate(
        [bins[...], jnp.zeros((128 - tok_count, bins.shape[1]), jnp.int32)], axis=0
    )
    return padded.T


def single_kernel(
    plan,
    hidden_hbm, mix_hbm, norm_gain_hbm, norm_bias_hbm, proj_in_hbm, proj_in_bias_hbm,
    proj_out_hbm, proj_out_bias_hbm, tokens_hbm, residue_hbm, pair_gain_hbm, pair_bias_hbm,
    qk_hbm, qk_bias_hbm, chain_hbm, bins_hbm, pair_weight_hbm, relpos_hbm, chain_table_hbm,
    single, query_ref, copies_ref, first, right, minus,
    hidden, mix, norm_gain, norm_bias, proj_in, proj_in_bias, proj_out, proj_out_bias, tokens,
    residue, pair_gain, pair_bias, qk, qk_bias, chain, bins, pair_weight, relpos, chain_table,
    mixture, residue_rows, bin_rows, sem_hidden, sem_in, sem_out, sem_small,
):
    in_pieces, out_pieces = plan
    tok_count = mixture.shape[0]
    inner_dim = qk.shape[1] // 2

    small = [
        (mix_hbm, mix), (tokens_hbm, tokens), (residue_hbm, residue),
        (norm_gain_hbm, norm_gain), (norm_bias_hbm, norm_bias),
        (proj_in_bias_hbm, proj_in_bias), (proj_out_bias_hbm, proj_out_bias),
        (pair_gain_hbm, pair_gain), (pair_bias_hbm, pair_bias),
        (qk_hbm, qk), (qk_bias_hbm, qk_bias), (chain_hbm, chain), (bins_hbm, bins),
        (pair_weight_hbm, pair_weight), (relpos_hbm, relpos), (chain_table_hbm, chain_table),
    ]
    small = [
        pltpu.make_async_copy(source, target, sem_small.at[at])
        for at, (source, target) in enumerate(small)
    ]
    states = [
        pltpu.make_async_copy(
            hidden_hbm.at[:, :, pl.ds(low, size)],
            hidden.at[:, :, pl.ds(low, size)],
            sem_hidden.at[at],
        )
        for at, (low, size) in enumerate(in_pieces)
    ]
    firsts = [
        pltpu.make_async_copy(
            proj_in_hbm.at[pl.ds(low, size)], proj_in.at[pl.ds(low, size)], sem_in.at[at]
        )
        for at, (low, size) in enumerate(in_pieces)
    ]
    seconds = [
        pltpu.make_async_copy(
            proj_out_hbm.at[pl.ds(low, size)], proj_out.at[pl.ds(low, size)], sem_out.at[at]
        )
        for at, (low, size) in enumerate(out_pieces)
    ]
    small[0].start()
    states[0].start()
    for copy in small[1:] + states[1:] + firsts + seconds:
        copy.start()

    width = mixture.shape[1]
    small[0].wait()
    shift = sums = squares = None
    for at, (low, size) in enumerate(in_pieces):
        states[at].wait()
        total = None
        for state in range(hidden.shape[0]):
            term = mix[state] * hidden[state, :, low:low + size].astype(F32)
            total = term if total is None else total + term
        mixture[:, low:low + size] = total
        if shift is None:
            shift = jnp.mean(total, axis=1, keepdims=True)
        total = total - shift
        for lane in range(0, size, 128):
            part = total[:, lane:lane + 128]
            sums = part if sums is None else sums + part
            squares = part * part if squares is None else squares + part * part
        if at == min(1, len(in_pieces) - 1):
            for copy in small[1:]:
                copy.wait()
            bins_col = operand_rows(
                bins, pair_weight, relpos, chain_table, bin_rows, right, minus, tok_count
            )
            flags = chain_flags(chain, tok_count, inner_dim)
            for row in range(tok_count):
                residue_rows[pl.ds(row, 1), :] = residue[pl.ds(tokens[row], 1), :]

    offset = jnp.sum(sums, axis=1, keepdims=True) / width
    spread = jnp.sum(squares, axis=1, keepdims=True) / width - offset * offset
    mean = shift + offset
    scale = lax.rsqrt(jnp.maximum(spread, 0.0) + epsilon)
    gain, bias = norm_gain[...].reshape(1, width), norm_bias[...].reshape(1, width)
    bin_table = bin_rows[...].astype(BF16)
    lanes = lax.broadcasted_iota(jnp.int32, (bins_col.shape[0], bin_table.shape[0]), 1)
    row_pieces = pieces(tok_count, max(1, len(in_pieces) - 1))
    total = None
    for at, (low, size) in enumerate(in_pieces):
        span = slice(low, low + size)
        normed = ((mixture[:, span] - mean) * scale * gain[:, span] + bias[:, span]).astype(BF16)
        firsts[at].wait()
        term = jnp.dot(normed, proj_in[pl.ds(low, size), :], preferred_element_type=F32)
        total = term if total is None else total + term
        if at < len(row_pieces):
            for row in range(row_pieces[at][0], sum(row_pieces[at])):
                onehot = jnp.where(bins_col[:, row:row + 1] == lanes, 1.0, 0.0).astype(BF16)
                first[row] = jnp.dot(onehot, bin_table, preferred_element_type=F32)
    middle = jnp.maximum(total + proj_in_bias[...], 0.0).astype(BF16)

    total = None
    for at, (low, size) in enumerate(out_pieces):
        seconds[at].wait()
        term = jnp.dot(
            middle[:, low:low + size], proj_out[pl.ds(low, size), :], preferred_element_type=F32
        )
        total = term if total is None else total + term
    single_f = total + proj_out_bias[...] + residue_rows[...]
    single[...] = single_f.astype(BF16)

    pair_in = row_norm(single_f, pair_gain[...], pair_bias[...]).astype(BF16)
    query_key = jnp.dot(pair_in, qk[...], preferred_element_type=F32) + qk_bias[...]

    front = lax.broadcasted_iota(jnp.int32, flags.shape, 1) < inner_dim
    query_ref[...] = jnp.where(front, query_key, flags).astype(BF16)
    block = jnp.where(front, pltpu.roll(query_key, inner_dim, 1), flags).astype(BF16)
    for peer in range(copies_ref.shape[0]):
        copies_ref[peer] = block


def single_part(device_count, operands):
    (hidden, mix, norm_gain, norm_bias, proj_in, proj_in_bias, proj_out, proj_out_bias, tokens,
     residue, pair_gain, pair_bias, qk, qk_bias, chain, bins, pair_weight, relpos,
     chain_table) = operands
    tok_count, width = hidden.shape[1:]
    channels = proj_out.shape[1]
    lanes = qk.shape[1]
    table_rows = -(-relpos.shape[0] // 128) * 128
    vmem = pl.BlockSpec(memory_space=pltpu.VMEM)
    plan = (pieces(width, 5), pieces(channels, 2))
    args = (
        hidden, mix, norm_gain, norm_bias, proj_in, proj_in_bias[None],
        proj_out, proj_out_bias[None], tokens, residue, pair_gain[None], pair_bias[None],
        qk, qk_bias[None], chain[None], bins, pair_weight, relpos, chain_table,
    )
    args = [pltpu.with_memory_space_constraint(arg, pltpu.HBM) for arg in args]
    in_smem = (1, 8)
    scratch = [
        (pltpu.SMEM if at in in_smem else pltpu.VMEM)(arg.shape, arg.dtype)
        for at, arg in enumerate(args)
    ]
    scratch += [
        pltpu.VMEM((tok_count, width), F32),
        pltpu.VMEM((tok_count, channels), F32),
        pltpu.VMEM((table_rows, pair_weight.shape[1]), F32),
        pltpu.SemaphoreType.DMA((len(plan[0]),)),
        pltpu.SemaphoreType.DMA((len(plan[0]),)),
        pltpu.SemaphoreType.DMA((len(plan[1]),)),
        pltpu.SemaphoreType.DMA((16,)),
    ]
    moved = sum(arg.size * arg.dtype.itemsize for arg in args)
    return pl.pallas_call(
        functools.partial(single_kernel, plan),
        out_shape=(
            jax.ShapeDtypeStruct((tok_count, channels), BF16),
            jax.ShapeDtypeStruct((tok_count, lanes), BF16),
            jax.ShapeDtypeStruct((device_count, tok_count, lanes), BF16),
            jax.ShapeDtypeStruct(bins.shape + pair_weight.shape[1:], F32),
            jax.ShapeDtypeStruct(pair_weight.shape, BF16),
            jax.ShapeDtypeStruct(pair_weight.shape, BF16),
        ),
        in_specs=[pl.BlockSpec(memory_space=pltpu.HBM)] * len(args),
        out_specs=(vmem,) * 6,
        scratch_shapes=scratch,
        compiler_params=pltpu.CompilerParams(vmem_limit_bytes=32 * 2**20),
        cost_estimate=pl.CostEstimate(
            flops=2 * tok_count * channels * (width + channels + lanes),
            bytes_accessed=moved,
            transcendentals=0,
        ),
        name="single_path",
    )(*args)


def pair_kernel(
    blocks, queries, first, right, minus, single, single_hbm, pair_hbm, pair, sem, sem_single
):
    single_copy = pltpu.make_async_copy(single, single_hbm, sem_single)
    single_copy.start()
    keys = jnp.concatenate([blocks[1:].reshape(-1, blocks.shape[2]), blocks[0]], axis=0)
    row_diff = jnp.dot(queries[...], minus[...], preferred_element_type=F32)
    col_diff = jnp.dot(keys, minus[...], preferred_element_type=F32)
    copies = []
    for row in range(first.shape[0]):
        products = keys * queries[row:row + 1, :]
        value = jnp.dot(products, right[...], preferred_element_type=F32)
        value = value + first[row] + (row_diff[row:row + 1, :] - col_diff)
        pair[row] = value.astype(BF16)
        copy = pltpu.make_async_copy(pair.at[row], pair_hbm.at[row], sem.at[row])
        copy.start()
        copies.append(copy)
    for copy in copies:
        copy.wait()
    single_copy.wait()


def pair_part(blocks, queries, first, right, minus, single):
    tok_count = first.shape[0]
    vmem = pl.BlockSpec(memory_space=pltpu.VMEM)
    return pl.pallas_call(
        pair_kernel,
        out_shape=(
            jax.ShapeDtypeStruct(single.shape, BF16),
            jax.ShapeDtypeStruct(first.shape, BF16),
        ),
        in_specs=[vmem] * 6,
        out_specs=(pl.BlockSpec(memory_space=pltpu.HBM),) * 2,
        scratch_shapes=[
            pltpu.VMEM(first.shape, BF16),
            pltpu.SemaphoreType.DMA((tok_count,)),
            pltpu.SemaphoreType.DMA,
        ],
        compiler_params=pltpu.CompilerParams(vmem_limit_bytes=32 * 2**20),
        cost_estimate=pl.CostEstimate(
            flops=2 * first.size * right.shape[0],
            bytes_accessed=6 * first.size,
            transcendentals=0,
        ),
        name="pair_rows",
    )(blocks, queries, first, right, minus, single)


def shards(
    hidden_states,
    layer_mix,
    norm_gain,
    norm_bias,
    proj_in,
    proj_in_bias,
    proj_out,
    proj_out_bias,
    residue_tokens,
    residue_table,
    pair_norm_gain,
    pair_norm_bias,
    qk_weight,
    qk_bias,
    pair_weight,
    relpos_bins,
    relpos_table,
    chain_ids,
    chain_table,
):
    device_count = lax.axis_size("seq")
    single, queries, copies, first, right, minus = single_part(
        device_count,
        (
            hidden_states, layer_mix, norm_gain, norm_bias, proj_in, proj_in_bias, proj_out,
            proj_out_bias, residue_tokens, residue_table, pair_norm_gain, pair_norm_bias,
            qk_weight, qk_bias, chain_ids, relpos_bins, pair_weight, relpos_table, chain_table,
        ),
    )
    order = [device_count - 1] + list(range(device_count - 1))
    blocks = lax.all_to_all(
        copies, "seq", split_axis=0, concat_axis=0, axis_index_groups=[order]
    )
    return pair_part(blocks, queries, first, right, minus, single)


def solution(mesh):
    in_specs = (
        P(None, ("groups", "seq"), None),
        P(),
        P(),
        P(),
        P(),
        P(),
        P(),
        P(),
        P(("groups", "seq")),
        P(),
        P(),
        P(),
        P(),
        P(),
        P(),
        P(("groups", "seq"), None),
        P(),
        P(("groups", "seq")),
        P(),
    )
    out_specs = (P(("groups", "seq"), None), P(("groups", "seq"), None, None))
    return jax.shard_map(shards, mesh=mesh, in_specs=in_specs, out_specs=out_specs, check_vma=False)
```

```python
import functools

import jax
import jax.numpy as jnp
from jax import lax
from jax.experimental import pallas as pl
from jax.experimental.pallas import tpu as pltpu
from jax.sharding import PartitionSpec as P

epsilon = 1e-05
BF16 = jnp.bfloat16
F32 = jnp.float32


def pieces(total, count):
    count = max(1, min(count, total))
    ends = [total * step // count for step in range(count + 1)]
    return [(low, high - low) for low, high in zip(ends[:-1], ends[1:])]


def row_norm(values, gain, bias):
    center = values - jnp.mean(values, axis=-1, keepdims=True)
    spread = jnp.mean(center * center, axis=-1, keepdims=True)
    return center * lax.rsqrt(spread + epsilon) * gain + bias


def chain_flags(chain, tok_count, inner_dim):
    lanes = lax.broadcasted_iota(jnp.int32, (tok_count, 2 * inner_dim), 1)
    flag = lax.rem(lanes, inner_dim // 2).astype(F32)
    square = (tok_count, tok_count)
    own = lax.broadcasted_iota(jnp.int32, square, 0) == lax.broadcasted_iota(jnp.int32, square, 1)
    chain_col = jnp.sum(jnp.where(own, chain[...].astype(F32), 0.0), axis=1, keepdims=True)
    return jnp.where(flag == chain_col, 1.0, 0.0)


def operand_rows(bins, pair_weight, relpos, chain_table, bin_rows, right, minus, tok_count):
    bin_count = relpos.shape[0]
    inner_dim = pair_weight.shape[0] // 2
    flag_count = inner_dim // 2
    step = chain_table[1:2, :] - chain_table[0:1, :]
    step_high = step.astype(BF16).astype(F32)
    shape = (flag_count, step.shape[1])
    right[0:inner_dim, :] = pair_weight[0:inner_dim, :]
    right[inner_dim:inner_dim + flag_count, :] = jnp.broadcast_to(step_high, shape).astype(BF16)
    right[inner_dim + flag_count:, :] = jnp.broadcast_to(step - step_high, shape).astype(BF16)
    minus[0:inner_dim, :] = pair_weight[inner_dim:, :]
    minus[inner_dim:, :] = jnp.zeros((inner_dim, step.shape[1]), BF16)
    bin_rows[...] = jnp.zeros(bin_rows.shape, F32)
    bin_rows[0:bin_count, :] = relpos[...] + chain_table[0:1, :]
    padded = jnp.concatenate(
        [bins[...], jnp.zeros((128 - tok_count, bins.shape[1]), jnp.int32)], axis=0
    )
    return padded.T


def single_kernel(
    plan,
    hidden_hbm, mix_hbm, norm_gain_hbm, norm_bias_hbm, proj_in_hbm, proj_in_bias_hbm,
    proj_out_hbm, proj_out_bias_hbm, tokens_hbm, residue_hbm, pair_gain_hbm, pair_bias_hbm,
    qk_hbm, qk_bias_hbm, chain_hbm, bins_hbm, pair_weight_hbm, relpos_hbm, chain_table_hbm,
    single, query_ref, copies_ref, first, right, minus,
    hidden, mix, norm_gain, norm_bias, proj_in, proj_in_bias, proj_out, proj_out_bias, tokens,
    residue, pair_gain, pair_bias, qk, qk_bias, chain, bins, pair_weight, relpos, chain_table,
    mixture, residue_rows, bin_rows, sem_hidden, sem_in, sem_out, sem_small,
):
    in_pieces, out_pieces = plan
    tok_count = mixture.shape[0]
    inner_dim = qk.shape[1] // 2

    small = [
        (mix_hbm, mix), (tokens_hbm, tokens), (residue_hbm, residue),
        (norm_gain_hbm, norm_gain), (norm_bias_hbm, norm_bias),
        (proj_in_bias_hbm, proj_in_bias), (proj_out_bias_hbm, proj_out_bias),
        (pair_gain_hbm, pair_gain), (pair_bias_hbm, pair_bias),
        (qk_hbm, qk), (qk_bias_hbm, qk_bias), (chain_hbm, chain), (bins_hbm, bins),
        (pair_weight_hbm, pair_weight), (relpos_hbm, relpos), (chain_table_hbm, chain_table),
    ]
    small = [
        pltpu.make_async_copy(source, target, sem_small.at[at])
        for at, (source, target) in enumerate(small)
    ]
    states = [
        pltpu.make_async_copy(
            hidden_hbm.at[:, :, pl.ds(low, size)],
            hidden.at[:, :, pl.ds(low, size)],
            sem_hidden.at[at],
        )
        for at, (low, size) in enumerate(in_pieces)
    ]
    firsts = [
        pltpu.make_async_copy(
            proj_in_hbm.at[pl.ds(low, size)], proj_in.at[pl.ds(low, size)], sem_in.at[at]
        )
        for at, (low, size) in enumerate(in_pieces)
    ]
    seconds = [
        pltpu.make_async_copy(
            proj_out_hbm.at[pl.ds(low, size)], proj_out.at[pl.ds(low, size)], sem_out.at[at]
        )
        for at, (low, size) in enumerate(out_pieces)
    ]
    small[0].start(priority=1)
    states[0].start(priority=1)
    for copy in small[1:] + states[1:]:
        copy.start(priority=1)
    for copy in firsts + seconds:
        copy.start()

    width = mixture.shape[1]
    small[0].wait()
    shift = sums = squares = None
    for at, (low, size) in enumerate(in_pieces):
        states[at].wait()
        total = None
        for state in range(hidden.shape[0]):
            term = mix[state] * hidden[state, :, low:low + size].astype(F32)
            total = term if total is None else total + term
        mixture[:, low:low + size] = total
        if shift is None:
            shift = jnp.mean(total, axis=1, keepdims=True)
        total = total - shift
        for lane in range(0, size, 128):
            part = total[:, lane:lane + 128]
            sums = part if sums is None else sums + part
            squares = part * part if squares is None else squares + part * part
        if at == min(1, len(in_pieces) - 1):
            for copy in small[1:]:
                copy.wait()
            bins_col = operand_rows(
                bins, pair_weight, relpos, chain_table, bin_rows, right, minus, tok_count
            )
            flags = chain_flags(chain, tok_count, inner_dim)
            for row in range(tok_count):
                residue_rows[pl.ds(row, 1), :] = residue[pl.ds(tokens[row], 1), :]

    offset = jnp.sum(sums, axis=1, keepdims=True) / width
    spread = jnp.sum(squares, axis=1, keepdims=True) / width - offset * offset
    mean = shift + offset
    scale = lax.rsqrt(jnp.maximum(spread, 0.0) + epsilon)
    gain, bias = norm_gain[...].reshape(1, width), norm_bias[...].reshape(1, width)
    bin_table = bin_rows[...].astype(BF16)
    lanes = lax.broadcasted_iota(jnp.int32, (bins_col.shape[0], bin_table.shape[0]), 1)
    row_pieces = pieces(tok_count, max(1, len(in_pieces) - 1))
    total = None
    for at, (low, size) in enumerate(in_pieces):
        span = slice(low, low + size)
        normed = ((mixture[:, span] - mean) * scale * gain[:, span] + bias[:, span]).astype(BF16)
        firsts[at].wait()
        term = jnp.dot(normed, proj_in[pl.ds(low, size), :], preferred_element_type=F32)
        total = term if total is None else total + term
        if at < len(row_pieces):
            for row in range(row_pieces[at][0], sum(row_pieces[at])):
                onehot = jnp.where(bins_col[:, row:row + 1] == lanes, 1.0, 0.0).astype(BF16)
                first[row] = jnp.dot(onehot, bin_table, preferred_element_type=F32)
    middle = jnp.maximum(total + proj_in_bias[...], 0.0).astype(BF16)

    total = None
    for at, (low, size) in enumerate(out_pieces):
        seconds[at].wait()
        term = jnp.dot(
            middle[:, low:low + size], proj_out[pl.ds(low, size), :], preferred_element_type=F32
        )
        total = term if total is None else total + term
    single_f = total + proj_out_bias[...] + residue_rows[...]
    single[...] = single_f.astype(BF16)

    pair_in = row_norm(single_f, pair_gain[...], pair_bias[...]).astype(BF16)
    query_key = jnp.dot(pair_in, qk[...], preferred_element_type=F32) + qk_bias[...]

    front = lax.broadcasted_iota(jnp.int32, flags.shape, 1) < inner_dim
    query_ref[...] = jnp.where(front, query_key, flags).astype(BF16)
    block = jnp.where(front, pltpu.roll(query_key, inner_dim, 1), flags).astype(BF16)
    for peer in range(copies_ref.shape[0]):
        copies_ref[peer] = block


def single_part(device_count, operands):
    (hidden, mix, norm_gain, norm_bias, proj_in, proj_in_bias, proj_out, proj_out_bias, tokens,
     residue, pair_gain, pair_bias, qk, qk_bias, chain, bins, pair_weight, relpos,
     chain_table) = operands
    tok_count, width = hidden.shape[1:]
    channels = proj_out.shape[1]
    lanes = qk.shape[1]
    table_rows = -(-relpos.shape[0] // 128) * 128
    vmem = pl.BlockSpec(memory_space=pltpu.VMEM)
    plan = (pieces(width, 5), pieces(channels, 2))
    args = (
        hidden, mix, norm_gain, norm_bias, proj_in, proj_in_bias[None],
        proj_out, proj_out_bias[None], tokens, residue, pair_gain[None], pair_bias[None],
        qk, qk_bias[None], chain[None], bins, pair_weight, relpos, chain_table,
    )
    args = [pltpu.with_memory_space_constraint(arg, pltpu.HBM) for arg in args]
    in_smem = (1, 8)
    scratch = [
        (pltpu.SMEM if at in in_smem else pltpu.VMEM)(arg.shape, arg.dtype)
        for at, arg in enumerate(args)
    ]
    scratch += [
        pltpu.VMEM((tok_count, width), F32),
        pltpu.VMEM((tok_count, channels), F32),
        pltpu.VMEM((table_rows, pair_weight.shape[1]), F32),
        pltpu.SemaphoreType.DMA((len(plan[0]),)),
        pltpu.SemaphoreType.DMA((len(plan[0]),)),
        pltpu.SemaphoreType.DMA((len(plan[1]),)),
        pltpu.SemaphoreType.DMA((16,)),
    ]
    moved = sum(arg.size * arg.dtype.itemsize for arg in args)
    return pl.pallas_call(
        functools.partial(single_kernel, plan),
        out_shape=(
            jax.ShapeDtypeStruct((tok_count, channels), BF16),
            jax.ShapeDtypeStruct((tok_count, lanes), BF16),
            jax.ShapeDtypeStruct((device_count, tok_count, lanes), BF16),
            jax.ShapeDtypeStruct(bins.shape + pair_weight.shape[1:], F32),
            jax.ShapeDtypeStruct(pair_weight.shape, BF16),
            jax.ShapeDtypeStruct(pair_weight.shape, BF16),
        ),
        in_specs=[pl.BlockSpec(memory_space=pltpu.HBM)] * len(args),
        out_specs=(vmem,) * 6,
        scratch_shapes=scratch,
        compiler_params=pltpu.CompilerParams(vmem_limit_bytes=32 * 2**20),
        cost_estimate=pl.CostEstimate(
            flops=2 * tok_count * channels * (width + channels + lanes),
            bytes_accessed=moved,
            transcendentals=0,
        ),
        name="single_path",
    )(*args)


def pair_kernel(
    blocks, queries, first, right, minus, single, single_hbm, pair_hbm, pair, sem, sem_single
):
    single_copy = pltpu.make_async_copy(single, single_hbm, sem_single)
    single_copy.start()
    keys = jnp.concatenate([blocks[1:].reshape(-1, blocks.shape[2]), blocks[0]], axis=0)
    row_diff = jnp.dot(queries[...], minus[...], preferred_element_type=F32)
    col_diff = jnp.dot(keys, minus[...], preferred_element_type=F32)
    copies = []
    for row in range(first.shape[0]):
        products = keys * queries[row:row + 1, :]
        value = jnp.dot(products, right[...], preferred_element_type=F32)
        value = value + first[row] + (row_diff[row:row + 1, :] - col_diff)
        pair[row] = value.astype(BF16)
        copy = pltpu.make_async_copy(pair.at[row], pair_hbm.at[row], sem.at[row])
        copy.start()
        copies.append(copy)
    for copy in copies:
        copy.wait()
    single_copy.wait()


def pair_part(blocks, queries, first, right, minus, single):
    tok_count = first.shape[0]
    vmem = pl.BlockSpec(memory_space=pltpu.VMEM)
    return pl.pallas_call(
        pair_kernel,
        out_shape=(
            jax.ShapeDtypeStruct(single.shape, BF16),
            jax.ShapeDtypeStruct(first.shape, BF16),
        ),
        in_specs=[vmem] * 6,
        out_specs=(pl.BlockSpec(memory_space=pltpu.HBM),) * 2,
        scratch_shapes=[
            pltpu.VMEM(first.shape, BF16),
            pltpu.SemaphoreType.DMA((tok_count,)),
            pltpu.SemaphoreType.DMA,
        ],
        compiler_params=pltpu.CompilerParams(vmem_limit_bytes=32 * 2**20),
        cost_estimate=pl.CostEstimate(
            flops=2 * first.size * right.shape[0],
            bytes_accessed=6 * first.size,
            transcendentals=0,
        ),
        name="pair_rows",
    )(blocks, queries, first, right, minus, single)


def shards(
    hidden_states,
    layer_mix,
    norm_gain,
    norm_bias,
    proj_in,
    proj_in_bias,
    proj_out,
    proj_out_bias,
    residue_tokens,
    residue_table,
    pair_norm_gain,
    pair_norm_bias,
    qk_weight,
    qk_bias,
    pair_weight,
    relpos_bins,
    relpos_table,
    chain_ids,
    chain_table,
):
    device_count = lax.axis_size("seq")
    single, queries, copies, first, right, minus = single_part(
        device_count,
        (
            hidden_states, layer_mix, norm_gain, norm_bias, proj_in, proj_in_bias, proj_out,
            proj_out_bias, residue_tokens, residue_table, pair_norm_gain, pair_norm_bias,
            qk_weight, qk_bias, chain_ids, relpos_bins, pair_weight, relpos_table, chain_table,
        ),
    )
    order = [device_count - 1] + list(range(device_count - 1))
    blocks = lax.all_to_all(
        copies, "seq", split_axis=0, concat_axis=0, axis_index_groups=[order]
    )
    return pair_part(blocks, queries, first, right, minus, single)


def solution(mesh):
    in_specs = (
        P(None, ("groups", "seq"), None),
        P(),
        P(),
        P(),
        P(),
        P(),
        P(),
        P(),
        P(("groups", "seq")),
        P(),
        P(),
        P(),
        P(),
        P(),
        P(),
        P(("groups", "seq"), None),
        P(),
        P(("groups", "seq")),
        P(),
    )
    out_specs = (P(("groups", "seq"), None), P(("groups", "seq"), None, None))
    return jax.shard_map(shards, mesh=mesh, in_specs=in_specs, out_specs=out_specs, check_vma=False)
```

```python
import functools

import jax
import jax.numpy as jnp
from jax import lax
from jax.experimental import pallas as pl
from jax.experimental.pallas import tpu as pltpu
from jax.sharding import PartitionSpec as P

epsilon = 1e-05
BF16 = jnp.bfloat16
F32 = jnp.float32


def pieces(total, count):
    count = max(1, min(count, total))
    ends = [total * step // count for step in range(count + 1)]
    return [(low, high - low) for low, high in zip(ends[:-1], ends[1:])]


def row_norm(values, gain, bias):
    center = values - jnp.mean(values, axis=-1, keepdims=True)
    spread = jnp.mean(center * center, axis=-1, keepdims=True)
    return center * lax.rsqrt(spread + epsilon) * gain + bias


def chain_flags(chain, tok_count, inner_dim):
    lanes = lax.broadcasted_iota(jnp.int32, (tok_count, 2 * inner_dim), 1)
    flag = lax.rem(lanes, inner_dim // 2).astype(F32)
    square = (tok_count, tok_count)
    own = lax.broadcasted_iota(jnp.int32, square, 0) == lax.broadcasted_iota(jnp.int32, square, 1)
    chain_col = jnp.sum(jnp.where(own, chain[...].astype(F32), 0.0), axis=1, keepdims=True)
    return jnp.where(flag == chain_col, 1.0, 0.0)


def operand_rows(bins, pair_weight, relpos, chain_table, bin_rows, right, minus, tok_count):
    bin_count = relpos.shape[0]
    inner_dim = pair_weight.shape[0] // 2
    flag_count = inner_dim // 2
    step = chain_table[1:2, :] - chain_table[0:1, :]
    step_high = step.astype(BF16).astype(F32)
    shape = (flag_count, step.shape[1])
    right[0:inner_dim, :] = pair_weight[0:inner_dim, :]
    right[inner_dim:inner_dim + flag_count, :] = jnp.broadcast_to(step_high, shape).astype(BF16)
    right[inner_dim + flag_count:, :] = jnp.broadcast_to(step - step_high, shape).astype(BF16)
    minus[0:inner_dim, :] = pair_weight[inner_dim:, :]
    minus[inner_dim:, :] = jnp.zeros((inner_dim, step.shape[1]), BF16)
    bin_rows[...] = jnp.zeros(bin_rows.shape, F32)
    bin_rows[0:bin_count, :] = relpos[...] + chain_table[0:1, :]
    padded = jnp.concatenate(
        [bins[...], jnp.zeros((128 - tok_count, bins.shape[1]), jnp.int32)], axis=0
    )
    return padded.T


def single_kernel(
    plan,
    hidden_hbm, mix_hbm, norm_gain_hbm, norm_bias_hbm, proj_in_hbm, proj_in_bias_hbm,
    proj_out_hbm, proj_out_bias_hbm, tokens_hbm, residue_hbm, pair_gain_hbm, pair_bias_hbm,
    qk_hbm, qk_bias_hbm, chain_hbm, bins_hbm, pair_weight_hbm, relpos_hbm, chain_table_hbm,
    single, query_ref, copies_ref, first, right, minus,
    hidden, mix, norm_gain, norm_bias, proj_in, proj_in_bias, proj_out, proj_out_bias, tokens,
    residue, pair_gain, pair_bias, qk, qk_bias, chain, bins, pair_weight, relpos, chain_table,
    mixture, residue_rows, bin_rows, sem_hidden, sem_in, sem_out, sem_small,
):
    in_pieces, out_pieces = plan
    tok_count = mixture.shape[0]
    inner_dim = qk.shape[1] // 2

    small = [
        (mix_hbm, mix), (tokens_hbm, tokens), (residue_hbm, residue),
        (norm_gain_hbm, norm_gain), (norm_bias_hbm, norm_bias),
        (proj_in_bias_hbm, proj_in_bias), (proj_out_bias_hbm, proj_out_bias),
        (pair_gain_hbm, pair_gain), (pair_bias_hbm, pair_bias),
        (qk_hbm, qk), (qk_bias_hbm, qk_bias), (chain_hbm, chain), (bins_hbm, bins),
        (pair_weight_hbm, pair_weight), (relpos_hbm, relpos), (chain_table_hbm, chain_table),
    ]
    small = [
        pltpu.make_async_copy(source, target, sem_small.at[at])
        for at, (source, target) in enumerate(small)
    ]
    states = [
        pltpu.make_async_copy(
            hidden_hbm.at[:, :, pl.ds(low, size)],
            hidden.at[:, :, pl.ds(low, size)],
            sem_hidden.at[at],
        )
        for at, (low, size) in enumerate(in_pieces)
    ]
    firsts = [
        pltpu.make_async_copy(
            proj_in_hbm.at[pl.ds(low, size)], proj_in.at[pl.ds(low, size)], sem_in.at[at]
        )
        for at, (low, size) in enumerate(in_pieces)
    ]
    seconds = [
        pltpu.make_async_copy(
            proj_out_hbm.at[pl.ds(low, size)], proj_out.at[pl.ds(low, size)], sem_out.at[at]
        )
        for at, (low, size) in enumerate(out_pieces)
    ]
    small[0].start()
    states[0].start()
    for copy in small[1:] + states[1:]:
        copy.start()
    for copy in firsts + seconds:
        copy.start(priority=1)

    width = mixture.shape[1]
    small[0].wait()
    shift = sums = squares = None
    for at, (low, size) in enumerate(in_pieces):
        states[at].wait()
        total = None
        for state in range(hidden.shape[0]):
            term = mix[state] * hidden[state, :, low:low + size].astype(F32)
            total = term if total is None else total + term
        mixture[:, low:low + size] = total
        if shift is None:
            shift = jnp.mean(total, axis=1, keepdims=True)
        total = total - shift
        for lane in range(0, size, 128):
            part = total[:, lane:lane + 128]
            sums = part if sums is None else sums + part
            squares = part * part if squares is None else squares + part * part
        if at == min(1, len(in_pieces) - 1):
            for copy in small[1:]:
                copy.wait()
            bins_col = operand_rows(
                bins, pair_weight, relpos, chain_table, bin_rows, right, minus, tok_count
            )
            flags = chain_flags(chain, tok_count, inner_dim)
            for row in range(tok_count):
                residue_rows[pl.ds(row, 1), :] = residue[pl.ds(tokens[row], 1), :]

    offset = jnp.sum(sums, axis=1, keepdims=True) / width
    spread = jnp.sum(squares, axis=1, keepdims=True) / width - offset * offset
    mean = shift + offset
    scale = lax.rsqrt(jnp.maximum(spread, 0.0) + epsilon)
    gain, bias = norm_gain[...].reshape(1, width), norm_bias[...].reshape(1, width)
    bin_table = bin_rows[...].astype(BF16)
    lanes = lax.broadcasted_iota(jnp.int32, (bins_col.shape[0], bin_table.shape[0]), 1)
    row_pieces = pieces(tok_count, max(1, len(in_pieces) - 1))
    total = None
    for at, (low, size) in enumerate(in_pieces):
        span = slice(low, low + size)
        normed = ((mixture[:, span] - mean) * scale * gain[:, span] + bias[:, span]).astype(BF16)
        firsts[at].wait()
        term = jnp.dot(normed, proj_in[pl.ds(low, size), :], preferred_element_type=F32)
        total = term if total is None else total + term
        if at < len(row_pieces):
            for row in range(row_pieces[at][0], sum(row_pieces[at])):
                onehot = jnp.where(bins_col[:, row:row + 1] == lanes, 1.0, 0.0).astype(BF16)
                first[row] = jnp.dot(onehot, bin_table, preferred_element_type=F32)
    middle = jnp.maximum(total + proj_in_bias[...], 0.0).astype(BF16)

    total = None
    for at, (low, size) in enumerate(out_pieces):
        seconds[at].wait()
        term = jnp.dot(
            middle[:, low:low + size], proj_out[pl.ds(low, size), :], preferred_element_type=F32
        )
        total = term if total is None else total + term
    single_f = total + proj_out_bias[...] + residue_rows[...]
    single[...] = single_f.astype(BF16)

    pair_in = row_norm(single_f, pair_gain[...], pair_bias[...]).astype(BF16)
    query_key = jnp.dot(pair_in, qk[...], preferred_element_type=F32) + qk_bias[...]

    front = lax.broadcasted_iota(jnp.int32, flags.shape, 1) < inner_dim
    query_ref[...] = jnp.where(front, query_key, flags).astype(BF16)
    block = jnp.where(front, pltpu.roll(query_key, inner_dim, 1), flags).astype(BF16)
    for peer in range(copies_ref.shape[0]):
        copies_ref[peer] = block


def single_part(device_count, operands):
    (hidden, mix, norm_gain, norm_bias, proj_in, proj_in_bias, proj_out, proj_out_bias, tokens,
     residue, pair_gain, pair_bias, qk, qk_bias, chain, bins, pair_weight, relpos,
     chain_table) = operands
    tok_count, width = hidden.shape[1:]
    channels = proj_out.shape[1]
    lanes = qk.shape[1]
    table_rows = -(-relpos.shape[0] // 128) * 128
    vmem = pl.BlockSpec(memory_space=pltpu.VMEM)
    plan = (pieces(width, 5), pieces(channels, 2))
    args = (
        hidden, mix, norm_gain, norm_bias, proj_in, proj_in_bias[None],
        proj_out, proj_out_bias[None], tokens, residue, pair_gain[None], pair_bias[None],
        qk, qk_bias[None], chain[None], bins, pair_weight, relpos, chain_table,
    )
    args = [pltpu.with_memory_space_constraint(arg, pltpu.HBM) for arg in args]
    in_smem = (1, 8)
    scratch = [
        (pltpu.SMEM if at in in_smem else pltpu.VMEM)(arg.shape, arg.dtype)
        for at, arg in enumerate(args)
    ]
    scratch += [
        pltpu.VMEM((tok_count, width), F32),
        pltpu.VMEM((tok_count, channels), F32),
        pltpu.VMEM((table_rows, pair_weight.shape[1]), F32),
        pltpu.SemaphoreType.DMA((len(plan[0]),)),
        pltpu.SemaphoreType.DMA((len(plan[0]),)),
        pltpu.SemaphoreType.DMA((len(plan[1]),)),
        pltpu.SemaphoreType.DMA((16,)),
    ]
    moved = sum(arg.size * arg.dtype.itemsize for arg in args)
    return pl.pallas_call(
        functools.partial(single_kernel, plan),
        out_shape=(
            jax.ShapeDtypeStruct((tok_count, channels), BF16),
            jax.ShapeDtypeStruct((tok_count, lanes), BF16),
            jax.ShapeDtypeStruct((device_count, tok_count, lanes), BF16),
            jax.ShapeDtypeStruct(bins.shape + pair_weight.shape[1:], F32),
            jax.ShapeDtypeStruct(pair_weight.shape, BF16),
            jax.ShapeDtypeStruct(pair_weight.shape, BF16),
        ),
        in_specs=[pl.BlockSpec(memory_space=pltpu.HBM)] * len(args),
        out_specs=(vmem,) * 6,
        scratch_shapes=scratch,
        compiler_params=pltpu.CompilerParams(vmem_limit_bytes=32 * 2**20),
        cost_estimate=pl.CostEstimate(
            flops=2 * tok_count * channels * (width + channels + lanes),
            bytes_accessed=moved,
            transcendentals=0,
        ),
        name="single_path",
    )(*args)


def pair_kernel(
    blocks, queries, first, right, minus, single, single_hbm, pair_hbm, pair, sem, sem_single
):
    single_copy = pltpu.make_async_copy(single, single_hbm, sem_single)
    single_copy.start()
    keys = jnp.concatenate([blocks[1:].reshape(-1, blocks.shape[2]), blocks[0]], axis=0)
    row_diff = jnp.dot(queries[...], minus[...], preferred_element_type=F32)
    col_diff = jnp.dot(keys, minus[...], preferred_element_type=F32)
    copies = []
    for row in range(first.shape[0]):
        products = keys * queries[row:row + 1, :]
        value = jnp.dot(products, right[...], preferred_element_type=F32)
        value = value + first[row] + (row_diff[row:row + 1, :] - col_diff)
        pair[row] = value.astype(BF16)
        copy = pltpu.make_async_copy(pair.at[row], pair_hbm.at[row], sem.at[row])
        copy.start()
        copies.append(copy)
    for copy in copies:
        copy.wait()
    single_copy.wait()


def pair_part(blocks, queries, first, right, minus, single):
    tok_count = first.shape[0]
    vmem = pl.BlockSpec(memory_space=pltpu.VMEM)
    return pl.pallas_call(
        pair_kernel,
        out_shape=(
            jax.ShapeDtypeStruct(single.shape, BF16),
            jax.ShapeDtypeStruct(first.shape, BF16),
        ),
        in_specs=[vmem] * 6,
        out_specs=(pl.BlockSpec(memory_space=pltpu.HBM),) * 2,
        scratch_shapes=[
            pltpu.VMEM(first.shape, BF16),
            pltpu.SemaphoreType.DMA((tok_count,)),
            pltpu.SemaphoreType.DMA,
        ],
        compiler_params=pltpu.CompilerParams(vmem_limit_bytes=32 * 2**20),
        cost_estimate=pl.CostEstimate(
            flops=2 * first.size * right.shape[0],
            bytes_accessed=6 * first.size,
            transcendentals=0,
        ),
        name="pair_rows",
    )(blocks, queries, first, right, minus, single)


def shards(
    hidden_states,
    layer_mix,
    norm_gain,
    norm_bias,
    proj_in,
    proj_in_bias,
    proj_out,
    proj_out_bias,
    residue_tokens,
    residue_table,
    pair_norm_gain,
    pair_norm_bias,
    qk_weight,
    qk_bias,
    pair_weight,
    relpos_bins,
    relpos_table,
    chain_ids,
    chain_table,
):
    device_count = lax.axis_size("seq")
    single, queries, copies, first, right, minus = single_part(
        device_count,
        (
            hidden_states, layer_mix, norm_gain, norm_bias, proj_in, proj_in_bias, proj_out,
            proj_out_bias, residue_tokens, residue_table, pair_norm_gain, pair_norm_bias,
            qk_weight, qk_bias, chain_ids, relpos_bins, pair_weight, relpos_table, chain_table,
        ),
    )
    order = [device_count - 1] + list(range(device_count - 1))
    blocks = lax.all_to_all(
        copies, "seq", split_axis=0, concat_axis=0, axis_index_groups=[order]
    )
    return pair_part(blocks, queries, first, right, minus, single)


def solution(mesh):
    in_specs = (
        P(None, ("groups", "seq"), None),
        P(),
        P(),
        P(),
        P(),
        P(),
        P(),
        P(),
        P(("groups", "seq")),
        P(),
        P(),
        P(),
        P(),
        P(),
        P(),
        P(("groups", "seq"), None),
        P(),
        P(("groups", "seq")),
        P(),
    )
    out_specs = (P(("groups", "seq"), None), P(("groups", "seq"), None, None))
    return jax.shard_map(shards, mesh=mesh, in_specs=in_specs, out_specs=out_specs, check_vma=False)
```

```python
import functools

import jax
import jax.numpy as jnp
from jax import lax
from jax.experimental import pallas as pl
from jax.experimental.pallas import tpu as pltpu
from jax.sharding import PartitionSpec as P

epsilon = 1e-05
BF16 = jnp.bfloat16
F32 = jnp.float32


def pieces(total, count):
    count = max(1, min(count, total))
    ends = [total * step // count for step in range(count + 1)]
    return [(low, high - low) for low, high in zip(ends[:-1], ends[1:])]


def row_norm(values, gain, bias):
    center = values - jnp.mean(values, axis=-1, keepdims=True)
    spread = jnp.mean(center * center, axis=-1, keepdims=True)
    return center * lax.rsqrt(spread + epsilon) * gain + bias


def chain_flags(chain, tok_count, inner_dim):
    lanes = lax.broadcasted_iota(jnp.int32, (tok_count, 2 * inner_dim), 1)
    flag = lax.rem(lanes, inner_dim // 2).astype(F32)
    square = (tok_count, tok_count)
    own = lax.broadcasted_iota(jnp.int32, square, 0) == lax.broadcasted_iota(jnp.int32, square, 1)
    chain_col = jnp.sum(jnp.where(own, chain[...].astype(F32), 0.0), axis=1, keepdims=True)
    return jnp.where(flag == chain_col, 1.0, 0.0)


def operand_rows(bins, pair_weight, relpos, chain_table, bin_rows, right, minus, tok_count):
    bin_count = relpos.shape[0]
    inner_dim = pair_weight.shape[0] // 2
    flag_count = inner_dim // 2
    step = chain_table[1:2, :] - chain_table[0:1, :]
    step_high = step.astype(BF16).astype(F32)
    shape = (flag_count, step.shape[1])
    right[0:inner_dim, :] = pair_weight[0:inner_dim, :]
    right[inner_dim:inner_dim + flag_count, :] = jnp.broadcast_to(step_high, shape).astype(BF16)
    right[inner_dim + flag_count:, :] = jnp.broadcast_to(step - step_high, shape).astype(BF16)
    minus[0:inner_dim, :] = pair_weight[inner_dim:, :]
    minus[inner_dim:, :] = jnp.zeros((inner_dim, step.shape[1]), BF16)
    bin_rows[...] = jnp.zeros(bin_rows.shape, F32)
    bin_rows[0:bin_count, :] = relpos[...] + chain_table[0:1, :]
    padded = jnp.concatenate(
        [bins[...], jnp.zeros((128 - tok_count, bins.shape[1]), jnp.int32)], axis=0
    )
    return padded.T


def single_kernel(
    plan,
    hidden_hbm, mix_hbm, norm_gain_hbm, norm_bias_hbm, proj_in_hbm, proj_in_bias_hbm,
    proj_out_hbm, proj_out_bias_hbm, tokens_hbm, residue_hbm, pair_gain_hbm, pair_bias_hbm,
    qk_hbm, qk_bias_hbm, chain_hbm, bins_hbm, pair_weight_hbm, relpos_hbm, chain_table_hbm,
    single, query_ref, copies_ref, first, right, minus,
    hidden, mix, norm_gain, norm_bias, proj_in, proj_in_bias, proj_out, proj_out_bias, tokens,
    residue, pair_gain, pair_bias, qk, qk_bias, chain, bins, pair_weight, relpos, chain_table,
    mixture, residue_rows, bin_rows, sem_hidden, sem_in, sem_out, sem_small,
):
    in_pieces, out_pieces = plan
    tok_count = mixture.shape[0]
    inner_dim = qk.shape[1] // 2

    small = [
        (mix_hbm, mix), (tokens_hbm, tokens), (residue_hbm, residue),
        (norm_gain_hbm, norm_gain), (norm_bias_hbm, norm_bias),
        (proj_in_bias_hbm, proj_in_bias), (proj_out_bias_hbm, proj_out_bias),
        (pair_gain_hbm, pair_gain), (pair_bias_hbm, pair_bias),
        (qk_hbm, qk), (qk_bias_hbm, qk_bias), (chain_hbm, chain), (bins_hbm, bins),
        (pair_weight_hbm, pair_weight), (relpos_hbm, relpos), (chain_table_hbm, chain_table),
    ]
    small = [
        pltpu.make_async_copy(source, target, sem_small.at[at])
        for at, (source, target) in enumerate(small)
    ]
    states = [
        pltpu.make_async_copy(
            hidden_hbm.at[:, :, pl.ds(low, size)],
            hidden.at[:, :, pl.ds(low, size)],
            sem_hidden.at[at],
        )
        for at, (low, size) in enumerate(in_pieces)
    ]
    firsts = [
        pltpu.make_async_copy(
            proj_in_hbm.at[pl.ds(low, size)], proj_in.at[pl.ds(low, size)], sem_in.at[at]
        )
        for at, (low, size) in enumerate(in_pieces)
    ]
    seconds = [
        pltpu.make_async_copy(
            proj_out_hbm.at[pl.ds(low, size)], proj_out.at[pl.ds(low, size)], sem_out.at[at]
        )
        for at, (low, size) in enumerate(out_pieces)
    ]
    small[0].start()
    states[0].start()
    for copy in small[1:] + states[1:]:
        copy.start()
    later = firsts + seconds
    for copy in later[:3]:
        copy.start(priority=1)
    later = later[3:]

    width = mixture.shape[1]
    small[0].wait()
    shift = sums = squares = None
    for at, (low, size) in enumerate(in_pieces):
        states[at].wait()
        if at % 2 == 0:
            for copy in later if at >= len(in_pieces) - 2 else later[:1]:
                copy.start(priority=1)
            later = later[1:] if at < len(in_pieces) - 2 else []
        total = None
        for state in range(hidden.shape[0]):
            term = mix[state] * hidden[state, :, low:low + size].astype(F32)
            total = term if total is None else total + term
        mixture[:, low:low + size] = total
        if shift is None:
            shift = jnp.mean(total, axis=1, keepdims=True)
        total = total - shift
        for lane in range(0, size, 128):
            part = total[:, lane:lane + 128]
            sums = part if sums is None else sums + part
            squares = part * part if squares is None else squares + part * part
        if at == min(1, len(in_pieces) - 1):
            for copy in small[1:]:
                copy.wait()
            bins_col = operand_rows(
                bins, pair_weight, relpos, chain_table, bin_rows, right, minus, tok_count
            )
            flags = chain_flags(chain, tok_count, inner_dim)
            for row in range(tok_count):
                residue_rows[pl.ds(row, 1), :] = residue[pl.ds(tokens[row], 1), :]
    for copy in later:
        copy.start(priority=1)

    offset = jnp.sum(sums, axis=1, keepdims=True) / width
    spread = jnp.sum(squares, axis=1, keepdims=True) / width - offset * offset
    mean = shift + offset
    scale = lax.rsqrt(jnp.maximum(spread, 0.0) + epsilon)
    gain, bias = norm_gain[...].reshape(1, width), norm_bias[...].reshape(1, width)
    bin_table = bin_rows[...].astype(BF16)
    lanes = lax.broadcasted_iota(jnp.int32, (bins_col.shape[0], bin_table.shape[0]), 1)
    row_pieces = pieces(tok_count, max(1, len(in_pieces) - 1))
    total = None
    for at, (low, size) in enumerate(in_pieces):
        span = slice(low, low + size)
        normed = ((mixture[:, span] - mean) * scale * gain[:, span] + bias[:, span]).astype(BF16)
        firsts[at].wait()
        term = jnp.dot(normed, proj_in[pl.ds(low, size), :], preferred_element_type=F32)
        total = term if total is None else total + term
        if at < len(row_pieces):
            for row in range(row_pieces[at][0], sum(row_pieces[at])):
                onehot = jnp.where(bins_col[:, row:row + 1] == lanes, 1.0, 0.0).astype(BF16)
                first[row] = jnp.dot(onehot, bin_table, preferred_element_type=F32)
    middle = jnp.maximum(total + proj_in_bias[...], 0.0).astype(BF16)

    total = None
    for at, (low, size) in enumerate(out_pieces):
        seconds[at].wait()
        term = jnp.dot(
            middle[:, low:low + size], proj_out[pl.ds(low, size), :], preferred_element_type=F32
        )
        total = term if total is None else total + term
    single_f = total + proj_out_bias[...] + residue_rows[...]
    single[...] = single_f.astype(BF16)

    pair_in = row_norm(single_f, pair_gain[...], pair_bias[...]).astype(BF16)
    query_key = jnp.dot(pair_in, qk[...], preferred_element_type=F32) + qk_bias[...]

    front = lax.broadcasted_iota(jnp.int32, flags.shape, 1) < inner_dim
    query_ref[...] = jnp.where(front, query_key, flags).astype(BF16)
    block = jnp.where(front, pltpu.roll(query_key, inner_dim, 1), flags).astype(BF16)
    for peer in range(copies_ref.shape[0]):
        copies_ref[peer] = block


def single_part(device_count, operands):
    (hidden, mix, norm_gain, norm_bias, proj_in, proj_in_bias, proj_out, proj_out_bias, tokens,
     residue, pair_gain, pair_bias, qk, qk_bias, chain, bins, pair_weight, relpos,
     chain_table) = operands
    tok_count, width = hidden.shape[1:]
    channels = proj_out.shape[1]
    lanes = qk.shape[1]
    table_rows = -(-relpos.shape[0] // 128) * 128
    vmem = pl.BlockSpec(memory_space=pltpu.VMEM)
    plan = (pieces(width, 5), pieces(channels, 2))
    args = (
        hidden, mix, norm_gain, norm_bias, proj_in, proj_in_bias[None],
        proj_out, proj_out_bias[None], tokens, residue, pair_gain[None], pair_bias[None],
        qk, qk_bias[None], chain[None], bins, pair_weight, relpos, chain_table,
    )
    args = [pltpu.with_memory_space_constraint(arg, pltpu.HBM) for arg in args]
    in_smem = (1, 8)
    scratch = [
        (pltpu.SMEM if at in in_smem else pltpu.VMEM)(arg.shape, arg.dtype)
        for at, arg in enumerate(args)
    ]
    scratch += [
        pltpu.VMEM((tok_count, width), F32),
        pltpu.VMEM((tok_count, channels), F32),
        pltpu.VMEM((table_rows, pair_weight.shape[1]), F32),
        pltpu.SemaphoreType.DMA((len(plan[0]),)),
        pltpu.SemaphoreType.DMA((len(plan[0]),)),
        pltpu.SemaphoreType.DMA((len(plan[1]),)),
        pltpu.SemaphoreType.DMA((16,)),
    ]
    moved = sum(arg.size * arg.dtype.itemsize for arg in args)
    return pl.pallas_call(
        functools.partial(single_kernel, plan),
        out_shape=(
            jax.ShapeDtypeStruct((tok_count, channels), BF16),
            jax.ShapeDtypeStruct((tok_count, lanes), BF16),
            jax.ShapeDtypeStruct((device_count, tok_count, lanes), BF16),
            jax.ShapeDtypeStruct(bins.shape + pair_weight.shape[1:], F32),
            jax.ShapeDtypeStruct(pair_weight.shape, BF16),
            jax.ShapeDtypeStruct(pair_weight.shape, BF16),
        ),
        in_specs=[pl.BlockSpec(memory_space=pltpu.HBM)] * len(args),
        out_specs=(vmem,) * 6,
        scratch_shapes=scratch,
        compiler_params=pltpu.CompilerParams(vmem_limit_bytes=32 * 2**20),
        cost_estimate=pl.CostEstimate(
            flops=2 * tok_count * channels * (width + channels + lanes),
            bytes_accessed=moved,
            transcendentals=0,
        ),
        name="single_path",
    )(*args)


def pair_kernel(
    blocks, queries, first, right, minus, single, single_hbm, pair_hbm, pair, sem, sem_single
):
    single_copy = pltpu.make_async_copy(single, single_hbm, sem_single)
    single_copy.start()
    keys = jnp.concatenate([blocks[1:].reshape(-1, blocks.shape[2]), blocks[0]], axis=0)
    row_diff = jnp.dot(queries[...], minus[...], preferred_element_type=F32)
    col_diff = jnp.dot(keys, minus[...], preferred_element_type=F32)
    copies = []
    for row in range(first.shape[0]):
        products = keys * queries[row:row + 1, :]
        value = jnp.dot(products, right[...], preferred_element_type=F32)
        value = value + first[row] + (row_diff[row:row + 1, :] - col_diff)
        pair[row] = value.astype(BF16)
        copy = pltpu.make_async_copy(pair.at[row], pair_hbm.at[row], sem.at[row])
        copy.start()
        copies.append(copy)
    for copy in copies:
        copy.wait()
    single_copy.wait()


def pair_part(blocks, queries, first, right, minus, single):
    tok_count = first.shape[0]
    vmem = pl.BlockSpec(memory_space=pltpu.VMEM)
    return pl.pallas_call(
        pair_kernel,
        out_shape=(
            jax.ShapeDtypeStruct(single.shape, BF16),
            jax.ShapeDtypeStruct(first.shape, BF16),
        ),
        in_specs=[vmem] * 6,
        out_specs=(pl.BlockSpec(memory_space=pltpu.HBM),) * 2,
        scratch_shapes=[
            pltpu.VMEM(first.shape, BF16),
            pltpu.SemaphoreType.DMA((tok_count,)),
            pltpu.SemaphoreType.DMA,
        ],
        compiler_params=pltpu.CompilerParams(vmem_limit_bytes=32 * 2**20),
        cost_estimate=pl.CostEstimate(
            flops=2 * first.size * right.shape[0],
            bytes_accessed=6 * first.size,
            transcendentals=0,
        ),
        name="pair_rows",
    )(blocks, queries, first, right, minus, single)


def shards(
    hidden_states,
    layer_mix,
    norm_gain,
    norm_bias,
    proj_in,
    proj_in_bias,
    proj_out,
    proj_out_bias,
    residue_tokens,
    residue_table,
    pair_norm_gain,
    pair_norm_bias,
    qk_weight,
    qk_bias,
    pair_weight,
    relpos_bins,
    relpos_table,
    chain_ids,
    chain_table,
):
    device_count = lax.axis_size("seq")
    single, queries, copies, first, right, minus = single_part(
        device_count,
        (
            hidden_states, layer_mix, norm_gain, norm_bias, proj_in, proj_in_bias, proj_out,
            proj_out_bias, residue_tokens, residue_table, pair_norm_gain, pair_norm_bias,
            qk_weight, qk_bias, chain_ids, relpos_bins, pair_weight, relpos_table, chain_table,
        ),
    )
    order = [device_count - 1] + list(range(device_count - 1))
    blocks = lax.all_to_all(
        copies, "seq", split_axis=0, concat_axis=0, axis_index_groups=[order]
    )
    return pair_part(blocks, queries, first, right, minus, single)


def solution(mesh):
    in_specs = (
        P(None, ("groups", "seq"), None),
        P(),
        P(),
        P(),
        P(),
        P(),
        P(),
        P(),
        P(("groups", "seq")),
        P(),
        P(),
        P(),
        P(),
        P(),
        P(),
        P(("groups", "seq"), None),
        P(),
        P(("groups", "seq")),
        P(),
    )
    out_specs = (P(("groups", "seq"), None), P(("groups", "seq"), None, None))
    return jax.shard_map(shards, mesh=mesh, in_specs=in_specs, out_specs=out_specs, check_vma=False)
```

```python
import functools

import jax
import jax.numpy as jnp
from jax import lax
from jax.experimental import pallas as pl
from jax.experimental.pallas import tpu as pltpu
from jax.sharding import PartitionSpec as P

epsilon = 1e-05
BF16 = jnp.bfloat16
F32 = jnp.float32


def pieces(total, count):
    count = max(1, min(count, total))
    ends = [total * step // count for step in range(count + 1)]
    return [(low, high - low) for low, high in zip(ends[:-1], ends[1:])]


def row_norm(values, gain, bias):
    center = values - jnp.mean(values, axis=-1, keepdims=True)
    spread = jnp.mean(center * center, axis=-1, keepdims=True)
    return center * lax.rsqrt(spread + epsilon) * gain + bias


def chain_flags(chain, tok_count, inner_dim):
    lanes = lax.broadcasted_iota(jnp.int32, (tok_count, 2 * inner_dim), 1)
    flag = lax.rem(lanes, inner_dim // 2).astype(F32)
    square = (tok_count, tok_count)
    own = lax.broadcasted_iota(jnp.int32, square, 0) == lax.broadcasted_iota(jnp.int32, square, 1)
    chain_col = jnp.sum(jnp.where(own, chain[...].astype(F32), 0.0), axis=1, keepdims=True)
    return jnp.where(flag == chain_col, 1.0, 0.0)


def operand_rows(bins, pair_weight, relpos, chain_table, bin_rows, right, minus, tok_count):
    bin_count = relpos.shape[0]
    inner_dim = pair_weight.shape[0] // 2
    flag_count = inner_dim // 2
    step = chain_table[1:2, :] - chain_table[0:1, :]
    step_high = step.astype(BF16).astype(F32)
    shape = (flag_count, step.shape[1])
    right[0:inner_dim, :] = pair_weight[0:inner_dim, :]
    right[inner_dim:inner_dim + flag_count, :] = jnp.broadcast_to(step_high, shape).astype(BF16)
    right[inner_dim + flag_count:, :] = jnp.broadcast_to(step - step_high, shape).astype(BF16)
    minus[0:inner_dim, :] = pair_weight[inner_dim:, :]
    minus[inner_dim:, :] = jnp.zeros((inner_dim, step.shape[1]), BF16)
    bin_rows[...] = jnp.zeros(bin_rows.shape, F32)
    bin_rows[0:bin_count, :] = relpos[...] + chain_table[0:1, :]
    padded = jnp.concatenate(
        [bins[...], jnp.zeros((128 - tok_count, bins.shape[1]), jnp.int32)], axis=0
    )
    return padded.T


def single_kernel(
    plan,
    hidden_hbm, mix_hbm, norm_gain_hbm, norm_bias_hbm, proj_in_hbm, proj_in_bias_hbm,
    proj_out_hbm, proj_out_bias_hbm, tokens_hbm, residue_hbm, pair_gain_hbm, pair_bias_hbm,
    qk_hbm, qk_bias_hbm, chain_hbm, bins_hbm, pair_weight_hbm, relpos_hbm, chain_table_hbm,
    single, query_ref, copies_ref, first, right, minus,
    hidden, mix, norm_gain, norm_bias, proj_in, proj_in_bias, proj_out, proj_out_bias, tokens,
    residue, pair_gain, pair_bias, qk, qk_bias, chain, bins, pair_weight, relpos, chain_table,
    mixture, residue_rows, bin_rows, sem_hidden, sem_in, sem_out, sem_small,
):
    in_pieces, out_pieces = plan
    tok_count = mixture.shape[0]
    inner_dim = qk.shape[1] // 2

    small = [
        (bins_hbm, bins), (relpos_hbm, relpos), (chain_table_hbm, chain_table),
        (pair_weight_hbm, pair_weight), (chain_hbm, chain), (mix_hbm, mix),
        (norm_gain_hbm, norm_gain), (norm_bias_hbm, norm_bias), (tokens_hbm, tokens),
        (residue_hbm, residue), (proj_in_bias_hbm, proj_in_bias),
        (proj_out_bias_hbm, proj_out_bias), (pair_gain_hbm, pair_gain),
        (pair_bias_hbm, pair_bias), (qk_hbm, qk), (qk_bias_hbm, qk_bias),
    ]
    first_small = 6
    small = [
        pltpu.make_async_copy(source, target, sem_small.at[at])
        for at, (source, target) in enumerate(small)
    ]
    states = [
        pltpu.make_async_copy(
            hidden_hbm.at[:, :, pl.ds(low, size)],
            hidden.at[:, :, pl.ds(low, size)],
            sem_hidden.at[at],
        )
        for at, (low, size) in enumerate(in_pieces)
    ]
    firsts = [
        pltpu.make_async_copy(
            proj_in_hbm.at[pl.ds(low, size)], proj_in.at[pl.ds(low, size)], sem_in.at[at]
        )
        for at, (low, size) in enumerate(in_pieces)
    ]
    seconds = [
        pltpu.make_async_copy(
            proj_out_hbm.at[pl.ds(low, size)], proj_out.at[pl.ds(low, size)], sem_out.at[at]
        )
        for at, (low, size) in enumerate(out_pieces)
    ]
    for copy in small[:first_small] + states + small[first_small:]:
        copy.start()
    for copy in firsts + seconds:
        copy.start(priority=1)

    for copy in small[:first_small]:
        copy.wait()
    bins_col = operand_rows(
        bins, pair_weight, relpos, chain_table, bin_rows, right, minus, tok_count
    )
    bin_table = bin_rows[...].astype(BF16)
    lanes = lax.broadcasted_iota(jnp.int32, (bins_col.shape[0], bin_table.shape[0]), 1)
    for row in range(tok_count):
        onehot = jnp.where(bins_col[:, row:row + 1] == lanes, 1.0, 0.0).astype(BF16)
        first[row] = jnp.dot(onehot, bin_table, preferred_element_type=F32)
    flags = chain_flags(chain, tok_count, inner_dim)

    width = mixture.shape[1]
    shift = sums = squares = None
    for at, (low, size) in enumerate(in_pieces):
        states[at].wait()
        total = None
        for state in range(hidden.shape[0]):
            term = mix[state] * hidden[state, :, low:low + size].astype(F32)
            total = term if total is None else total + term
        mixture[:, low:low + size] = total
        if shift is None:
            shift = jnp.mean(total, axis=1, keepdims=True)
        total = total - shift
        for lane in range(0, size, 128):
            part = total[:, lane:lane + 128]
            sums = part if sums is None else sums + part
            squares = part * part if squares is None else squares + part * part
        if at == min(1, len(in_pieces) - 1):
            for copy in small[first_small:]:
                copy.wait()
            for row in range(tok_count):
                residue_rows[pl.ds(row, 1), :] = residue[pl.ds(tokens[row], 1), :]

    offset = jnp.sum(sums, axis=1, keepdims=True) / width
    spread = jnp.sum(squares, axis=1, keepdims=True) / width - offset * offset
    mean = shift + offset
    scale = lax.rsqrt(jnp.maximum(spread, 0.0) + epsilon)
    gain, bias = norm_gain[...].reshape(1, width), norm_bias[...].reshape(1, width)
    total = None
    for at, (low, size) in enumerate(in_pieces):
        span = slice(low, low + size)
        normed = ((mixture[:, span] - mean) * scale * gain[:, span] + bias[:, span]).astype(BF16)
        firsts[at].wait()
        term = jnp.dot(normed, proj_in[pl.ds(low, size), :], preferred_element_type=F32)
        total = term if total is None else total + term
    middle = jnp.maximum(total + proj_in_bias[...], 0.0).astype(BF16)

    total = None
    for at, (low, size) in enumerate(out_pieces):
        seconds[at].wait()
        term = jnp.dot(
            middle[:, low:low + size], proj_out[pl.ds(low, size), :], preferred_element_type=F32
        )
        total = term if total is None else total + term
    single_f = total + proj_out_bias[...] + residue_rows[...]
    single[...] = single_f.astype(BF16)

    pair_in = row_norm(single_f, pair_gain[...], pair_bias[...]).astype(BF16)
    query_key = jnp.dot(pair_in, qk[...], preferred_element_type=F32) + qk_bias[...]

    front = lax.broadcasted_iota(jnp.int32, flags.shape, 1) < inner_dim
    query_ref[...] = jnp.where(front, query_key, flags).astype(BF16)
    block = jnp.where(front, pltpu.roll(query_key, inner_dim, 1), flags).astype(BF16)
    for peer in range(copies_ref.shape[0]):
        copies_ref[peer] = block


def single_part(device_count, operands):
    (hidden, mix, norm_gain, norm_bias, proj_in, proj_in_bias, proj_out, proj_out_bias, tokens,
     residue, pair_gain, pair_bias, qk, qk_bias, chain, bins, pair_weight, relpos,
     chain_table) = operands
    tok_count, width = hidden.shape[1:]
    channels = proj_out.shape[1]
    lanes = qk.shape[1]
    table_rows = -(-relpos.shape[0] // 128) * 128
    vmem = pl.BlockSpec(memory_space=pltpu.VMEM)
    plan = (pieces(width, 5), pieces(channels, 2))
    args = (
        hidden, mix, norm_gain, norm_bias, proj_in, proj_in_bias[None],
        proj_out, proj_out_bias[None], tokens, residue, pair_gain[None], pair_bias[None],
        qk, qk_bias[None], chain[None], bins, pair_weight, relpos, chain_table,
    )
    args = [pltpu.with_memory_space_constraint(arg, pltpu.HBM) for arg in args]
    in_smem = (1, 8)
    scratch = [
        (pltpu.SMEM if at in in_smem else pltpu.VMEM)(arg.shape, arg.dtype)
        for at, arg in enumerate(args)
    ]
    scratch += [
        pltpu.VMEM((tok_count, width), F32),
        pltpu.VMEM((tok_count, channels), F32),
        pltpu.VMEM((table_rows, pair_weight.shape[1]), F32),
        pltpu.SemaphoreType.DMA((len(plan[0]),)),
        pltpu.SemaphoreType.DMA((len(plan[0]),)),
        pltpu.SemaphoreType.DMA((len(plan[1]),)),
        pltpu.SemaphoreType.DMA((16,)),
    ]
    moved = sum(arg.size * arg.dtype.itemsize for arg in args)
    return pl.pallas_call(
        functools.partial(single_kernel, plan),
        out_shape=(
            jax.ShapeDtypeStruct((tok_count, channels), BF16),
            jax.ShapeDtypeStruct((tok_count, lanes), BF16),
            jax.ShapeDtypeStruct((device_count, tok_count, lanes), BF16),
            jax.ShapeDtypeStruct(bins.shape + pair_weight.shape[1:], F32),
            jax.ShapeDtypeStruct(pair_weight.shape, BF16),
            jax.ShapeDtypeStruct(pair_weight.shape, BF16),
        ),
        in_specs=[pl.BlockSpec(memory_space=pltpu.HBM)] * len(args),
        out_specs=(vmem,) * 6,
        scratch_shapes=scratch,
        compiler_params=pltpu.CompilerParams(vmem_limit_bytes=32 * 2**20),
        cost_estimate=pl.CostEstimate(
            flops=2 * tok_count * channels * (width + channels + lanes),
            bytes_accessed=moved,
            transcendentals=0,
        ),
        name="single_path",
    )(*args)


def pair_kernel(
    blocks, queries, first, right, minus, single, single_hbm, pair_hbm, pair, sem, sem_single
):
    single_copy = pltpu.make_async_copy(single, single_hbm, sem_single)
    single_copy.start()
    keys = jnp.concatenate([blocks[1:].reshape(-1, blocks.shape[2]), blocks[0]], axis=0)
    row_diff = jnp.dot(queries[...], minus[...], preferred_element_type=F32)
    col_diff = jnp.dot(keys, minus[...], preferred_element_type=F32)
    copies = []
    for row in range(first.shape[0]):
        products = keys * queries[row:row + 1, :]
        value = jnp.dot(products, right[...], preferred_element_type=F32)
        value = value + first[row] + (row_diff[row:row + 1, :] - col_diff)
        pair[row] = value.astype(BF16)
        copy = pltpu.make_async_copy(pair.at[row], pair_hbm.at[row], sem.at[row])
        copy.start()
        copies.append(copy)
    for copy in copies:
        copy.wait()
    single_copy.wait()


def pair_part(blocks, queries, first, right, minus, single):
    tok_count = first.shape[0]
    vmem = pl.BlockSpec(memory_space=pltpu.VMEM)
    return pl.pallas_call(
        pair_kernel,
        out_shape=(
            jax.ShapeDtypeStruct(single.shape, BF16),
            jax.ShapeDtypeStruct(first.shape, BF16),
        ),
        in_specs=[vmem] * 6,
        out_specs=(pl.BlockSpec(memory_space=pltpu.HBM),) * 2,
        scratch_shapes=[
            pltpu.VMEM(first.shape, BF16),
            pltpu.SemaphoreType.DMA((tok_count,)),
            pltpu.SemaphoreType.DMA,
        ],
        compiler_params=pltpu.CompilerParams(vmem_limit_bytes=32 * 2**20),
        cost_estimate=pl.CostEstimate(
            flops=2 * first.size * right.shape[0],
            bytes_accessed=6 * first.size,
            transcendentals=0,
        ),
        name="pair_rows",
    )(blocks, queries, first, right, minus, single)


def shards(
    hidden_states,
    layer_mix,
    norm_gain,
    norm_bias,
    proj_in,
    proj_in_bias,
    proj_out,
    proj_out_bias,
    residue_tokens,
    residue_table,
    pair_norm_gain,
    pair_norm_bias,
    qk_weight,
    qk_bias,
    pair_weight,
    relpos_bins,
    relpos_table,
    chain_ids,
    chain_table,
):
    device_count = lax.axis_size("seq")
    single, queries, copies, first, right, minus = single_part(
        device_count,
        (
            hidden_states, layer_mix, norm_gain, norm_bias, proj_in, proj_in_bias, proj_out,
            proj_out_bias, residue_tokens, residue_table, pair_norm_gain, pair_norm_bias,
            qk_weight, qk_bias, chain_ids, relpos_bins, pair_weight, relpos_table, chain_table,
        ),
    )
    order = [device_count - 1] + list(range(device_count - 1))
    blocks = lax.all_to_all(
        copies, "seq", split_axis=0, concat_axis=0, axis_index_groups=[order]
    )
    return pair_part(blocks, queries, first, right, minus, single)


def solution(mesh):
    in_specs = (
        P(None, ("groups", "seq"), None),
        P(),
        P(),
        P(),
        P(),
        P(),
        P(),
        P(),
        P(("groups", "seq")),
        P(),
        P(),
        P(),
        P(),
        P(),
        P(),
        P(("groups", "seq"), None),
        P(),
        P(("groups", "seq")),
        P(),
    )
    out_specs = (P(("groups", "seq"), None), P(("groups", "seq"), None, None))
    return jax.shard_map(shards, mesh=mesh, in_specs=in_specs, out_specs=out_specs, check_vma=False)
```

```python
import functools

import jax
import jax.numpy as jnp
from jax import lax
from jax.experimental import pallas as pl
from jax.experimental.pallas import tpu as pltpu
from jax.sharding import PartitionSpec as P

epsilon = 1e-05
BF16 = jnp.bfloat16
F32 = jnp.float32


def pieces(total, count):
    count = max(1, min(count, total))
    ends = [total * step // count for step in range(count + 1)]
    return [(low, high - low) for low, high in zip(ends[:-1], ends[1:])]


def row_norm(values, gain, bias):
    center = values - jnp.mean(values, axis=-1, keepdims=True)
    spread = jnp.mean(center * center, axis=-1, keepdims=True)
    return center * lax.rsqrt(spread + epsilon) * gain + bias


def chain_flags(chain, tok_count, inner_dim):
    lanes = lax.broadcasted_iota(jnp.int32, (tok_count, 2 * inner_dim), 1)
    flag = lax.rem(lanes, inner_dim // 2).astype(F32)
    square = (tok_count, tok_count)
    own = lax.broadcasted_iota(jnp.int32, square, 0) == lax.broadcasted_iota(jnp.int32, square, 1)
    chain_col = jnp.sum(jnp.where(own, chain[...].astype(F32), 0.0), axis=1, keepdims=True)
    return jnp.where(flag == chain_col, 1.0, 0.0)


def operand_rows(bins, pair_weight, relpos, chain_table, bin_rows, right, minus, tok_count):
    bin_count = relpos.shape[0]
    inner_dim = pair_weight.shape[0] // 2
    flag_count = inner_dim // 2
    step = chain_table[1:2, :] - chain_table[0:1, :]
    step_high = step.astype(BF16).astype(F32)
    shape = (flag_count, step.shape[1])
    right[0:inner_dim, :] = pair_weight[0:inner_dim, :]
    right[inner_dim:inner_dim + flag_count, :] = jnp.broadcast_to(step_high, shape).astype(BF16)
    right[inner_dim + flag_count:, :] = jnp.broadcast_to(step - step_high, shape).astype(BF16)
    minus[0:inner_dim, :] = pair_weight[inner_dim:, :]
    minus[inner_dim:, :] = jnp.zeros((inner_dim, step.shape[1]), BF16)
    bin_rows[...] = jnp.zeros(bin_rows.shape, F32)
    bin_rows[0:bin_count, :] = relpos[...] + chain_table[0:1, :]
    padded = jnp.concatenate(
        [bins[...], jnp.zeros((128 - tok_count, bins.shape[1]), jnp.int32)], axis=0
    )
    return padded.T


def single_kernel(
    plan,
    hidden_hbm, mix_hbm, norm_gain_hbm, norm_bias_hbm, proj_in_hbm, proj_in_bias_hbm,
    proj_out_hbm, proj_out_bias_hbm, tokens_hbm, residue_hbm, pair_gain_hbm, pair_bias_hbm,
    qk_hbm, qk_bias_hbm, chain_hbm, bins_hbm, pair_weight_hbm, relpos_hbm, chain_table_hbm,
    single, query_ref, copies_ref, first, right, minus,
    hidden, mix, norm_gain, norm_bias, proj_in, proj_in_bias, proj_out, proj_out_bias, tokens,
    residue, pair_gain, pair_bias, qk, qk_bias, chain, bins, pair_weight, relpos, chain_table,
    mixture, residue_rows, bin_rows, sem_hidden, sem_in, sem_out, sem_small,
):
    in_pieces, out_pieces = plan
    tok_count = mixture.shape[0]
    inner_dim = qk.shape[1] // 2

    small = [
        (bins_hbm, bins), (relpos_hbm, relpos), (chain_table_hbm, chain_table),
        (pair_weight_hbm, pair_weight), (chain_hbm, chain), (mix_hbm, mix),
        (norm_gain_hbm, norm_gain), (norm_bias_hbm, norm_bias), (tokens_hbm, tokens),
        (residue_hbm, residue), (proj_in_bias_hbm, proj_in_bias),
        (proj_out_bias_hbm, proj_out_bias), (pair_gain_hbm, pair_gain),
        (pair_bias_hbm, pair_bias), (qk_hbm, qk), (qk_bias_hbm, qk_bias),
    ]
    first_small = 6
    small = [
        pltpu.make_async_copy(source, target, sem_small.at[at])
        for at, (source, target) in enumerate(small)
    ]
    states = [
        pltpu.make_async_copy(
            hidden_hbm.at[:, :, pl.ds(low, size)],
            hidden.at[:, :, pl.ds(low, size)],
            sem_hidden.at[at],
        )
        for at, (low, size) in enumerate(in_pieces)
    ]
    firsts = [
        pltpu.make_async_copy(
            proj_in_hbm.at[pl.ds(low, size)], proj_in.at[pl.ds(low, size)], sem_in.at[at]
        )
        for at, (low, size) in enumerate(in_pieces)
    ]
    seconds = [
        pltpu.make_async_copy(
            proj_out_hbm.at[pl.ds(low, size)], proj_out.at[pl.ds(low, size)], sem_out.at[at]
        )
        for at, (low, size) in enumerate(out_pieces)
    ]
    for copy in small[:first_small] + states + small[first_small:]:
        copy.start()
    for copy in firsts + seconds:
        copy.start(priority=1)

    for copy in small[:first_small]:
        copy.wait()
    bins_col = operand_rows(
        bins, pair_weight, relpos, chain_table, bin_rows, right, minus, tok_count
    )
    bin_table = bin_rows[...].astype(BF16)
    lanes = lax.broadcasted_iota(jnp.int32, (bins_col.shape[0], bin_table.shape[0]), 1)
    for row in range(tok_count):
        onehot = jnp.where(bins_col[:, row:row + 1] == lanes, 1.0, 0.0).astype(BF16)
        first[row] = jnp.dot(onehot, bin_table, preferred_element_type=F32)
    flags = chain_flags(chain, tok_count, inner_dim)

    width = mixture.shape[1]
    shift = sums = squares = None
    for at, (low, size) in enumerate(in_pieces):
        states[at].wait()
        total = None
        for state in range(hidden.shape[0]):
            term = mix[state] * hidden[state, :, low:low + size].astype(F32)
            total = term if total is None else total + term
        mixture[:, low:low + size] = total
        if shift is None:
            shift = jnp.mean(total, axis=1, keepdims=True)
        total = total - shift
        for lane in range(0, size, 128):
            part = total[:, lane:lane + 128]
            sums = part if sums is None else sums + part
            squares = part * part if squares is None else squares + part * part
        if at == min(1, len(in_pieces) - 1):
            for copy in small[first_small:]:
                copy.wait()
            for row in range(tok_count):
                residue_rows[pl.ds(row, 1), :] = (
                    residue[pl.ds(tokens[row], 1), :] + proj_out_bias[...]
                )

    offset = jnp.sum(sums, axis=1, keepdims=True) / width
    spread = jnp.sum(squares, axis=1, keepdims=True) / width - offset * offset
    mean = shift + offset
    scale = lax.rsqrt(jnp.maximum(spread, 0.0) + epsilon)
    gain, bias = norm_gain[...].reshape(1, width), norm_bias[...].reshape(1, width)
    total = None
    for at, (low, size) in enumerate(in_pieces):
        span = slice(low, low + size)
        normed = ((mixture[:, span] - mean) * scale * gain[:, span] + bias[:, span]).astype(BF16)
        firsts[at].wait()
        term = jnp.dot(normed, proj_in[pl.ds(low, size), :], preferred_element_type=F32)
        total = term if total is None else total + term
    middle = jnp.maximum(total + proj_in_bias[...], 0.0).astype(BF16)

    total = None
    for at, (low, size) in enumerate(out_pieces):
        seconds[at].wait()
        term = jnp.dot(
            middle[:, low:low + size], proj_out[pl.ds(low, size), :], preferred_element_type=F32
        )
        total = term if total is None else total + term
    single_f = total + residue_rows[...]
    single[...] = single_f.astype(BF16)

    pair_in = row_norm(single_f, pair_gain[...], pair_bias[...]).astype(BF16)
    query_key = jnp.dot(pair_in, qk[...], preferred_element_type=F32) + qk_bias[...]

    front = lax.broadcasted_iota(jnp.int32, flags.shape, 1) < inner_dim
    query_ref[...] = jnp.where(front, query_key, flags).astype(BF16)
    block = jnp.where(front, pltpu.roll(query_key, inner_dim, 1), flags).astype(BF16)
    for peer in range(copies_ref.shape[0]):
        copies_ref[peer] = block


def single_part(device_count, operands):
    (hidden, mix, norm_gain, norm_bias, proj_in, proj_in_bias, proj_out, proj_out_bias, tokens,
     residue, pair_gain, pair_bias, qk, qk_bias, chain, bins, pair_weight, relpos,
     chain_table) = operands
    tok_count, width = hidden.shape[1:]
    channels = proj_out.shape[1]
    lanes = qk.shape[1]
    table_rows = -(-relpos.shape[0] // 128) * 128
    vmem = pl.BlockSpec(memory_space=pltpu.VMEM)
    plan = (pieces(width, 5), pieces(channels, 4))
    args = (
        hidden, mix, norm_gain, norm_bias, proj_in, proj_in_bias[None],
        proj_out, proj_out_bias[None], tokens, residue, pair_gain[None], pair_bias[None],
        qk, qk_bias[None], chain[None], bins, pair_weight, relpos, chain_table,
    )
    args = [pltpu.with_memory_space_constraint(arg, pltpu.HBM) for arg in args]
    in_smem = (1, 8)
    scratch = [
        (pltpu.SMEM if at in in_smem else pltpu.VMEM)(arg.shape, arg.dtype)
        for at, arg in enumerate(args)
    ]
    scratch += [
        pltpu.VMEM((tok_count, width), F32),
        pltpu.VMEM((tok_count, channels), F32),
        pltpu.VMEM((table_rows, pair_weight.shape[1]), F32),
        pltpu.SemaphoreType.DMA((len(plan[0]),)),
        pltpu.SemaphoreType.DMA((len(plan[0]),)),
        pltpu.SemaphoreType.DMA((len(plan[1]),)),
        pltpu.SemaphoreType.DMA((16,)),
    ]
    moved = sum(arg.size * arg.dtype.itemsize for arg in args)
    return pl.pallas_call(
        functools.partial(single_kernel, plan),
        out_shape=(
            jax.ShapeDtypeStruct((tok_count, channels), BF16),
            jax.ShapeDtypeStruct((tok_count, lanes), BF16),
            jax.ShapeDtypeStruct((device_count, tok_count, lanes), BF16),
            jax.ShapeDtypeStruct(bins.shape + pair_weight.shape[1:], F32),
            jax.ShapeDtypeStruct(pair_weight.shape, BF16),
            jax.ShapeDtypeStruct(pair_weight.shape, BF16),
        ),
        in_specs=[pl.BlockSpec(memory_space=pltpu.HBM)] * len(args),
        out_specs=(vmem,) * 6,
        scratch_shapes=scratch,
        compiler_params=pltpu.CompilerParams(vmem_limit_bytes=32 * 2**20),
        cost_estimate=pl.CostEstimate(
            flops=2 * tok_count * channels * (width + channels + lanes),
            bytes_accessed=moved,
            transcendentals=0,
        ),
        name="single_path",
    )(*args)


def pair_kernel(
    blocks, queries, first, right, minus, single, single_hbm, pair_hbm, pair, sem, sem_single
):
    single_copy = pltpu.make_async_copy(single, single_hbm, sem_single)
    single_copy.start()
    keys = jnp.concatenate([blocks[1:].reshape(-1, blocks.shape[2]), blocks[0]], axis=0)
    row_diff = jnp.dot(queries[...], minus[...], preferred_element_type=F32)
    col_diff = jnp.dot(keys, minus[...], preferred_element_type=F32)
    copies = []
    for row in range(first.shape[0]):
        products = keys * queries[row:row + 1, :]
        value = jnp.dot(products, right[...], preferred_element_type=F32)
        value = value + first[row] + (row_diff[row:row + 1, :] - col_diff)
        pair[row] = value.astype(BF16)
        copy = pltpu.make_async_copy(pair.at[row], pair_hbm.at[row], sem.at[row])
        copy.start()
        copies.append(copy)
    for copy in copies:
        copy.wait()
    single_copy.wait()


def pair_part(blocks, queries, first, right, minus, single):
    tok_count = first.shape[0]
    vmem = pl.BlockSpec(memory_space=pltpu.VMEM)
    return pl.pallas_call(
        pair_kernel,
        out_shape=(
            jax.ShapeDtypeStruct(single.shape, BF16),
            jax.ShapeDtypeStruct(first.shape, BF16),
        ),
        in_specs=[vmem] * 6,
        out_specs=(pl.BlockSpec(memory_space=pltpu.HBM),) * 2,
        scratch_shapes=[
            pltpu.VMEM(first.shape, BF16),
            pltpu.SemaphoreType.DMA((tok_count,)),
            pltpu.SemaphoreType.DMA,
        ],
        compiler_params=pltpu.CompilerParams(vmem_limit_bytes=32 * 2**20),
        cost_estimate=pl.CostEstimate(
            flops=2 * first.size * right.shape[0],
            bytes_accessed=6 * first.size,
            transcendentals=0,
        ),
        name="pair_rows",
    )(blocks, queries, first, right, minus, single)


def shards(
    hidden_states,
    layer_mix,
    norm_gain,
    norm_bias,
    proj_in,
    proj_in_bias,
    proj_out,
    proj_out_bias,
    residue_tokens,
    residue_table,
    pair_norm_gain,
    pair_norm_bias,
    qk_weight,
    qk_bias,
    pair_weight,
    relpos_bins,
    relpos_table,
    chain_ids,
    chain_table,
):
    device_count = lax.axis_size("seq")
    single, queries, copies, first, right, minus = single_part(
        device_count,
        (
            hidden_states, layer_mix, norm_gain, norm_bias, proj_in, proj_in_bias, proj_out,
            proj_out_bias, residue_tokens, residue_table, pair_norm_gain, pair_norm_bias,
            qk_weight, qk_bias, chain_ids, relpos_bins, pair_weight, relpos_table, chain_table,
        ),
    )
    order = [device_count - 1] + list(range(device_count - 1))
    blocks = lax.all_to_all(
        copies, "seq", split_axis=0, concat_axis=0, axis_index_groups=[order]
    )
    return pair_part(blocks, queries, first, right, minus, single)


def solution(mesh):
    in_specs = (
        P(None, ("groups", "seq"), None),
        P(),
        P(),
        P(),
        P(),
        P(),
        P(),
        P(),
        P(("groups", "seq")),
        P(),
        P(),
        P(),
        P(),
        P(),
        P(),
        P(("groups", "seq"), None),
        P(),
        P(("groups", "seq")),
        P(),
    )
    out_specs = (P(("groups", "seq"), None), P(("groups", "seq"), None, None))
    return jax.shard_map(shards, mesh=mesh, in_specs=in_specs, out_specs=out_specs, check_vma=False)
```

```python
import functools

import jax
import jax.numpy as jnp
from jax import lax
from jax.experimental import pallas as pl
from jax.experimental.pallas import tpu as pltpu
from jax.sharding import PartitionSpec as P

epsilon = 1e-05
BF16 = jnp.bfloat16
F32 = jnp.float32


def pieces(total, count):
    count = max(1, min(count, total))
    ends = [total * step // count for step in range(count + 1)]
    return [(low, high - low) for low, high in zip(ends[:-1], ends[1:])]


def row_norm(values, gain, bias):
    center = values - jnp.mean(values, axis=-1, keepdims=True)
    spread = jnp.mean(center * center, axis=-1, keepdims=True)
    return center * lax.rsqrt(spread + epsilon) * gain + bias


def chain_flags(chain, tok_count, inner_dim):
    lanes = lax.broadcasted_iota(jnp.int32, (tok_count, 2 * inner_dim), 1)
    flag = lax.rem(lanes, inner_dim // 2).astype(F32)
    square = (tok_count, tok_count)
    own = lax.broadcasted_iota(jnp.int32, square, 0) == lax.broadcasted_iota(jnp.int32, square, 1)
    chain_col = jnp.sum(jnp.where(own, chain[...].astype(F32), 0.0), axis=1, keepdims=True)
    return jnp.where(flag == chain_col, 1.0, 0.0)


def operand_rows(bins, pair_weight, relpos, chain_table, bin_rows, right, minus, tok_count):
    bin_count = relpos.shape[0]
    inner_dim = pair_weight.shape[0] // 2
    flag_count = inner_dim // 2
    step = chain_table[1:2, :] - chain_table[0:1, :]
    step_high = step.astype(BF16).astype(F32)
    shape = (flag_count, step.shape[1])
    right[0:inner_dim, :] = pair_weight[0:inner_dim, :]
    right[inner_dim:inner_dim + flag_count, :] = jnp.broadcast_to(step_high, shape).astype(BF16)
    right[inner_dim + flag_count:, :] = jnp.broadcast_to(step - step_high, shape).astype(BF16)
    minus[0:inner_dim, :] = pair_weight[inner_dim:, :]
    minus[inner_dim:, :] = jnp.zeros((inner_dim, step.shape[1]), BF16)
    bin_rows[...] = jnp.zeros(bin_rows.shape, F32)
    bin_rows[0:bin_count, :] = relpos[...] + chain_table[0:1, :]
    padded = jnp.concatenate(
        [bins[...], jnp.zeros((128 - tok_count, bins.shape[1]), jnp.int32)], axis=0
    )
    return padded.T


def single_kernel(
    plan,
    hidden_hbm, mix_hbm, norm_gain_hbm, norm_bias_hbm, proj_in_hbm, proj_in_bias_hbm,
    proj_out_hbm, proj_out_bias_hbm, tokens_hbm, residue_hbm, pair_gain_hbm, pair_bias_hbm,
    qk_hbm, qk_bias_hbm, chain_hbm, bins_hbm, pair_weight_hbm, relpos_hbm, chain_table_hbm,
    single, query_ref, copies_ref, first, right, minus,
    hidden, mix, norm_gain, norm_bias, proj_in, proj_in_bias, proj_out, proj_out_bias, tokens,
    residue, pair_gain, pair_bias, qk, qk_bias, chain, bins, pair_weight, relpos, chain_table,
    mixture, residue_rows, bin_rows, sem_hidden, sem_in, sem_out, sem_small,
):
    in_pieces, out_pieces = plan
    tok_count = mixture.shape[0]
    inner_dim = qk.shape[1] // 2

    small = [
        (bins_hbm, bins), (relpos_hbm, relpos), (chain_table_hbm, chain_table),
        (pair_weight_hbm, pair_weight), (chain_hbm, chain), (mix_hbm, mix),
        (norm_gain_hbm, norm_gain), (norm_bias_hbm, norm_bias), (tokens_hbm, tokens),
        (residue_hbm, residue), (proj_in_bias_hbm, proj_in_bias),
        (proj_out_bias_hbm, proj_out_bias), (pair_gain_hbm, pair_gain),
        (pair_bias_hbm, pair_bias), (qk_hbm, qk), (qk_bias_hbm, qk_bias),
    ]
    first_small = 6
    small = [
        pltpu.make_async_copy(source, target, sem_small.at[at])
        for at, (source, target) in enumerate(small)
    ]
    states = [
        pltpu.make_async_copy(
            hidden_hbm.at[:, :, pl.ds(low, size)],
            hidden.at[:, :, pl.ds(low, size)],
            sem_hidden.at[at],
        )
        for at, (low, size) in enumerate(in_pieces)
    ]
    firsts = [
        pltpu.make_async_copy(
            proj_in_hbm.at[pl.ds(low, size)], proj_in.at[pl.ds(low, size)], sem_in.at[at]
        )
        for at, (low, size) in enumerate(in_pieces)
    ]
    seconds = [
        pltpu.make_async_copy(
            proj_out_hbm.at[pl.ds(low, size)], proj_out.at[pl.ds(low, size)], sem_out.at[at]
        )
        for at, (low, size) in enumerate(out_pieces)
    ]
    for copy in small[:first_small] + states + small[first_small:]:
        copy.start()
    for copy in firsts + seconds:
        copy.start(priority=1)

    for copy in small[:first_small]:
        copy.wait()
    bins_col = operand_rows(
        bins, pair_weight, relpos, chain_table, bin_rows, right, minus, tok_count
    )
    bin_table = bin_rows[...].astype(BF16)
    lanes = lax.broadcasted_iota(jnp.int32, (bins_col.shape[0], bin_table.shape[0]), 1)
    for row in range(tok_count):
        onehot = jnp.where(bins_col[:, row:row + 1] == lanes, 1.0, 0.0).astype(BF16)
        first[row] = jnp.dot(onehot, bin_table, preferred_element_type=F32)
    flags = chain_flags(chain, tok_count, inner_dim)

    width = mixture.shape[1]
    shift = sums = squares = None
    for at, (low, size) in enumerate(in_pieces):
        states[at].wait()
        total = None
        for state in range(hidden.shape[0]):
            term = mix[state] * hidden[state, :, low:low + size].astype(F32)
            total = term if total is None else total + term
        mixture[:, low:low + size] = total
        if shift is None:
            shift = jnp.mean(total, axis=1, keepdims=True)
        total = total - shift
        for lane in range(0, size, 128):
            part = total[:, lane:lane + 128]
            sums = part if sums is None else sums + part
            squares = part * part if squares is None else squares + part * part
        if at == min(1, len(in_pieces) - 1):
            for copy in small[first_small:]:
                copy.wait()
            for row in range(tok_count):
                residue_rows[pl.ds(row, 1), :] = residue[pl.ds(tokens[row], 1), :]

    offset = jnp.sum(sums, axis=1, keepdims=True) / width
    spread = jnp.sum(squares, axis=1, keepdims=True) / width - offset * offset
    mean = shift + offset
    scale = lax.rsqrt(jnp.maximum(spread, 0.0) + epsilon)
    gain, bias = norm_gain[...].reshape(1, width), norm_bias[...].reshape(1, width)
    total = None
    half = -(-len(in_pieces) // 2)
    for group in (range(0, half), range(half, len(in_pieces))):
        low = in_pieces[group[0]][0]
        size = sum(in_pieces[group[-1]]) - low
        span = slice(low, low + size)
        normed = ((mixture[:, span] - mean) * scale * gain[:, span] + bias[:, span]).astype(BF16)
        for at in group:
            firsts[at].wait()
        term = jnp.dot(normed, proj_in[pl.ds(low, size), :], preferred_element_type=F32)
        total = term if total is None else total + term
    middle = jnp.maximum(total + proj_in_bias[...], 0.0).astype(BF16)

    total = None
    for at, (low, size) in enumerate(out_pieces):
        seconds[at].wait()
        term = jnp.dot(
            middle[:, low:low + size], proj_out[pl.ds(low, size), :], preferred_element_type=F32
        )
        total = term if total is None else total + term
    single_f = total + proj_out_bias[...] + residue_rows[...]
    single[...] = single_f.astype(BF16)

    pair_in = row_norm(single_f, pair_gain[...], pair_bias[...]).astype(BF16)
    query_key = jnp.dot(pair_in, qk[...], preferred_element_type=F32) + qk_bias[...]

    front = lax.broadcasted_iota(jnp.int32, flags.shape, 1) < inner_dim
    query_ref[...] = jnp.where(front, query_key, flags).astype(BF16)
    block = jnp.where(front, pltpu.roll(query_key, inner_dim, 1), flags).astype(BF16)
    for peer in range(copies_ref.shape[0]):
        copies_ref[peer] = block


def single_part(device_count, operands):
    (hidden, mix, norm_gain, norm_bias, proj_in, proj_in_bias, proj_out, proj_out_bias, tokens,
     residue, pair_gain, pair_bias, qk, qk_bias, chain, bins, pair_weight, relpos,
     chain_table) = operands
    tok_count, width = hidden.shape[1:]
    channels = proj_out.shape[1]
    lanes = qk.shape[1]
    table_rows = -(-relpos.shape[0] // 128) * 128
    vmem = pl.BlockSpec(memory_space=pltpu.VMEM)
    plan = (pieces(width, 5), pieces(channels, 1))
    args = (
        hidden, mix, norm_gain, norm_bias, proj_in, proj_in_bias[None],
        proj_out, proj_out_bias[None], tokens, residue, pair_gain[None], pair_bias[None],
        qk, qk_bias[None], chain[None], bins, pair_weight, relpos, chain_table,
    )
    args = [pltpu.with_memory_space_constraint(arg, pltpu.HBM) for arg in args]
    in_smem = (1, 8)
    scratch = [
        (pltpu.SMEM if at in in_smem else pltpu.VMEM)(arg.shape, arg.dtype)
        for at, arg in enumerate(args)
    ]
    scratch += [
        pltpu.VMEM((tok_count, width), F32),
        pltpu.VMEM((tok_count, channels), F32),
        pltpu.VMEM((table_rows, pair_weight.shape[1]), F32),
        pltpu.SemaphoreType.DMA((len(plan[0]),)),
        pltpu.SemaphoreType.DMA((len(plan[0]),)),
        pltpu.SemaphoreType.DMA((len(plan[1]),)),
        pltpu.SemaphoreType.DMA((16,)),
    ]
    moved = sum(arg.size * arg.dtype.itemsize for arg in args)
    return pl.pallas_call(
        functools.partial(single_kernel, plan),
        out_shape=(
            jax.ShapeDtypeStruct((tok_count, channels), BF16),
            jax.ShapeDtypeStruct((tok_count, lanes), BF16),
            jax.ShapeDtypeStruct((device_count, tok_count, lanes), BF16),
            jax.ShapeDtypeStruct(bins.shape + pair_weight.shape[1:], F32),
            jax.ShapeDtypeStruct(pair_weight.shape, BF16),
            jax.ShapeDtypeStruct(pair_weight.shape, BF16),
        ),
        in_specs=[pl.BlockSpec(memory_space=pltpu.HBM)] * len(args),
        out_specs=(vmem,) * 6,
        scratch_shapes=scratch,
        compiler_params=pltpu.CompilerParams(vmem_limit_bytes=32 * 2**20),
        cost_estimate=pl.CostEstimate(
            flops=2 * tok_count * channels * (width + channels + lanes),
            bytes_accessed=moved,
            transcendentals=0,
        ),
        name="single_path",
    )(*args)


def pair_kernel(
    blocks, queries, first, right, minus, single, single_hbm, pair_hbm, pair, sem, sem_single
):
    single_copy = pltpu.make_async_copy(single, single_hbm, sem_single)
    single_copy.start()
    keys = jnp.concatenate([blocks[1:].reshape(-1, blocks.shape[2]), blocks[0]], axis=0)
    row_diff = jnp.dot(queries[...], minus[...], preferred_element_type=F32)
    col_diff = jnp.dot(keys, minus[...], preferred_element_type=F32)
    copies = []
    for row in range(first.shape[0]):
        products = keys * queries[row:row + 1, :]
        value = jnp.dot(products, right[...], preferred_element_type=F32)
        value = value + first[row] + (row_diff[row:row + 1, :] - col_diff)
        pair[row] = value.astype(BF16)
        copy = pltpu.make_async_copy(pair.at[row], pair_hbm.at[row], sem.at[row])
        copy.start()
        copies.append(copy)
    for copy in copies:
        copy.wait()
    single_copy.wait()


def pair_part(blocks, queries, first, right, minus, single):
    tok_count = first.shape[0]
    vmem = pl.BlockSpec(memory_space=pltpu.VMEM)
    return pl.pallas_call(
        pair_kernel,
        out_shape=(
            jax.ShapeDtypeStruct(single.shape, BF16),
            jax.ShapeDtypeStruct(first.shape, BF16),
        ),
        in_specs=[vmem] * 6,
        out_specs=(pl.BlockSpec(memory_space=pltpu.HBM),) * 2,
        scratch_shapes=[
            pltpu.VMEM(first.shape, BF16),
            pltpu.SemaphoreType.DMA((tok_count,)),
            pltpu.SemaphoreType.DMA,
        ],
        compiler_params=pltpu.CompilerParams(vmem_limit_bytes=32 * 2**20),
        cost_estimate=pl.CostEstimate(
            flops=2 * first.size * right.shape[0],
            bytes_accessed=6 * first.size,
            transcendentals=0,
        ),
        name="pair_rows",
    )(blocks, queries, first, right, minus, single)


def shards(
    hidden_states,
    layer_mix,
    norm_gain,
    norm_bias,
    proj_in,
    proj_in_bias,
    proj_out,
    proj_out_bias,
    residue_tokens,
    residue_table,
    pair_norm_gain,
    pair_norm_bias,
    qk_weight,
    qk_bias,
    pair_weight,
    relpos_bins,
    relpos_table,
    chain_ids,
    chain_table,
):
    device_count = lax.axis_size("seq")
    single, queries, copies, first, right, minus = single_part(
        device_count,
        (
            hidden_states, layer_mix, norm_gain, norm_bias, proj_in, proj_in_bias, proj_out,
            proj_out_bias, residue_tokens, residue_table, pair_norm_gain, pair_norm_bias,
            qk_weight, qk_bias, chain_ids, relpos_bins, pair_weight, relpos_table, chain_table,
        ),
    )
    order = [device_count - 1] + list(range(device_count - 1))
    blocks = lax.all_to_all(
        copies, "seq", split_axis=0, concat_axis=0, axis_index_groups=[order]
    )
    return pair_part(blocks, queries, first, right, minus, single)


def solution(mesh):
    in_specs = (
        P(None, ("groups", "seq"), None),
        P(),
        P(),
        P(),
        P(),
        P(),
        P(),
        P(),
        P(("groups", "seq")),
        P(),
        P(),
        P(),
        P(),
        P(),
        P(),
        P(("groups", "seq"), None),
        P(),
        P(("groups", "seq")),
        P(),
    )
    out_specs = (P(("groups", "seq"), None), P(("groups", "seq"), None, None))
    return jax.shard_map(shards, mesh=mesh, in_specs=in_specs, out_specs=out_specs, check_vma=False)
```

```python
import functools

import jax
import jax.numpy as jnp
from jax import lax
from jax.experimental import pallas as pl
from jax.experimental.pallas import tpu as pltpu
from jax.sharding import PartitionSpec as P

epsilon = 1e-05
BF16 = jnp.bfloat16
F32 = jnp.float32


def pieces(total, count):
    count = max(1, min(count, total))
    ends = [total * step // count for step in range(count + 1)]
    return [(low, high - low) for low, high in zip(ends[:-1], ends[1:])]


def row_norm(values, gain, bias):
    center = values - jnp.mean(values, axis=-1, keepdims=True)
    spread = jnp.mean(center * center, axis=-1, keepdims=True)
    return center * lax.rsqrt(spread + epsilon) * gain + bias


def chain_flags(chain, tok_count, inner_dim):
    lanes = lax.broadcasted_iota(jnp.int32, (tok_count, 2 * inner_dim), 1)
    flag = lax.rem(lanes, inner_dim // 2).astype(F32)
    square = (tok_count, tok_count)
    own = lax.broadcasted_iota(jnp.int32, square, 0) == lax.broadcasted_iota(jnp.int32, square, 1)
    chain_col = jnp.sum(jnp.where(own, chain[...].astype(F32), 0.0), axis=1, keepdims=True)
    return jnp.where(flag == chain_col, 1.0, 0.0)


def operand_rows(bins, pair_weight, relpos, chain_table, bin_rows, right, minus, tok_count):
    bin_count = relpos.shape[0]
    inner_dim = pair_weight.shape[0] // 2
    flag_count = inner_dim // 2
    step = chain_table[1:2, :] - chain_table[0:1, :]
    step_high = step.astype(BF16).astype(F32)
    shape = (flag_count, step.shape[1])
    right[0:inner_dim, :] = pair_weight[0:inner_dim, :]
    right[inner_dim:inner_dim + flag_count, :] = jnp.broadcast_to(step_high, shape).astype(BF16)
    right[inner_dim + flag_count:, :] = jnp.broadcast_to(step - step_high, shape).astype(BF16)
    minus[0:inner_dim, :] = pair_weight[inner_dim:, :]
    minus[inner_dim:, :] = jnp.zeros((inner_dim, step.shape[1]), BF16)
    bin_rows[...] = jnp.zeros(bin_rows.shape, F32)
    bin_rows[0:bin_count, :] = relpos[...] + chain_table[0:1, :]
    padded = jnp.concatenate(
        [bins[...], jnp.zeros((128 - tok_count, bins.shape[1]), jnp.int32)], axis=0
    )
    return padded.T


def single_kernel(
    plan,
    hidden_hbm, mix_hbm, norm_gain_hbm, norm_bias_hbm, proj_in_hbm, proj_in_bias_hbm,
    proj_out_hbm, proj_out_bias_hbm, tokens_hbm, residue_hbm, pair_gain_hbm, pair_bias_hbm,
    qk_hbm, qk_bias_hbm, chain_hbm, bins_hbm, pair_weight_hbm, relpos_hbm, chain_table_hbm,
    single, query_ref, copies_ref, first, right, minus,
    hidden, mix, norm_gain, norm_bias, proj_in, proj_in_bias, proj_out, proj_out_bias, tokens,
    residue, pair_gain, pair_bias, qk, qk_bias, chain, bins, pair_weight, relpos, chain_table,
    mixture, normed, residue_rows, bin_rows, sem_hidden, sem_in, sem_out, sem_small,
):
    in_pieces, out_pieces = plan
    tok_count = mixture.shape[0]
    inner_dim = qk.shape[1] // 2

    small = [
        (bins_hbm, bins), (relpos_hbm, relpos), (chain_table_hbm, chain_table),
        (pair_weight_hbm, pair_weight), (chain_hbm, chain), (mix_hbm, mix),
        (norm_gain_hbm, norm_gain), (norm_bias_hbm, norm_bias), (tokens_hbm, tokens),
        (residue_hbm, residue), (proj_in_bias_hbm, proj_in_bias),
        (proj_out_bias_hbm, proj_out_bias), (pair_gain_hbm, pair_gain),
        (pair_bias_hbm, pair_bias), (qk_hbm, qk), (qk_bias_hbm, qk_bias),
    ]
    first_small = 6
    small = [
        pltpu.make_async_copy(source, target, sem_small.at[at])
        for at, (source, target) in enumerate(small)
    ]
    states = [
        pltpu.make_async_copy(
            hidden_hbm.at[:, :, pl.ds(low, size)],
            hidden.at[:, :, pl.ds(low, size)],
            sem_hidden.at[at],
        )
        for at, (low, size) in enumerate(in_pieces)
    ]
    firsts = [
        pltpu.make_async_copy(
            proj_in_hbm.at[pl.ds(low, size)], proj_in.at[pl.ds(low, size)], sem_in.at[at]
        )
        for at, (low, size) in enumerate(in_pieces)
    ]
    seconds = [
        pltpu.make_async_copy(
            proj_out_hbm.at[pl.ds(low, size)], proj_out.at[pl.ds(low, size)], sem_out.at[at]
        )
        for at, (low, size) in enumerate(out_pieces)
    ]
    for copy in small[:first_small] + states + small[first_small:]:
        copy.start()
    for copy in firsts + seconds:
        copy.start(priority=1)

    for copy in small[:first_small]:
        copy.wait()
    bins_col = operand_rows(
        bins, pair_weight, relpos, chain_table, bin_rows, right, minus, tok_count
    )
    bin_table = bin_rows[...].astype(BF16)
    lanes = lax.broadcasted_iota(jnp.int32, (bins_col.shape[0], bin_table.shape[0]), 1)
    for row in range(tok_count):
        onehot = jnp.where(bins_col[:, row:row + 1] == lanes, 1.0, 0.0).astype(BF16)
        first[row] = jnp.dot(onehot, bin_table, preferred_element_type=F32)
    flags = chain_flags(chain, tok_count, inner_dim)

    width = mixture.shape[1]
    count, size = len(in_pieces), in_pieces[0][1]

    def mixed(low):
        total = None
        for state in range(hidden.shape[0]):
            term = mix[state] * hidden[state, :, pl.ds(low, size)].astype(F32)
            total = term if total is None else total + term
        mixture[:, pl.ds(low, size)] = total
        return total

    def sums_of(values):
        parts = [values[:, lane:lane + 128] for lane in range(0, size, 128)]
        return sum(parts[1:], parts[0]), sum([part * part for part in parts[1:]], parts[0] ** 2)

    states[0].wait()
    total = mixed(0)
    shift = jnp.mean(total, axis=1, keepdims=True)
    first_sums = sums_of(total - shift)
    for copy in small[first_small:]:
        copy.wait()
    for row in range(tok_count):
        residue_rows[pl.ds(row, 1), :] = residue[pl.ds(tokens[row], 1), :]

    def mixture_step(at, carry):
        low = pl.multiple_of(at * size, size)
        columns = pl.ds(low, size)
        pltpu.make_async_copy(
            hidden_hbm.at[:, :, columns], hidden.at[:, :, columns], sem_hidden.at[at]
        ).wait()
        sums, squares = sums_of(mixed(low) - shift)
        return carry[0] + sums, carry[1] + squares

    sums, squares = lax.fori_loop(1, count, mixture_step, first_sums)
    offset = jnp.sum(sums, axis=1, keepdims=True) / width
    spread = jnp.sum(squares, axis=1, keepdims=True) / width - offset * offset
    mean = shift + offset
    scale = lax.rsqrt(jnp.maximum(spread, 0.0) + epsilon)
    gain, bias = norm_gain[...].reshape(1, width), norm_bias[...].reshape(1, width)
    normed[...] = ((mixture[...] - mean) * scale * gain + bias).astype(BF16)

    def product_step(at, total):
        low = pl.multiple_of(at * size, size)
        rows = pl.ds(low, size)
        pltpu.make_async_copy(proj_in_hbm.at[rows], proj_in.at[rows], sem_in.at[at]).wait()
        return total + jnp.dot(normed[:, rows], proj_in[rows, :], preferred_element_type=F32)

    total = lax.fori_loop(
        0, count, product_step, jnp.zeros((tok_count, proj_in.shape[1]), F32)
    )
    middle = jnp.maximum(total + proj_in_bias[...], 0.0).astype(BF16)

    total = None
    for at, (low, size) in enumerate(out_pieces):
        seconds[at].wait()
        term = jnp.dot(
            middle[:, low:low + size], proj_out[pl.ds(low, size), :], preferred_element_type=F32
        )
        total = term if total is None else total + term
    single_f = total + proj_out_bias[...] + residue_rows[...]
    single[...] = single_f.astype(BF16)

    pair_in = row_norm(single_f, pair_gain[...], pair_bias[...]).astype(BF16)
    query_key = jnp.dot(pair_in, qk[...], preferred_element_type=F32) + qk_bias[...]

    front = lax.broadcasted_iota(jnp.int32, flags.shape, 1) < inner_dim
    query_ref[...] = jnp.where(front, query_key, flags).astype(BF16)
    block = jnp.where(front, pltpu.roll(query_key, inner_dim, 1), flags).astype(BF16)
    for peer in range(copies_ref.shape[0]):
        copies_ref[peer] = block


def single_part(device_count, operands):
    (hidden, mix, norm_gain, norm_bias, proj_in, proj_in_bias, proj_out, proj_out_bias, tokens,
     residue, pair_gain, pair_bias, qk, qk_bias, chain, bins, pair_weight, relpos,
     chain_table) = operands
    tok_count, width = hidden.shape[1:]
    channels = proj_out.shape[1]
    lanes = qk.shape[1]
    table_rows = -(-relpos.shape[0] // 128) * 128
    vmem = pl.BlockSpec(memory_space=pltpu.VMEM)
    plan = (pieces(width, 5 if width % (5 * 128) == 0 else 1), pieces(channels, 2))
    args = (
        hidden, mix, norm_gain, norm_bias, proj_in, proj_in_bias[None],
        proj_out, proj_out_bias[None], tokens, residue, pair_gain[None], pair_bias[None],
        qk, qk_bias[None], chain[None], bins, pair_weight, relpos, chain_table,
    )
    args = [pltpu.with_memory_space_constraint(arg, pltpu.HBM) for arg in args]
    in_smem = (1, 8)
    scratch = [
        (pltpu.SMEM if at in in_smem else pltpu.VMEM)(arg.shape, arg.dtype)
        for at, arg in enumerate(args)
    ]
    scratch += [
        pltpu.VMEM((tok_count, width), F32),
        pltpu.VMEM((tok_count, width), BF16),
        pltpu.VMEM((tok_count, channels), F32),
        pltpu.VMEM((table_rows, pair_weight.shape[1]), F32),
        pltpu.SemaphoreType.DMA((len(plan[0]),)),
        pltpu.SemaphoreType.DMA((len(plan[0]),)),
        pltpu.SemaphoreType.DMA((len(plan[1]),)),
        pltpu.SemaphoreType.DMA((16,)),
    ]
    moved = sum(arg.size * arg.dtype.itemsize for arg in args)
    return pl.pallas_call(
        functools.partial(single_kernel, plan),
        out_shape=(
            jax.ShapeDtypeStruct((tok_count, channels), BF16),
            jax.ShapeDtypeStruct((tok_count, lanes), BF16),
            jax.ShapeDtypeStruct((device_count, tok_count, lanes), BF16),
            jax.ShapeDtypeStruct(bins.shape + pair_weight.shape[1:], F32),
            jax.ShapeDtypeStruct(pair_weight.shape, BF16),
            jax.ShapeDtypeStruct(pair_weight.shape, BF16),
        ),
        in_specs=[pl.BlockSpec(memory_space=pltpu.HBM)] * len(args),
        out_specs=(vmem,) * 6,
        scratch_shapes=scratch,
        compiler_params=pltpu.CompilerParams(vmem_limit_bytes=32 * 2**20),
        cost_estimate=pl.CostEstimate(
            flops=2 * tok_count * channels * (width + channels + lanes),
            bytes_accessed=moved,
            transcendentals=0,
        ),
        name="single_path",
    )(*args)


def pair_kernel(
    blocks, queries, first, right, minus, single, single_hbm, pair_hbm, pair, sem, sem_single
):
    single_copy = pltpu.make_async_copy(single, single_hbm, sem_single)
    single_copy.start()
    keys = jnp.concatenate([blocks[1:].reshape(-1, blocks.shape[2]), blocks[0]], axis=0)
    row_diff = jnp.dot(queries[...], minus[...], preferred_element_type=F32)
    col_diff = jnp.dot(keys, minus[...], preferred_element_type=F32)
    copies = []
    for row in range(first.shape[0]):
        products = keys * queries[row:row + 1, :]
        value = jnp.dot(products, right[...], preferred_element_type=F32)
        value = value + first[row] + (row_diff[row:row + 1, :] - col_diff)
        pair[row] = value.astype(BF16)
        copy = pltpu.make_async_copy(pair.at[row], pair_hbm.at[row], sem.at[row])
        copy.start()
        copies.append(copy)
    for copy in copies:
        copy.wait()
    single_copy.wait()


def pair_part(blocks, queries, first, right, minus, single):
    tok_count = first.shape[0]
    vmem = pl.BlockSpec(memory_space=pltpu.VMEM)
    return pl.pallas_call(
        pair_kernel,
        out_shape=(
            jax.ShapeDtypeStruct(single.shape, BF16),
            jax.ShapeDtypeStruct(first.shape, BF16),
        ),
        in_specs=[vmem] * 6,
        out_specs=(pl.BlockSpec(memory_space=pltpu.HBM),) * 2,
        scratch_shapes=[
            pltpu.VMEM(first.shape, BF16),
            pltpu.SemaphoreType.DMA((tok_count,)),
            pltpu.SemaphoreType.DMA,
        ],
        compiler_params=pltpu.CompilerParams(vmem_limit_bytes=32 * 2**20),
        cost_estimate=pl.CostEstimate(
            flops=2 * first.size * right.shape[0],
            bytes_accessed=6 * first.size,
            transcendentals=0,
        ),
        name="pair_rows",
    )(blocks, queries, first, right, minus, single)


def shards(
    hidden_states,
    layer_mix,
    norm_gain,
    norm_bias,
    proj_in,
    proj_in_bias,
    proj_out,
    proj_out_bias,
    residue_tokens,
    residue_table,
    pair_norm_gain,
    pair_norm_bias,
    qk_weight,
    qk_bias,
    pair_weight,
    relpos_bins,
    relpos_table,
    chain_ids,
    chain_table,
):
    device_count = lax.axis_size("seq")
    single, queries, copies, first, right, minus = single_part(
        device_count,
        (
            hidden_states, layer_mix, norm_gain, norm_bias, proj_in, proj_in_bias, proj_out,
            proj_out_bias, residue_tokens, residue_table, pair_norm_gain, pair_norm_bias,
            qk_weight, qk_bias, chain_ids, relpos_bins, pair_weight, relpos_table, chain_table,
        ),
    )
    order = [device_count - 1] + list(range(device_count - 1))
    blocks = lax.all_to_all(
        copies, "seq", split_axis=0, concat_axis=0, axis_index_groups=[order]
    )
    return pair_part(blocks, queries, first, right, minus, single)


def solution(mesh):
    in_specs = (
        P(None, ("groups", "seq"), None),
        P(),
        P(),
        P(),
        P(),
        P(),
        P(),
        P(),
        P(("groups", "seq")),
        P(),
        P(),
        P(),
        P(),
        P(),
        P(),
        P(("groups", "seq"), None),
        P(),
        P(("groups", "seq")),
        P(),
    )
    out_specs = (P(("groups", "seq"), None), P(("groups", "seq"), None, None))
    return jax.shard_map(shards, mesh=mesh, in_specs=in_specs, out_specs=out_specs, check_vma=False)
```

```python
import functools

import jax
import jax.numpy as jnp
from jax import lax
from jax.experimental import pallas as pl
from jax.experimental.pallas import tpu as pltpu
from jax.sharding import PartitionSpec as P

epsilon = 1e-05
BF16 = jnp.bfloat16
F32 = jnp.float32


def pieces(total, count):
    count = max(1, min(count, total))
    ends = [total * step // count for step in range(count + 1)]
    return [(low, high - low) for low, high in zip(ends[:-1], ends[1:])]


def row_norm(values, gain, bias):
    center = values - jnp.mean(values, axis=-1, keepdims=True)
    spread = jnp.mean(center * center, axis=-1, keepdims=True)
    return center * lax.rsqrt(spread + epsilon) * gain + bias


def chain_flags(chain, tok_count, inner_dim):
    lanes = lax.broadcasted_iota(jnp.int32, (tok_count, 2 * inner_dim), 1)
    flag = lax.rem(lanes, inner_dim // 2).astype(F32)
    square = (tok_count, tok_count)
    own = lax.broadcasted_iota(jnp.int32, square, 0) == lax.broadcasted_iota(jnp.int32, square, 1)
    chain_col = jnp.sum(jnp.where(own, chain[...].astype(F32), 0.0), axis=1, keepdims=True)
    return jnp.where(flag == chain_col, 1.0, 0.0)


def operand_rows(bins, pair_weight, relpos, chain_table, bin_rows, right, minus, tok_count):
    bin_count = relpos.shape[0]
    inner_dim = pair_weight.shape[0] // 2
    flag_count = inner_dim // 2
    step = chain_table[1:2, :] - chain_table[0:1, :]
    step_high = step.astype(BF16).astype(F32)
    shape = (flag_count, step.shape[1])
    right[0:inner_dim, :] = pair_weight[0:inner_dim, :]
    right[inner_dim:inner_dim + flag_count, :] = jnp.broadcast_to(step_high, shape).astype(BF16)
    right[inner_dim + flag_count:, :] = jnp.broadcast_to(step - step_high, shape).astype(BF16)
    minus[0:inner_dim, :] = pair_weight[inner_dim:, :]
    minus[inner_dim:, :] = jnp.zeros((inner_dim, step.shape[1]), BF16)
    bin_rows[...] = jnp.zeros(bin_rows.shape, F32)
    bin_rows[0:bin_count, :] = relpos[...] + chain_table[0:1, :]
    padded = jnp.concatenate(
        [bins[...], jnp.zeros((128 - tok_count, bins.shape[1]), jnp.int32)], axis=0
    )
    return padded.T


def single_kernel(
    plan,
    hidden_hbm, mix_hbm, norm_gain_hbm, norm_bias_hbm, proj_in_hbm, proj_in_bias_hbm,
    proj_out_hbm, proj_out_bias_hbm, tokens_hbm, residue_hbm, pair_gain_hbm, pair_bias_hbm,
    qk_hbm, qk_bias_hbm, chain_hbm, bins_hbm, pair_weight_hbm, relpos_hbm, chain_table_hbm,
    single, query_ref, copies_ref, first, right, minus,
    hidden, mix, norm_gain, norm_bias, proj_in, proj_in_bias, proj_out, proj_out_bias, tokens,
    residue, pair_gain, pair_bias, qk, qk_bias, chain, bins, pair_weight, relpos, chain_table,
    mixture, residue_rows, bin_rows, sem_hidden, sem_in, sem_out, sem_small,
):
    in_pieces, out_pieces = plan
    tok_count = mixture.shape[0]
    inner_dim = qk.shape[1] // 2

    small = [
        (bins_hbm, bins), (relpos_hbm, relpos), (chain_table_hbm, chain_table),
        (pair_weight_hbm, pair_weight), (chain_hbm, chain), (mix_hbm, mix),
        (norm_gain_hbm, norm_gain), (norm_bias_hbm, norm_bias), (tokens_hbm, tokens),
        (residue_hbm, residue), (proj_in_bias_hbm, proj_in_bias),
        (proj_out_bias_hbm, proj_out_bias), (pair_gain_hbm, pair_gain),
        (pair_bias_hbm, pair_bias), (qk_hbm, qk), (qk_bias_hbm, qk_bias),
    ]
    first_small = 6
    small = [
        pltpu.make_async_copy(source, target, sem_small.at[at])
        for at, (source, target) in enumerate(small)
    ]
    states = [
        pltpu.make_async_copy(
            hidden_hbm.at[:, :, pl.ds(low, size)],
            hidden.at[:, :, pl.ds(low, size)],
            sem_hidden.at[at],
        )
        for at, (low, size) in enumerate(in_pieces)
    ]
    firsts = [
        pltpu.make_async_copy(
            proj_in_hbm.at[pl.ds(low, size)], proj_in.at[pl.ds(low, size)], sem_in.at[at]
        )
        for at, (low, size) in enumerate(in_pieces)
    ]
    seconds = [
        pltpu.make_async_copy(
            proj_out_hbm.at[pl.ds(low, size)], proj_out.at[pl.ds(low, size)], sem_out.at[at]
        )
        for at, (low, size) in enumerate(out_pieces)
    ]
    for copy in small[:first_small] + states + small[first_small:]:
        copy.start()
    for copy in firsts + seconds:
        copy.start(priority=1)

    for copy in small[:first_small]:
        copy.wait()
    bins_col = operand_rows(
        bins, pair_weight, relpos, chain_table, bin_rows, right, minus, tok_count
    )
    bin_table = bin_rows[...].astype(BF16)
    lanes = lax.broadcasted_iota(jnp.int32, (bins_col.shape[0], bin_table.shape[0]), 1)
    for row in range(tok_count):
        onehot = jnp.where(bins_col[:, row:row + 1] == lanes, 1.0, 0.0).astype(BF16)
        first[row] = jnp.dot(onehot, bin_table, preferred_element_type=F32)
    flags = chain_flags(chain, tok_count, inner_dim)

    width = mixture.shape[1]
    shift = sums = squares = None
    for at, (low, size) in enumerate(in_pieces):
        states[at].wait()
        total = None
        for state in range(hidden.shape[0]):
            term = mix[state] * hidden[state, :, low:low + size].astype(F32)
            total = term if total is None else total + term
        mixture[:, low:low + size] = total
        if shift is None:
            shift = jnp.mean(total, axis=1, keepdims=True)
        total = total - shift
        for lane in range(0, size, 128):
            part = total[:, lane:lane + 128]
            sums = part if sums is None else sums + part
            squares = part * part if squares is None else squares + part * part
        if at == min(1, len(in_pieces) - 1):
            for copy in small[first_small:]:
                copy.wait()
            for row in range(tok_count):
                residue_rows[pl.ds(row, 1), :] = residue[pl.ds(tokens[row], 1), :]

    offset = jnp.sum(sums, axis=1, keepdims=True) / width
    spread = jnp.sum(squares, axis=1, keepdims=True) / width - offset * offset
    mean = shift + offset
    scale = lax.rsqrt(jnp.maximum(spread, 0.0) + epsilon)
    gain, bias = norm_gain[...].reshape(1, width), norm_bias[...].reshape(1, width)
    total = None
    for at, (low, size) in enumerate(in_pieces):
        span = slice(low, low + size)
        normed = ((mixture[:, span] - mean) * scale * gain[:, span] + bias[:, span]).astype(BF16)
        firsts[at].wait()
        term = jnp.dot(normed, proj_in[pl.ds(low, size), :], preferred_element_type=F32)
        total = term if total is None else total + term
    middle = jnp.maximum(total + proj_in_bias[...], 0.0).astype(BF16)

    total = None
    for at, (low, size) in enumerate(out_pieces):
        seconds[at].wait()
        term = jnp.dot(
            middle[:, low:low + size], proj_out[pl.ds(low, size), :], preferred_element_type=F32
        )
        total = term if total is None else total + term
    single_f = total + proj_out_bias[...] + residue_rows[...]
    single[...] = single_f.astype(BF16)

    pair_in = row_norm(single_f, pair_gain[...], pair_bias[...]).astype(BF16)
    query_key = jnp.dot(pair_in, qk[...], preferred_element_type=F32) + qk_bias[...]

    front = lax.broadcasted_iota(jnp.int32, flags.shape, 1) < inner_dim
    query_ref[...] = jnp.where(front, query_key, flags).astype(BF16)
    block = jnp.where(front, pltpu.roll(query_key, inner_dim, 1), flags).astype(BF16)
    for peer in range(copies_ref.shape[0]):
        copies_ref[peer] = block


def single_part(device_count, operands):
    (hidden, mix, norm_gain, norm_bias, proj_in, proj_in_bias, proj_out, proj_out_bias, tokens,
     residue, pair_gain, pair_bias, qk, qk_bias, chain, bins, pair_weight, relpos,
     chain_table) = operands
    tok_count, width = hidden.shape[1:]
    channels = proj_out.shape[1]
    lanes = qk.shape[1]
    table_rows = -(-relpos.shape[0] // 128) * 128
    vmem = pl.BlockSpec(memory_space=pltpu.VMEM)
    plan = (pieces(width, 5), pieces(channels, 2))
    args = (
        hidden, mix, norm_gain, norm_bias, proj_in, proj_in_bias[None],
        proj_out, proj_out_bias[None], tokens, residue, pair_gain[None], pair_bias[None],
        qk, qk_bias[None], chain[None], bins, pair_weight, relpos, chain_table,
    )
    args = [pltpu.with_memory_space_constraint(arg, pltpu.HBM) for arg in args]
    in_smem = (1, 8)
    scratch = [
        (pltpu.SMEM if at in in_smem else pltpu.VMEM)(arg.shape, arg.dtype)
        for at, arg in enumerate(args)
    ]
    scratch += [
        pltpu.VMEM((tok_count, width), F32),
        pltpu.VMEM((tok_count, channels), F32),
        pltpu.VMEM((table_rows, pair_weight.shape[1]), F32),
        pltpu.SemaphoreType.DMA((len(plan[0]),)),
        pltpu.SemaphoreType.DMA((len(plan[0]),)),
        pltpu.SemaphoreType.DMA((len(plan[1]),)),
        pltpu.SemaphoreType.DMA((16,)),
    ]
    moved = sum(arg.size * arg.dtype.itemsize for arg in args)
    return pl.pallas_call(
        functools.partial(single_kernel, plan),
        out_shape=(
            jax.ShapeDtypeStruct((tok_count, channels), BF16),
            jax.ShapeDtypeStruct((tok_count, lanes), BF16),
            jax.ShapeDtypeStruct((device_count, tok_count, lanes), BF16),
            jax.ShapeDtypeStruct(bins.shape + pair_weight.shape[1:], F32),
            jax.ShapeDtypeStruct(pair_weight.shape, BF16),
            jax.ShapeDtypeStruct(pair_weight.shape, BF16),
        ),
        in_specs=[pl.BlockSpec(memory_space=pltpu.HBM)] * len(args),
        out_specs=(vmem,) * 6,
        scratch_shapes=scratch,
        compiler_params=pltpu.CompilerParams(vmem_limit_bytes=32 * 2**20),
        cost_estimate=pl.CostEstimate(
            flops=2 * tok_count * channels * (width + channels + lanes),
            bytes_accessed=moved,
            transcendentals=0,
        ),
        name="single_path",
    )(*args)


def pair_kernel(
    blocks, queries, first, right, minus, single, single_hbm, pair_hbm, pair, sem, sem_single
):
    single_copy = pltpu.make_async_copy(single, single_hbm, sem_single)
    single_copy.start()
    last = blocks.shape[0] - 1
    keys = jnp.concatenate(
        [blocks[1:last].reshape(-1, blocks.shape[2]), blocks[0], blocks[last]], axis=0
    )
    row_diff = jnp.dot(queries[...], minus[...], preferred_element_type=F32)
    col_diff = jnp.dot(keys, minus[...], preferred_element_type=F32)
    copies = []
    for row in range(first.shape[0]):
        products = keys * queries[row:row + 1, :]
        value = jnp.dot(products, right[...], preferred_element_type=F32)
        value = value + first[row] + (row_diff[row:row + 1, :] - col_diff)
        pair[row] = value.astype(BF16)
        copy = pltpu.make_async_copy(pair.at[row], pair_hbm.at[row], sem.at[row])
        copy.start()
        copies.append(copy)
    for copy in copies:
        copy.wait()
    single_copy.wait()


def pair_part(blocks, queries, first, right, minus, single):
    tok_count = first.shape[0]
    vmem = pl.BlockSpec(memory_space=pltpu.VMEM)
    return pl.pallas_call(
        pair_kernel,
        out_shape=(
            jax.ShapeDtypeStruct(single.shape, BF16),
            jax.ShapeDtypeStruct(first.shape, BF16),
        ),
        in_specs=[vmem] * 6,
        out_specs=(pl.BlockSpec(memory_space=pltpu.HBM),) * 2,
        scratch_shapes=[
            pltpu.VMEM(first.shape, BF16),
            pltpu.SemaphoreType.DMA((tok_count,)),
            pltpu.SemaphoreType.DMA,
        ],
        compiler_params=pltpu.CompilerParams(vmem_limit_bytes=32 * 2**20),
        cost_estimate=pl.CostEstimate(
            flops=2 * first.size * right.shape[0],
            bytes_accessed=6 * first.size,
            transcendentals=0,
        ),
        name="pair_rows",
    )(blocks, queries, first, right, minus, single)


def shards(
    hidden_states,
    layer_mix,
    norm_gain,
    norm_bias,
    proj_in,
    proj_in_bias,
    proj_out,
    proj_out_bias,
    residue_tokens,
    residue_table,
    pair_norm_gain,
    pair_norm_bias,
    qk_weight,
    qk_bias,
    pair_weight,
    relpos_bins,
    relpos_table,
    chain_ids,
    chain_table,
):
    device_count = lax.axis_size("seq")
    single, queries, copies, first, right, minus = single_part(
        device_count,
        (
            hidden_states, layer_mix, norm_gain, norm_bias, proj_in, proj_in_bias, proj_out,
            proj_out_bias, residue_tokens, residue_table, pair_norm_gain, pair_norm_bias,
            qk_weight, qk_bias, chain_ids, relpos_bins, pair_weight, relpos_table, chain_table,
        ),
    )
    order = [device_count - 2] + list(range(device_count - 2)) + [device_count - 1]
    blocks = lax.all_to_all(
        copies, "seq", split_axis=0, concat_axis=0, axis_index_groups=[order]
    )
    return pair_part(blocks, queries, first, right, minus, single)


def solution(mesh):
    in_specs = (
        P(None, ("groups", "seq"), None),
        P(),
        P(),
        P(),
        P(),
        P(),
        P(),
        P(),
        P(("groups", "seq")),
        P(),
        P(),
        P(),
        P(),
        P(),
        P(),
        P(("groups", "seq"), None),
        P(),
        P(("groups", "seq")),
        P(),
    )
    out_specs = (P(("groups", "seq"), None), P(("groups", "seq"), None, None))
    return jax.shard_map(shards, mesh=mesh, in_specs=in_specs, out_specs=out_specs, check_vma=False)
```

```python
import functools

import jax
import jax.numpy as jnp
from jax import lax
from jax.experimental import pallas as pl
from jax.experimental.pallas import tpu as pltpu
from jax.sharding import PartitionSpec as P

epsilon = 1e-05
BF16 = jnp.bfloat16
F32 = jnp.float32


def pieces(total, count):
    count = max(1, min(count, total))
    ends = [total * step // count for step in range(count + 1)]
    return [(low, high - low) for low, high in zip(ends[:-1], ends[1:])]


def row_norm(values, gain, bias):
    center = values - jnp.mean(values, axis=-1, keepdims=True)
    spread = jnp.mean(center * center, axis=-1, keepdims=True)
    return center * lax.rsqrt(spread + epsilon) * gain + bias


def chain_flags(chain, tok_count, inner_dim):
    lanes = lax.broadcasted_iota(jnp.int32, (tok_count, 2 * inner_dim), 1)
    flag = lax.rem(lanes, inner_dim // 2).astype(F32)
    square = (tok_count, tok_count)
    own = lax.broadcasted_iota(jnp.int32, square, 0) == lax.broadcasted_iota(jnp.int32, square, 1)
    chain_col = jnp.sum(jnp.where(own, chain[...].astype(F32), 0.0), axis=1, keepdims=True)
    return jnp.where(flag == chain_col, 1.0, 0.0)


def operand_rows(bins, pair_weight, relpos, chain_table, bin_rows, right, minus, tok_count):
    bin_count = relpos.shape[0]
    inner_dim = pair_weight.shape[0] // 2
    flag_count = inner_dim // 2
    step = chain_table[1:2, :] - chain_table[0:1, :]
    step_high = step.astype(BF16).astype(F32)
    shape = (flag_count, step.shape[1])
    right[0:inner_dim, :] = pair_weight[0:inner_dim, :]
    right[inner_dim:inner_dim + flag_count, :] = jnp.broadcast_to(step_high, shape).astype(BF16)
    right[inner_dim + flag_count:, :] = jnp.broadcast_to(step - step_high, shape).astype(BF16)
    minus[0:inner_dim, :] = pair_weight[inner_dim:, :]
    minus[inner_dim:, :] = jnp.zeros((inner_dim, step.shape[1]), BF16)
    bin_rows[...] = jnp.zeros(bin_rows.shape, F32)
    bin_rows[0:bin_count, :] = relpos[...] + chain_table[0:1, :]
    padded = jnp.concatenate(
        [bins[...], jnp.zeros((128 - tok_count, bins.shape[1]), jnp.int32)], axis=0
    )
    return padded.T


def single_kernel(
    plan,
    hidden_hbm, mix_hbm, norm_gain_hbm, norm_bias_hbm, proj_in_hbm, proj_in_bias_hbm,
    proj_out_hbm, proj_out_bias_hbm, tokens_hbm, residue_hbm, pair_gain_hbm, pair_bias_hbm,
    qk_hbm, qk_bias_hbm, chain_hbm, bins_hbm, pair_weight_hbm, relpos_hbm, chain_table_hbm,
    single, query_ref, copies_ref, first, right, minus,
    hidden, mix, norm_gain, norm_bias, proj_in, proj_in_bias, proj_out, proj_out_bias, tokens,
    residue, pair_gain, pair_bias, qk, qk_bias, chain, bins, pair_weight, relpos, chain_table,
    mixture, residue_rows, bin_rows, sem_hidden, sem_in, sem_out, sem_small,
):
    in_pieces, out_pieces = plan
    tok_count = mixture.shape[0]
    inner_dim = qk.shape[1] // 2

    small = [
        (bins_hbm, bins), (relpos_hbm, relpos), (chain_table_hbm, chain_table),
        (pair_weight_hbm, pair_weight), (chain_hbm, chain), (mix_hbm, mix),
        (norm_gain_hbm, norm_gain), (norm_bias_hbm, norm_bias), (tokens_hbm, tokens),
        (residue_hbm, residue), (proj_in_bias_hbm, proj_in_bias),
        (proj_out_bias_hbm, proj_out_bias), (pair_gain_hbm, pair_gain),
        (pair_bias_hbm, pair_bias), (qk_hbm, qk), (qk_bias_hbm, qk_bias),
    ]
    first_small = 6
    small = [
        pltpu.make_async_copy(source, target, sem_small.at[at])
        for at, (source, target) in enumerate(small)
    ]
    states = [
        pltpu.make_async_copy(
            hidden_hbm.at[:, :, pl.ds(low, size)],
            hidden.at[:, :, pl.ds(low, size)],
            sem_hidden.at[at],
        )
        for at, (low, size) in enumerate(in_pieces)
    ]
    firsts = [
        pltpu.make_async_copy(
            proj_in_hbm.at[pl.ds(low, size)], proj_in.at[pl.ds(low, size)], sem_in.at[at]
        )
        for at, (low, size) in enumerate(in_pieces)
    ]
    seconds = [
        pltpu.make_async_copy(
            proj_out_hbm.at[pl.ds(low, size)], proj_out.at[pl.ds(low, size)], sem_out.at[at]
        )
        for at, (low, size) in enumerate(out_pieces)
    ]
    for copy in small[:first_small] + states + small[first_small:]:
        copy.start()
    for copy in firsts + seconds:
        copy.start(priority=1)

    for copy in small[:first_small]:
        copy.wait()
    bins_col = operand_rows(
        bins, pair_weight, relpos, chain_table, bin_rows, right, minus, tok_count
    )
    bin_table = bin_rows[...].astype(BF16)
    lanes = lax.broadcasted_iota(jnp.int32, (bins_col.shape[0], bin_table.shape[0]), 1)
    for row in range(tok_count):
        onehot = jnp.where(bins_col[:, row:row + 1] == lanes, 1.0, 0.0).astype(BF16)
        first[row] = jnp.dot(onehot, bin_table, preferred_element_type=F32)
    flags = chain_flags(chain, tok_count, inner_dim)

    width = mixture.shape[1]
    shift = sums = squares = None
    for at, (low, size) in enumerate(in_pieces):
        states[at].wait()
        total = None
        for state in range(hidden.shape[0]):
            term = mix[state] * hidden[state, :, low:low + size].astype(F32)
            total = term if total is None else total + term
        mixture[:, low:low + size] = total
        if shift is None:
            shift = jnp.mean(total, axis=1, keepdims=True)
        total = total - shift
        for lane in range(0, size, 128):
            part = total[:, lane:lane + 128]
            sums = part if sums is None else sums + part
            squares = part * part if squares is None else squares + part * part
        if at == min(1, len(in_pieces) - 1):
            for copy in small[first_small:]:
                copy.wait()
            for row in range(tok_count):
                residue_rows[pl.ds(row, 1), :] = residue[pl.ds(tokens[row], 1), :]

    offset = jnp.sum(sums, axis=1, keepdims=True) / width
    spread = jnp.sum(squares, axis=1, keepdims=True) / width - offset * offset
    mean = shift + offset
    scale = lax.rsqrt(jnp.maximum(spread, 0.0) + epsilon)
    gain, bias = norm_gain[...].reshape(1, width), norm_bias[...].reshape(1, width)
    total = None
    for at, (low, size) in enumerate(in_pieces):
        span = slice(low, low + size)
        normed = ((mixture[:, span] - mean) * scale * gain[:, span] + bias[:, span]).astype(BF16)
        firsts[at].wait()
        term = jnp.dot(normed, proj_in[pl.ds(low, size), :], preferred_element_type=F32)
        total = term if total is None else total + term
    middle = jnp.maximum(total + proj_in_bias[...], 0.0).astype(BF16)

    total = None
    for at, (low, size) in enumerate(out_pieces):
        seconds[at].wait()
        term = jnp.dot(
            middle[:, low:low + size], proj_out[pl.ds(low, size), :], preferred_element_type=F32
        )
        total = term if total is None else total + term
    single_f = total + proj_out_bias[...] + residue_rows[...]
    single[...] = single_f.astype(BF16)

    pair_in = row_norm(single_f, pair_gain[...], pair_bias[...]).astype(BF16)
    query_key = jnp.dot(pair_in, qk[...], preferred_element_type=F32) + qk_bias[...]

    front = lax.broadcasted_iota(jnp.int32, flags.shape, 1) < inner_dim
    query_ref[...] = jnp.where(front, query_key, flags).astype(BF16)
    block = jnp.where(front, pltpu.roll(query_key, inner_dim, 1), flags).astype(BF16)
    for peer in range(copies_ref.shape[0]):
        copies_ref[peer] = block


def single_part(device_count, operands):
    (hidden, mix, norm_gain, norm_bias, proj_in, proj_in_bias, proj_out, proj_out_bias, tokens,
     residue, pair_gain, pair_bias, qk, qk_bias, chain, bins, pair_weight, relpos,
     chain_table) = operands
    tok_count, width = hidden.shape[1:]
    channels = proj_out.shape[1]
    lanes = qk.shape[1]
    table_rows = -(-relpos.shape[0] // 128) * 128
    vmem = pl.BlockSpec(memory_space=pltpu.VMEM)
    plan = (pieces(width, 5), pieces(channels, 2))
    args = (
        hidden, mix, norm_gain, norm_bias, proj_in, proj_in_bias[None],
        proj_out, proj_out_bias[None], tokens, residue, pair_gain[None], pair_bias[None],
        qk, qk_bias[None], chain[None], bins, pair_weight, relpos, chain_table,
    )
    args = [pltpu.with_memory_space_constraint(arg, pltpu.HBM) for arg in args]
    in_smem = (1, 8)
    scratch = [
        (pltpu.SMEM if at in in_smem else pltpu.VMEM)(arg.shape, arg.dtype)
        for at, arg in enumerate(args)
    ]
    scratch += [
        pltpu.VMEM((tok_count, width), F32),
        pltpu.VMEM((tok_count, channels), F32),
        pltpu.VMEM((table_rows, pair_weight.shape[1]), F32),
        pltpu.SemaphoreType.DMA((len(plan[0]),)),
        pltpu.SemaphoreType.DMA((len(plan[0]),)),
        pltpu.SemaphoreType.DMA((len(plan[1]),)),
        pltpu.SemaphoreType.DMA((16,)),
    ]
    moved = sum(arg.size * arg.dtype.itemsize for arg in args)
    return pl.pallas_call(
        functools.partial(single_kernel, plan),
        out_shape=(
            jax.ShapeDtypeStruct((tok_count, channels), BF16),
            jax.ShapeDtypeStruct((tok_count, lanes), BF16),
            jax.ShapeDtypeStruct((device_count, tok_count, lanes), BF16),
            jax.ShapeDtypeStruct(bins.shape + pair_weight.shape[1:], F32),
            jax.ShapeDtypeStruct(pair_weight.shape, BF16),
            jax.ShapeDtypeStruct(pair_weight.shape, BF16),
        ),
        in_specs=[pl.BlockSpec(memory_space=pltpu.HBM)] * len(args),
        out_specs=(vmem,) * 6,
        scratch_shapes=scratch,
        compiler_params=pltpu.CompilerParams(vmem_limit_bytes=32 * 2**20),
        cost_estimate=pl.CostEstimate(
            flops=2 * tok_count * channels * (width + channels + lanes),
            bytes_accessed=moved,
            transcendentals=0,
        ),
        name="single_path",
    )(*args)


def pair_kernel(
    blocks, queries, first, right, minus, single, single_hbm, pair_hbm, pair, sem, sem_single
):
    single_copy = pltpu.make_async_copy(single, single_hbm, sem_single)
    single_copy.start()
    keys = jnp.concatenate([blocks[1:].reshape(-1, blocks.shape[2]), blocks[0]], axis=0)
    row_diff = jnp.dot(queries[...], minus[...], preferred_element_type=F32)
    col_diff = jnp.dot(keys, minus[...], preferred_element_type=F32)
    copies = []
    tok_count, col_count, channels = first.shape
    for at, (low, size) in enumerate(pieces(tok_count, tok_count // 2)):
        products = [keys * queries[row:row + 1, :] for row in range(low, low + size)]
        value = jnp.dot(
            jnp.concatenate(products, axis=0), right[...], preferred_element_type=F32
        ).reshape(size, col_count, channels)
        for row in range(low, low + size):
            rest = first[row] + (row_diff[row:row + 1, :] - col_diff)
            pair[row] = (value[row - low] + rest).astype(BF16)
        rows = pl.ds(low, size)
        copy = pltpu.make_async_copy(pair.at[rows], pair_hbm.at[rows], sem.at[at])
        copy.start()
        copies.append(copy)
    for copy in copies:
        copy.wait()
    single_copy.wait()


def pair_part(blocks, queries, first, right, minus, single):
    tok_count = first.shape[0]
    vmem = pl.BlockSpec(memory_space=pltpu.VMEM)
    return pl.pallas_call(
        pair_kernel,
        out_shape=(
            jax.ShapeDtypeStruct(single.shape, BF16),
            jax.ShapeDtypeStruct(first.shape, BF16),
        ),
        in_specs=[vmem] * 6,
        out_specs=(pl.BlockSpec(memory_space=pltpu.HBM),) * 2,
        scratch_shapes=[
            pltpu.VMEM(first.shape, BF16),
            pltpu.SemaphoreType.DMA((tok_count,)),
            pltpu.SemaphoreType.DMA,
        ],
        compiler_params=pltpu.CompilerParams(vmem_limit_bytes=32 * 2**20),
        cost_estimate=pl.CostEstimate(
            flops=2 * first.size * right.shape[0],
            bytes_accessed=6 * first.size,
            transcendentals=0,
        ),
        name="pair_rows",
    )(blocks, queries, first, right, minus, single)


def shards(
    hidden_states,
    layer_mix,
    norm_gain,
    norm_bias,
    proj_in,
    proj_in_bias,
    proj_out,
    proj_out_bias,
    residue_tokens,
    residue_table,
    pair_norm_gain,
    pair_norm_bias,
    qk_weight,
    qk_bias,
    pair_weight,
    relpos_bins,
    relpos_table,
    chain_ids,
    chain_table,
):
    device_count = lax.axis_size("seq")
    single, queries, copies, first, right, minus = single_part(
        device_count,
        (
            hidden_states, layer_mix, norm_gain, norm_bias, proj_in, proj_in_bias, proj_out,
            proj_out_bias, residue_tokens, residue_table, pair_norm_gain, pair_norm_bias,
            qk_weight, qk_bias, chain_ids, relpos_bins, pair_weight, relpos_table, chain_table,
        ),
    )
    order = [device_count - 1] + list(range(device_count - 1))
    blocks = lax.all_to_all(
        copies, "seq", split_axis=0, concat_axis=0, axis_index_groups=[order]
    )
    return pair_part(blocks, queries, first, right, minus, single)


def solution(mesh):
    in_specs = (
        P(None, ("groups", "seq"), None),
        P(),
        P(),
        P(),
        P(),
        P(),
        P(),
        P(),
        P(("groups", "seq")),
        P(),
        P(),
        P(),
        P(),
        P(),
        P(),
        P(("groups", "seq"), None),
        P(),
        P(("groups", "seq")),
        P(),
    )
    out_specs = (P(("groups", "seq"), None), P(("groups", "seq"), None, None))
    return jax.shard_map(shards, mesh=mesh, in_specs=in_specs, out_specs=out_specs, check_vma=False)
```

```python
import functools

import jax
import jax.numpy as jnp
from jax import lax
from jax.experimental import pallas as pl
from jax.experimental.pallas import tpu as pltpu
from jax.sharding import PartitionSpec as P

epsilon = 1e-05
BF16 = jnp.bfloat16
F32 = jnp.float32


def pieces(total, count):
    count = max(1, min(count, total))
    ends = [total * step // count for step in range(count + 1)]
    return [(low, high - low) for low, high in zip(ends[:-1], ends[1:])]


def row_norm(values, gain, bias):
    center = values - jnp.mean(values, axis=-1, keepdims=True)
    spread = jnp.mean(center * center, axis=-1, keepdims=True)
    return center * lax.rsqrt(spread + epsilon) * gain + bias


def chain_flags(chain, tok_count, inner_dim):
    lanes = lax.broadcasted_iota(jnp.int32, (tok_count, 2 * inner_dim), 1)
    flag = lax.rem(lanes, inner_dim // 2).astype(F32)
    square = (tok_count, tok_count)
    own = lax.broadcasted_iota(jnp.int32, square, 0) == lax.broadcasted_iota(jnp.int32, square, 1)
    chain_col = jnp.sum(jnp.where(own, chain[...].astype(F32), 0.0), axis=1, keepdims=True)
    return jnp.where(flag == chain_col, 1.0, 0.0)


def operand_rows(bins, pair_weight, relpos, chain_table, bin_rows, right, minus, tok_count):
    bin_count = relpos.shape[0]
    inner_dim = pair_weight.shape[0] // 2
    flag_count = inner_dim // 2
    step = chain_table[1:2, :] - chain_table[0:1, :]
    step_high = step.astype(BF16).astype(F32)
    shape = (flag_count, step.shape[1])
    right[0:inner_dim, :] = pair_weight[0:inner_dim, :]
    right[inner_dim:inner_dim + flag_count, :] = jnp.broadcast_to(step_high, shape).astype(BF16)
    right[inner_dim + flag_count:, :] = jnp.broadcast_to(step - step_high, shape).astype(BF16)
    minus[0:inner_dim, :] = pair_weight[inner_dim:, :]
    minus[inner_dim:, :] = jnp.zeros((inner_dim, step.shape[1]), BF16)
    bin_rows[...] = jnp.zeros(bin_rows.shape, F32)
    bin_rows[0:bin_count, :] = relpos[...] + chain_table[0:1, :]
    padded = jnp.concatenate(
        [bins[...], jnp.zeros((128 - tok_count, bins.shape[1]), jnp.int32)], axis=0
    )
    return padded.T


def single_kernel(
    plan,
    hidden_hbm, mix_hbm, norm_gain_hbm, norm_bias_hbm, proj_in_hbm, proj_in_bias_hbm,
    proj_out_hbm, proj_out_bias_hbm, tokens_hbm, residue_hbm, pair_gain_hbm, pair_bias_hbm,
    qk_hbm, qk_bias_hbm, chain_hbm, bins_hbm, pair_weight_hbm, relpos_hbm, chain_table_hbm,
    single, query_ref, copies_ref, first, right, minus,
    hidden, mix, norm_gain, norm_bias, proj_in, proj_in_bias, proj_out, proj_out_bias, tokens,
    residue, pair_gain, pair_bias, qk, qk_bias, chain, bins, pair_weight, relpos, chain_table,
    mixture, residue_rows, bin_rows, sem_hidden, sem_in, sem_out, sem_small,
):
    in_pieces, out_pieces = plan
    tok_count = mixture.shape[0]
    inner_dim = qk.shape[1] // 2

    small = [
        (bins_hbm, bins), (relpos_hbm, relpos), (chain_table_hbm, chain_table),
        (pair_weight_hbm, pair_weight), (chain_hbm, chain), (mix_hbm, mix),
        (norm_gain_hbm, norm_gain), (norm_bias_hbm, norm_bias), (tokens_hbm, tokens),
        (residue_hbm, residue), (proj_in_bias_hbm, proj_in_bias),
        (proj_out_bias_hbm, proj_out_bias), (pair_gain_hbm, pair_gain),
        (pair_bias_hbm, pair_bias), (qk_hbm, qk), (qk_bias_hbm, qk_bias),
    ]
    first_small = 6
    small = [
        pltpu.make_async_copy(source, target, sem_small.at[at])
        for at, (source, target) in enumerate(small)
    ]
    states = [
        pltpu.make_async_copy(
            hidden_hbm.at[:, :, pl.ds(low, size)],
            hidden.at[:, :, pl.ds(low, size)],
            sem_hidden.at[at],
        )
        for at, (low, size) in enumerate(in_pieces)
    ]
    firsts = [
        pltpu.make_async_copy(
            proj_in_hbm.at[pl.ds(low, size)], proj_in.at[pl.ds(low, size)], sem_in.at[at]
        )
        for at, (low, size) in enumerate(in_pieces)
    ]
    seconds = [
        pltpu.make_async_copy(
            proj_out_hbm.at[pl.ds(low, size)], proj_out.at[pl.ds(low, size)], sem_out.at[at]
        )
        for at, (low, size) in enumerate(out_pieces)
    ]
    for copy in small[:first_small] + states + small[first_small:]:
        copy.start()
    for copy in firsts + seconds:
        copy.start(priority=1)

    for copy in small[:first_small]:
        copy.wait()
    bins_col = operand_rows(
        bins, pair_weight, relpos, chain_table, bin_rows, right, minus, tok_count
    )
    bin_table = bin_rows[...].astype(BF16)
    lanes = lax.broadcasted_iota(jnp.int32, (bins_col.shape[0], bin_table.shape[0]), 1)
    for row in range(tok_count):
        onehot = jnp.where(bins_col[:, row:row + 1] == lanes, 1.0, 0.0).astype(BF16)
        first[row] = jnp.dot(onehot, bin_table, preferred_element_type=F32)
    flags = chain_flags(chain, tok_count, inner_dim)

    width = mixture.shape[1]
    shift = sums = squares = None
    for at, (low, size) in enumerate(in_pieces):
        states[at].wait()
        total = None
        for state in range(hidden.shape[0]):
            term = mix[state] * hidden[state, :, low:low + size].astype(F32)
            total = term if total is None else total + term
        mixture[:, low:low + size] = total
        if shift is None:
            shift = jnp.mean(total, axis=1, keepdims=True)
        total = total - shift
        for lane in range(0, size, 128):
            part = total[:, lane:lane + 128]
            sums = part if sums is None else sums + part
            squares = part * part if squares is None else squares + part * part
        if at == min(1, len(in_pieces) - 1):
            for copy in small[first_small:]:
                copy.wait()
            for row in range(tok_count):
                residue_rows[pl.ds(row, 1), :] = residue[pl.ds(tokens[row], 1), :]

    offset = jnp.sum(sums, axis=1, keepdims=True) / width
    spread = jnp.sum(squares, axis=1, keepdims=True) / width - offset * offset
    mean = shift + offset
    scale = lax.rsqrt(jnp.maximum(spread, 0.0) + epsilon)
    gain, bias = norm_gain[...].reshape(1, width), norm_bias[...].reshape(1, width)
    total = None
    for at, (low, size) in enumerate(in_pieces):
        span = slice(low, low + size)
        normed = ((mixture[:, span] - mean) * scale * gain[:, span] + bias[:, span]).astype(BF16)
        firsts[at].wait()
        term = jnp.dot(normed, proj_in[pl.ds(low, size), :], preferred_element_type=F32)
        total = term if total is None else total + term
    middle = jnp.maximum(total + proj_in_bias[...], 0.0).astype(BF16)

    total = None
    for at, (low, size) in enumerate(out_pieces):
        seconds[at].wait()
        term = jnp.dot(
            middle[:, low:low + size], proj_out[pl.ds(low, size), :], preferred_element_type=F32
        )
        total = term if total is None else total + term
    single_f = total + proj_out_bias[...] + residue_rows[...]
    single[...] = single_f.astype(BF16)

    pair_in = row_norm(single_f, pair_gain[...], pair_bias[...]).astype(BF16)
    query_key = jnp.dot(pair_in, qk[...], preferred_element_type=F32) + qk_bias[...]

    front = lax.broadcasted_iota(jnp.int32, flags.shape, 1) < inner_dim
    query_ref[...] = jnp.where(front, query_key, flags).astype(BF16)
    block = jnp.where(front, pltpu.roll(query_key, inner_dim, 1), flags).astype(BF16)
    for peer in range(copies_ref.shape[0]):
        copies_ref[peer] = block


def single_part(device_count, operands):
    (hidden, mix, norm_gain, norm_bias, proj_in, proj_in_bias, proj_out, proj_out_bias, tokens,
     residue, pair_gain, pair_bias, qk, qk_bias, chain, bins, pair_weight, relpos,
     chain_table) = operands
    tok_count, width = hidden.shape[1:]
    channels = proj_out.shape[1]
    lanes = qk.shape[1]
    table_rows = -(-relpos.shape[0] // 128) * 128
    vmem = pl.BlockSpec(memory_space=pltpu.VMEM)
    plan = (pieces(width, 5), pieces(channels, 2))
    args = (
        hidden, mix, norm_gain, norm_bias, proj_in, proj_in_bias[None],
        proj_out, proj_out_bias[None], tokens, residue, pair_gain[None], pair_bias[None],
        qk, qk_bias[None], chain[None], bins, pair_weight, relpos, chain_table,
    )
    args = [pltpu.with_memory_space_constraint(arg, pltpu.HBM) for arg in args]
    in_smem = (1, 8)
    scratch = [
        (pltpu.SMEM if at in in_smem else pltpu.VMEM)(arg.shape, arg.dtype)
        for at, arg in enumerate(args)
    ]
    scratch += [
        pltpu.VMEM((tok_count, width), F32),
        pltpu.VMEM((tok_count, channels), F32),
        pltpu.VMEM((table_rows, pair_weight.shape[1]), F32),
        pltpu.SemaphoreType.DMA((len(plan[0]),)),
        pltpu.SemaphoreType.DMA((len(plan[0]),)),
        pltpu.SemaphoreType.DMA((len(plan[1]),)),
        pltpu.SemaphoreType.DMA((16,)),
    ]
    moved = sum(arg.size * arg.dtype.itemsize for arg in args)
    return pl.pallas_call(
        functools.partial(single_kernel, plan),
        out_shape=(
            jax.ShapeDtypeStruct((tok_count, channels), BF16),
            jax.ShapeDtypeStruct((tok_count, lanes), BF16),
            jax.ShapeDtypeStruct((device_count, tok_count, lanes), BF16),
            jax.ShapeDtypeStruct(bins.shape + pair_weight.shape[1:], F32),
            jax.ShapeDtypeStruct(pair_weight.shape, BF16),
            jax.ShapeDtypeStruct(pair_weight.shape, BF16),
        ),
        in_specs=[pl.BlockSpec(memory_space=pltpu.HBM)] * len(args),
        out_specs=(vmem,) * 6,
        scratch_shapes=scratch,
        compiler_params=pltpu.CompilerParams(vmem_limit_bytes=32 * 2**20),
        cost_estimate=pl.CostEstimate(
            flops=2 * tok_count * channels * (width + channels + lanes),
            bytes_accessed=moved,
            transcendentals=0,
        ),
        name="single_path",
    )(*args)


def pair_kernel(
    blocks, queries, first, right, minus, single, single_hbm, pair_hbm, pair, sem, sem_single
):
    single_copy = pltpu.make_async_copy(single, single_hbm, sem_single)
    single_copy.start()
    keys = jnp.concatenate([blocks[1:].reshape(-1, blocks.shape[2]), blocks[0]], axis=0)
    query_rows = queries[...]
    row_diff = jnp.dot(query_rows, minus[...], preferred_element_type=F32)
    both = jnp.concatenate([right[...], -minus[...]], axis=0)
    copies = []
    for row in range(first.shape[0]):
        products = jnp.concatenate([keys * query_rows[row:row + 1, :], keys], axis=1)
        value = jnp.dot(products, both, preferred_element_type=F32)
        value = value + first[row] + row_diff[row:row + 1, :]
        pair[row] = value.astype(BF16)
        copy = pltpu.make_async_copy(pair.at[row], pair_hbm.at[row], sem.at[row])
        copy.start()
        copies.append(copy)
    for copy in copies:
        copy.wait()
    single_copy.wait()


def pair_part(blocks, queries, first, right, minus, single):
    tok_count = first.shape[0]
    vmem = pl.BlockSpec(memory_space=pltpu.VMEM)
    return pl.pallas_call(
        pair_kernel,
        out_shape=(
            jax.ShapeDtypeStruct(single.shape, BF16),
            jax.ShapeDtypeStruct(first.shape, BF16),
        ),
        in_specs=[vmem] * 6,
        out_specs=(pl.BlockSpec(memory_space=pltpu.HBM),) * 2,
        scratch_shapes=[
            pltpu.VMEM(first.shape, BF16),
            pltpu.SemaphoreType.DMA((tok_count,)),
            pltpu.SemaphoreType.DMA,
        ],
        compiler_params=pltpu.CompilerParams(vmem_limit_bytes=32 * 2**20),
        cost_estimate=pl.CostEstimate(
            flops=2 * first.size * right.shape[0],
            bytes_accessed=6 * first.size,
            transcendentals=0,
        ),
        name="pair_rows",
    )(blocks, queries, first, right, minus, single)


def shards(
    hidden_states,
    layer_mix,
    norm_gain,
    norm_bias,
    proj_in,
    proj_in_bias,
    proj_out,
    proj_out_bias,
    residue_tokens,
    residue_table,
    pair_norm_gain,
    pair_norm_bias,
    qk_weight,
    qk_bias,
    pair_weight,
    relpos_bins,
    relpos_table,
    chain_ids,
    chain_table,
):
    device_count = lax.axis_size("seq")
    single, queries, copies, first, right, minus = single_part(
        device_count,
        (
            hidden_states, layer_mix, norm_gain, norm_bias, proj_in, proj_in_bias, proj_out,
            proj_out_bias, residue_tokens, residue_table, pair_norm_gain, pair_norm_bias,
            qk_weight, qk_bias, chain_ids, relpos_bins, pair_weight, relpos_table, chain_table,
        ),
    )
    order = [device_count - 1] + list(range(device_count - 1))
    blocks = lax.all_to_all(
        copies, "seq", split_axis=0, concat_axis=0, axis_index_groups=[order]
    )
    return pair_part(blocks, queries, first, right, minus, single)


def solution(mesh):
    in_specs = (
        P(None, ("groups", "seq"), None),
        P(),
        P(),
        P(),
        P(),
        P(),
        P(),
        P(),
        P(("groups", "seq")),
        P(),
        P(),
        P(),
        P(),
        P(),
        P(),
        P(("groups", "seq"), None),
        P(),
        P(("groups", "seq")),
        P(),
    )
    out_specs = (P(("groups", "seq"), None), P(("groups", "seq"), None, None))
    return jax.shard_map(shards, mesh=mesh, in_specs=in_specs, out_specs=out_specs, check_vma=False)
```
